32 devices in a mesh: wide: 8 (over z, y), narrow: 4 (over x, core).
Axes of the slice: x: 2, y: 2, z: 4, core: 2. Of those that a mesh axis runs over, the one named last changes fastest.
Arguments:
- tokens: bfloat16 [96, 256, 512], P('wide'), may hold values from -6 to 6
- cotangent: bfloat16 [96, 256, 512], P('wide'), may hold values from -6 to 6
- counts: int32 [8], replicated, may hold values from 1 to 12, 64 in all
- group_order: int32 [64], replicated, may hold values from 0 to 63, each once
- query_weight: bfloat16 [512, 512], P(None, 'narrow'), may hold values from -0.25 to 0.25
- key_weight: bfloat16 [512, 512], P(None, 'narrow'), may hold values from -0.25 to 0.25
- value_weight: bfloat16 [512, 512], P(None, 'narrow'), may hold values from -0.25 to 0.25
- output_weight: bfloat16 [512, 512], P('narrow'), may hold values from -1 to 1
- gain_attn: float32 [512], replicated, may hold values from 0.5 to 1.5
- gain_mix: float32 [512], replicated, may hold values from 0.5 to 1.5
- controller: bfloat16 [512, 32], P(None, 'narrow'), may hold values from -0.375 to 0.375
- w_in: bfloat16 [32, 512, 2048], P('narrow'), may hold values from -0.25 to 0.25
- b_in: float32 [32, 2048], P('narrow'), may hold values from -0.625 to 0.625
- w_out: bfloat16 [32, 2048, 512], P('narrow'), may hold values from -5 to 5
- b_out: float32 [32, 512], P('narrow'), may hold values from -3 to 3
Outputs:
- mixed_out: bfloat16 [96, 256, 512], P('wide')
- d_tokens: bfloat16 [96, 256, 512], P('wide')
- query_weight_gradient: float32 [512, 512], P(None, 'narrow')
- key_weight_gradient: float32 [512, 512], P(None, 'narrow')
- value_weight_gradient: float32 [512, 512], P(None, 'narrow')
- output_weight_gradient: float32 [512, 512], P('narrow')
- g_gain_attn: float32 [512], replicated
- g_gain_mix: float32 [512], replicated
- g_controller: float32 [512, 32], P(None, 'narrow')
- g_w_in: float32 [32, 512, 2048], P('narrow', 'wide')
- g_b_in: float32 [32, 2048], P('narrow')
- g_w_out: float32 [32, 2048, 512], P('narrow', 'wide')
- g_b_out: float32 [32, 512], P('narrow')
The draws below stay inside these ranges and needn't reach their ends.
Inputs may be any that keep to these rules, and one draw needn't show every extreme that they name: Index i of wide holds counts[i] sequences, in its first slots; the counts sum to 64 and the largest is 12. `group_order`: each sequence once.
All inputs are finite; a program needn't handle non-finite values.
Results may differ from the reference program's by a relative error of at most 0.04.
Values may be sent and summed in bfloat16 or wider, within the bound.
No kernel may reach another device: no remote copies, remote signals or barrier semaphores. Data moves between devices by JAX's collectives and lax.ppermute only.
A program may use at most 256 MiB of HBM per device.

```python
import math
import jax
import jax.numpy as jnp
import numpy as np
from jax import lax

D = 512
ATTENTION_HEADS = 8
HEAD_WIDTH = 64
FF = 2048
EXPERTS = 32
GROUP = 32
SEQUENCE_LENGTH = 256
GROUPS = 2
SEQS = 64
CAP = 12
N_WIDE = 8


def block_scale(stream_key, extent, cuts, least, high):
    gain = 1.0
    for position, parts in cuts:
        steps = jax.random.uniform(jax.random.fold_in(jax.random.fold_in(stream_key, 6), position), (parts,), jnp.float32, least / len(cuts), high / len(cuts))
        gain = gain * jnp.repeat(jnp.exp(steps), extent[position] // parts).reshape((-1,) + (1,) * (len(extent) - 1 - position))
    return gain


def length_profile(count, total, limit, skew):
    loads = [(1 << 20) // math.isqrt(grade ** skew) + 1 for grade in range(2, count + 1)]
    surplus, given = total - limit - (count - 1), [1] * (count - 1)
    while surplus > 0:
        candidates = [i for i in range(count - 1) if given[i] < limit]
        mass, remaining = sum([loads[i] for i in candidates]), surplus
        for i in candidates:
            addition = min(limit - given[i], max(1, remaining * loads[i] // mass), surplus)
            given[i] = given[i] + addition
            surplus = surplus - addition
    return np.array([limit] + given)


def ragged_sizes(rng, count, total, limit, slope):
    if count == 2:
        one = jax.random.randint(rng, (), max(1, total - limit), min(limit, total - 1) + 1)
        return jnp.stack([one, total - one])
    tallies = jnp.asarray(length_profile(count, total, limit, slope), jnp.int32)
    pairs = (count - 1) // 2
    giver, sink = tallies[1:1 + 2 * pairs:2], tallies[2:2 + 2 * pairs:2]
    room = jnp.minimum(giver - 1, limit - sink)
    passed = jax.random.randint(jax.random.fold_in(rng, 1), (pairs,), 0, 1 << 20) % (room + 1)
    tallies = tallies.at[1:1 + 2 * pairs:2].set(giver - passed).at[2:2 + 2 * pairs:2].set(sink + passed)
    return tallies[jax.random.permutation(jax.random.fold_in(rng, 2), count)]


def noise(stream_key, extent, spread, limit, cuts=(), kind=jnp.bfloat16):
    loudness = block_scale(stream_key, extent, cuts, -0.22, 0.18) if cuts else 1.0
    values = jax.random.normal(stream_key, extent, jnp.float32) * spread * loudness
    return jnp.minimum(jnp.maximum(values, -limit), limit).astype(kind)


def setup_inputs(seed: int = 0) -> dict:
    key_of = jax.random.split(jax.random.key(seed), 16)
    return {
        "tokens": noise(key_of[0], (N_WIDE * CAP, SEQUENCE_LENGTH, D), 1.0, 6.0, ((0, 8),)),
        "cotangent": noise(key_of[1], (N_WIDE * CAP, SEQUENCE_LENGTH, D), 1.0, 6.0, ((0, 8),)),
        "counts": ragged_sizes(key_of[2], N_WIDE, SEQS, CAP, 2).astype(jnp.int32),
        "group_order": jax.random.permutation(key_of[3], SEQS).astype(jnp.int32),
        "query_weight": noise(key_of[4], (D, D), D ** -0.5, 0.25, ((1, 4),)),
        "key_weight": noise(key_of[5], (D, D), D ** -0.5, 0.25, ((1, 4),)),
        "value_weight": noise(key_of[6], (D, D), D ** -0.5, 0.25, ((1, 4),)),
        "output_weight": noise(key_of[7], (D, D), (D // 16) ** -0.5, 1.0, ((0, 4),)),
        "gain_attn": jnp.clip(1.0 + 0.1 * jax.random.normal(key_of[8], (D,), jnp.float32), 0.5, 1.5),
        "gain_mix": jnp.clip(1.0 + 0.1 * jax.random.normal(key_of[9], (D,), jnp.float32), 0.5, 1.5),
        "controller": noise(key_of[10], (D, EXPERTS), (D // 2) ** -0.5, 0.375, ((1, 4),)),
        "w_in": noise(key_of[11], (EXPERTS, D, FF), D ** -0.5, 0.25, ((0, 4),)),
        "b_in": noise(key_of[12], (EXPERTS, FF), 0.1, 0.625, ((0, 4),), jnp.float32),
        "w_out": noise(key_of[13], (EXPERTS, FF, D), 0.8, 5.0, ((0, 4),)),
        "b_out": noise(key_of[14], (EXPERTS, D), 0.5, 3.0, ((0, 4),), jnp.float32),
    }


EPSILON = 1e-05
NEGATIVE = -1e+30
EXACT_PRECISION = lax.Precision.HIGHEST

@jax.custom_vjp
def low(v):
    return lax.optimization_barrier(v.astype(jnp.bfloat16)).astype(jnp.float32)

@jax.custom_vjp
def reduced_backward(v):
    return v

def low_keep(v):
    return (low(v), None)

def low_pass(kept, grad):
    return (grad,)

def back_keep(v):
    return (v, None)

def back_low(kept, grad):
    return (low(grad),)
low.defvjp(low_keep, low_pass)
reduced_backward.defvjp(back_keep, back_low)

def rounded_pair(value_in):
    return reduced_backward(low(value_in))

def rms_norm(values):
    return values * lax.rsqrt(lax.optimization_barrier(jnp.mean(values * values, axis=-1, keepdims=True)) + EPSILON)

def attention_block(block_input, query_weight, key_weight, value_weight):
    batch_input = block_input.shape[0]
    query_rows = rounded_pair(jnp.einsum('pza,aq->pzq', block_input, query_weight, precision=EXACT_PRECISION)).reshape(batch_input, SEQUENCE_LENGTH, ATTENTION_HEADS, HEAD_WIDTH)
    key_matrix_rows = rounded_pair(jnp.einsum('pza,aq->pzq', block_input, key_weight, precision=EXACT_PRECISION)).reshape(batch_input, SEQUENCE_LENGTH, ATTENTION_HEADS, HEAD_WIDTH)
    value_matrix_rows = rounded_pair(jnp.einsum('pza,aq->pzq', block_input, value_weight, precision=EXACT_PRECISION)).reshape(batch_input, SEQUENCE_LENGTH, ATTENTION_HEADS, HEAD_WIDTH)
    scores = reduced_backward(jnp.einsum('sqhc,skhc->shqk', query_rows, key_matrix_rows, precision=EXACT_PRECISION) * float(HEAD_WIDTH) ** (-0.5))
    causal = jnp.arange(SEQUENCE_LENGTH)[:, None] >= jnp.arange(SEQUENCE_LENGTH)[None, :]
    scores = jnp.where(causal, scores, NEGATIVE)
    probs = rounded_pair(jax.nn.softmax(scores, axis=-1))
    context_rows = rounded_pair(jnp.einsum('shqk,skhc->sqhc', probs, value_matrix_rows, precision=EXACT_PRECISION))
    return context_rows.reshape(batch_input, SEQUENCE_LENGTH, D)

def token_mixture(mix_in, controller, w_in, b_in, w_out, b_out, members):
    grouped = mix_in[members].reshape(GROUPS, GROUP, SEQUENCE_LENGTH, D)
    logits = reduced_backward(jnp.einsum('grld,de->grle', grouped, controller, precision=EXACT_PRECISION))
    weights = rounded_pair(jax.nn.softmax(logits, axis=1))
    merged = rounded_pair(jnp.einsum('grle,grld->gled', weights, grouped, precision=EXACT_PRECISION))
    pre_act = reduced_backward(jnp.einsum('gled,edf->glef', merged, w_in, precision=EXACT_PRECISION) + b_in)
    activation = low(jax.nn.gelu(pre_act))
    expert_out = rounded_pair(jnp.einsum('glef,efd->gled', activation, w_out, precision=EXACT_PRECISION) + b_out)
    combined = jnp.einsum('grle,gled->grld', weights, expert_out, precision=EXACT_PRECISION).reshape(SEQS, SEQUENCE_LENGTH, D)
    return rounded_pair(jnp.zeros_like(mix_in).at[members].set(combined))

def forward(complete_tokens, query_weight, key_weight, value_weight, output_weight, gain_attn, gain_mix, controller, w_in, b_in, w_out, b_out, live_rows, members):
    attention_input = rounded_pair(rms_norm(complete_tokens) * gain_attn)

    def one_block(block_input):
        return attention_block(block_input, query_weight, key_weight, value_weight)
    blocks = attention_input.reshape(-1, 16, SEQUENCE_LENGTH, D)
    context_rows = lax.map(jax.checkpoint(one_block), blocks).reshape(-1, SEQUENCE_LENGTH, D)
    hidden_state = complete_tokens + reduced_backward(jnp.einsum('pza,aq->pzq', context_rows, output_weight, precision=EXACT_PRECISION))
    mix_in = rounded_pair(rms_norm(hidden_state) * gain_mix)
    mix_delta = token_mixture(mix_in, controller, w_in, b_in, w_out, b_out, members)
    return live_rows[:, None, None] * (hidden_state + mix_delta)

def reference(tokens, cotangent, counts, group_order, query_weight, key_weight, value_weight, output_weight, gain_attn, gain_mix, controller, w_in, b_in, w_out, b_out):
    seq_ends = jnp.cumsum(counts).astype(jnp.int32)
    seq_starts = (seq_ends - counts).astype(jnp.int32)
    device_ids = jnp.arange(N_WIDE, dtype=jnp.int32)
    owner_dev = lax.optimization_barrier(jnp.sum((seq_ends[None, :] <= group_order[:, None]).astype(jnp.int32), axis=1)).astype(jnp.int32)
    first_seq = lax.optimization_barrier(jnp.sum(jnp.where(owner_dev[:, None] == device_ids[None, :], seq_starts[None, :], 0), axis=1)).astype(jnp.int32)
    members = (owner_dev * CAP + group_order - first_seq).astype(jnp.int32)
    slot_ids = jnp.arange(N_WIDE * CAP, dtype=jnp.int32)
    slot_counts = counts[(slot_ids // CAP).astype(jnp.int32)]
    live_rows = (slot_ids % CAP < slot_counts).astype(jnp.float32)

    def layer(*params):
        return forward(*params, live_rows, members)
    primals = (tokens.astype(jnp.float32), query_weight.astype(jnp.float32), key_weight.astype(jnp.float32), value_weight.astype(jnp.float32), output_weight.astype(jnp.float32), gain_attn.astype(jnp.float32), gain_mix.astype(jnp.float32), controller.astype(jnp.float32), w_in.astype(jnp.float32), b_in.astype(jnp.float32), w_out.astype(jnp.float32), b_out.astype(jnp.float32))
    result, backward = jax.vjp(layer, *primals)
    grads = backward(cotangent.astype(jnp.float32))
    return (result.astype(jnp.bfloat16), grads[0].astype(jnp.bfloat16), grads[1], grads[2], grads[3], grads[4], grads[5], grads[6], grads[7], grads[8], grads[9], grads[10], grads[11])
```

```python
import functools

import jax
import jax.numpy as jnp
from jax import lax
from jax.experimental import pallas as pl
from jax.experimental.pallas import tpu as pltpu
from jax.sharding import PartitionSpec as P

HEAD_WIDTH = 64
GROUP = 32
GROUPS = 2
LANES = 128

EPSILON = 1e-05
NEGATIVE = -1e30
BOTH = ("wide", "narrow")
F32 = jnp.float32
BF16 = jnp.bfloat16
VMEM_LIMIT = 56 * 1024 * 1024


def mm(a, b):
    return lax.dot_general(a, b, (((1,), (0,)), ((), ())), preferred_element_type=F32)


def mm_nt(a, b):
    return lax.dot_general(a, b, (((1,), (1,)), ((), ())), preferred_element_type=F32)


def mm_tn(a, b):
    return lax.dot_general(a, b, (((0,), (0,)), ((), ())), preferred_element_type=F32)


def params(*semantics):
    return pltpu.CompilerParams(dimension_semantics=semantics or None, vmem_limit_bytes=VMEM_LIMIT)


def whole(shape):
    zeros = (0,) * len(shape)
    return pl.BlockSpec(tuple(shape), lambda *_: zeros)


def head_masks(rows):
    lane = lax.broadcasted_iota(jnp.int32, (rows, LANES), 1)
    return [(lane >= h * HEAD_WIDTH) & (lane < (h + 1) * HEAD_WIDTH) for h in range(LANES // HEAD_WIDTH)]


def keep(mask, rows):
    return jnp.where(mask, rows, jnp.zeros_like(rows))


def causal_probs(query_head, keys, causal):
    scores = mm_nt(query_head, keys) * (float(HEAD_WIDTH) ** -0.5)
    scores = jnp.where(causal, scores, NEGATIVE)
    powers = jnp.exp(scores - jnp.max(scores, axis=-1, keepdims=True))
    return powers / jnp.sum(powers, axis=-1, keepdims=True)


def causal_mask(length):
    return lax.broadcasted_iota(jnp.int32, (length, length), 0) >= lax.broadcasted_iota(
        jnp.int32, (length, length), 1
    )


def inverse_rms(rows):
    return lax.rsqrt(jnp.mean(rows * rows, axis=-1, keepdims=True) + EPSILON)


def attention_kernel(blocks, place, tokens, *refs):
    packs = refs[:blocks]
    gain_attn, gain_mix, mix_out, hidden_out, q_out, k_out, v_out, context_out = refs[blocks:]
    rows = tokens[0].astype(F32)
    length, width = rows.shape
    entry = (rows * inverse_rms(rows) * gain_attn[...]).astype(BF16)
    causal = causal_mask(length)
    masks = head_masks(length)
    attention = jnp.zeros((length, width), F32)
    for j in range(blocks):
        at = slice(j * LANES, (j + 1) * LANES)
        joint = mm(entry, packs[j][:, : 3 * LANES]).astype(BF16)
        q, k, v = (joint[:, i * LANES : (i + 1) * LANES] for i in range(3))
        context = jnp.zeros((length, LANES), F32)
        for mask in masks:
            probs = causal_probs(keep(mask, q), k, causal)
            context = context + mm(probs.astype(BF16), keep(mask, v))
        context = context.astype(BF16)
        attention = attention + mm_nt(context, packs[j][:, 3 * LANES :])
        q_out[0, :, at] = q
        k_out[0, :, at] = k
        v_out[0, :, at] = v
        context_out[0, :, at] = context
    hidden = rows + attention
    mixed = hidden * inverse_rms(hidden) * gain_mix[...]
    mix_out[...] = mixed.reshape(mix_out.shape).astype(BF16)
    hidden_out[0] = hidden


def attention_forward(place, tokens, packs, gain_attn, gain_mix, slots, spread):
    total, length, width = tokens.shape
    inner = packs[0].shape[1] // 4 * len(packs)
    part = length // spread

    def own(i, place):
        return (jnp.minimum(place[0] + i, total - 1), 0, 0)

    def local(i, place):
        return (i, 0, 0)

    saved = jax.ShapeDtypeStruct((slots, length, inner), BF16)
    return pl.pallas_call(
        functools.partial(attention_kernel, len(packs)),
        grid_spec=pltpu.PrefetchScalarGridSpec(
            num_scalar_prefetch=1,
            grid=(slots,),
            in_specs=[pl.BlockSpec((1, length, width), own)]
            + [whole(p.shape) for p in packs]
            + [whole((1, width))] * 2,
            out_specs=[
                pl.BlockSpec((spread, 1, part, width), lambda i, place: (0, i, 0, 0)),
                pl.BlockSpec((1, length, width), local),
            ]
            + [pl.BlockSpec((1, length, inner), local)] * 4,
        ),
        out_shape=[
            jax.ShapeDtypeStruct((spread, slots, part, width), BF16),
            jax.ShapeDtypeStruct((slots, length, width), F32),
        ]
        + [saved] * 4,
        compiler_params=params("arbitrary"),
        cost_estimate=pl.CostEstimate(
            flops=slots * 2 * length * (4 * width * inner + 4 * length * inner),
            bytes_accessed=slots * length * width * 16 + 4 * width * inner * 2,
            transcendentals=slots * length * length * inner // HEAD_WIDTH,
        ),
        name="attention_forward",
    )(place, tokens, *packs, gain_attn, gain_mix)


def slot_softmax(logits, codes, part):
    experts = logits.shape[1]
    logits = logits.reshape(-1, part, experts)
    codes = jnp.broadcast_to(codes, (codes.shape[0], experts)).reshape(-1, part, experts)
    total = jnp.zeros_like(logits)
    for g in range(GROUPS):
        inside = (codes >= g * part) & (codes < (g + 1) * part)
        held = jnp.where(inside, logits, NEGATIVE)
        powers = jnp.where(inside, jnp.exp(held - jnp.max(held, axis=0, keepdims=True)), 0.0)
        total = total + powers / jnp.sum(powers, axis=0, keepdims=True)
    return total.reshape(-1, experts)


def group_totals(terms, codes, part):
    experts = terms.shape[1]
    terms = terms.reshape(-1, part, experts)
    codes = jnp.broadcast_to(codes, (codes.shape[0], experts)).reshape(-1, part, experts)
    total = jnp.zeros_like(terms)
    for g in range(GROUPS):
        inside = (codes >= g * part) & (codes < (g + 1) * part)
        total = jnp.where(inside, jnp.sum(jnp.where(inside, terms, 0.0), axis=0, keepdims=True), total)
    return total.reshape(-1, experts)


def mix_kernel(part, rows, cots, controller, row_code, col_code, tile, probs_out, spread_out, sent):
    held = rows[...]
    probs = slot_softmax(mm(held, controller[...]), row_code[...], part)
    probs_out[...] = probs
    wide = mm(probs.astype(BF16), tile[...])
    spread = jnp.where(row_code[...] == col_code[...], wide, 0.0).astype(BF16)
    spread_out[...] = spread
    block = sent.shape[2]
    merged = mm_tn(spread, held).astype(BF16)
    grads = mm_tn(spread, cots[...]).astype(BF16)
    for n in range(sent.shape[0]):
        sent[n, 0] = merged[n * block : (n + 1) * block]
        sent[n, 1] = grads[n * block : (n + 1) * block]


def mix_forward(part, rows, cots, controller, row_code, col_code, tile, narrow):
    count, width = rows.shape
    experts, columns = tile.shape
    return pl.pallas_call(
        functools.partial(mix_kernel, part),
        out_shape=[
            jax.ShapeDtypeStruct((count, experts), F32),
            jax.ShapeDtypeStruct((count, columns), BF16),
            jax.ShapeDtypeStruct((narrow, 2, columns // narrow, width), BF16),
        ],
        compiler_params=params(),
        cost_estimate=pl.CostEstimate(
            flops=4 * count * columns * width,
            bytes_accessed=6 * count * width * 2,
            transcendentals=count * experts * 2,
        ),
        name="mix_forward",
    )(rows, cots, controller, row_code, col_code, tile)


def unmix_kernel(
    part, spread, rows, cots, probs, back, controller, row_code, col_code, tile, grad_out, mixed_out, gain_out
):
    columns = spread.shape[1]
    outs = back[:, 0].reshape(columns, -1)
    grads = back[:, 1].reshape(columns, -1)
    held = rows[...]
    pairs = (mm_nt(cots[...], outs) + mm_nt(held, grads)).astype(BF16)
    pairs = jnp.where(row_code[...] == col_code[...], pairs, jnp.zeros_like(pairs))
    d_weights = mm_nt(pairs, tile[...])
    p = probs[...]
    d_logits = (p * (d_weights - group_totals(p * d_weights, row_code[...], part))).astype(BF16)
    grad_out[...] = (mm(spread[...], grads) + mm_nt(d_logits, controller[...])).astype(BF16)
    mixed_out[...] = mm(spread[...], outs).astype(BF16)
    gain_out[...] = mm_tn(d_logits, held)


def mix_backward(part, spread, rows, cots, probs, back, controller, row_code, col_code, tile):
    count, width = rows.shape
    experts, columns = tile.shape
    return pl.pallas_call(
        functools.partial(unmix_kernel, part),
        out_shape=[
            jax.ShapeDtypeStruct((count, width), BF16),
            jax.ShapeDtypeStruct((count, width), BF16),
            jax.ShapeDtypeStruct((experts, width), F32),
        ],
        compiler_params=params(),
        cost_estimate=pl.CostEstimate(
            flops=8 * count * columns * width,
            bytes_accessed=8 * count * width * 2,
            transcendentals=0,
        ),
        name="mix_backward",
    )(spread, rows, cots, probs, back, controller, row_code, col_code, tile)


GELU_SLOPE = 0.7978845608028654
GELU_CUBE = 0.044715


def gelu_pair(x):
    square = x * x
    bend = jnp.tanh(GELU_SLOPE * x * (1.0 + GELU_CUBE * square))
    gate = 0.5 * (1.0 + bend)
    slope = gate + 0.5 * x * (1.0 - bend * bend) * (GELU_SLOPE * (1.0 + 3.0 * GELU_CUBE * square))
    return x * gate, slope


def expert_kernel(both, w_in, b_in, w_out, b_out, sent):
    block = both.shape
    merged = both[:, 0].reshape(-1, block[-1])
    grads = both[:, 1].reshape(-1, block[-1])
    act, slope = gelu_pair(mm(merged, w_in[0]) + b_in[0])
    outs = mm(act.astype(BF16), w_out[0]) + b_out[0]
    d_pre = (mm_nt(grads, w_out[0]) * slope).astype(BF16)
    d_merged = mm_nt(d_pre, w_in[0])
    shape = (block[0],) + block[2:]
    sent[:, 0] = outs.astype(BF16).reshape(shape)
    sent[:, 1] = d_merged.astype(BF16).reshape(shape)


def experts_at_positions(both, w_in, b_in, w_out, b_out):
    sources, _, count, width = both.shape
    experts, _, inner = w_in.shape
    rows = count // experts
    tokens = pl.BlockSpec((sources, 2, rows, width), lambda e: (0, 0, e, 0))
    return pl.pallas_call(
        expert_kernel,
        grid=(experts,),
        in_specs=[
            tokens,
            pl.BlockSpec((1, width, inner), lambda e: (e, 0, 0)),
            pl.BlockSpec((1, 1, inner), lambda e: (e, 0, 0)),
            pl.BlockSpec((1, inner, width), lambda e: (e, 0, 0)),
            pl.BlockSpec((1, 1, width), lambda e: (e, 0, 0)),
        ],
        out_specs=tokens,
        out_shape=jax.ShapeDtypeStruct(both.shape, BF16),
        compiler_params=params("arbitrary"),
        cost_estimate=pl.CostEstimate(
            flops=8 * sources * count * width * inner,
            bytes_accessed=4 * experts * width * inner + 4 * sources * count * width * 2,
            transcendentals=sources * count * inner,
        ),
        name="experts",
    )(both, w_in, b_in[:, None], w_out, b_out[:, None])


def weight_kernel(expert, both, w_in, b_in, w_out, g_in, g_out, merged, grads):
    width = both.shape[-1]

    @pl.when(pl.program_id(0) == 0)
    def _():
        merged[...] = both[:, :, 0].reshape(merged.shape)
        grads[...] = both[:, :, 1].reshape(grads.shape)

    act, slope = gelu_pair(mm(merged[...], w_in[0]) + b_in[0])
    d_pre = (mm_nt(grads[...], w_out[0]) * slope).astype(BF16)
    g_in[...] = mm_tn(merged[...], d_pre).astype(BF16)
    block = w_out.shape[1]
    g_out[0, :block] = mm_tn(act.astype(BF16), grads[...]).astype(BF16)
    bias_out = jnp.sum(grads[...].astype(F32), axis=0, keepdims=True)
    bias_in = jnp.sum(d_pre.astype(F32), axis=0, keepdims=True)
    g_out[0, block:] = jnp.zeros((g_out.shape[1] - block, width), BF16)
    g_out[0, block : block + 1] = bias_out.astype(BF16)
    g_out[0, block + 1 : block + 2] = jnp.concatenate(
        [bias_in, jnp.zeros((1, width - bias_in.shape[1]), F32)], axis=1
    ).astype(BF16)


def expert_weights(expert, both, w_in, b_in, w_out, wide):
    sources, inner_sources, _, rows, width = both.shape
    inner = w_in.shape[2]
    block = inner // wide
    count = sources * inner_sources * rows
    return pl.pallas_call(
        weight_kernel,
        grid_spec=pltpu.PrefetchScalarGridSpec(
            num_scalar_prefetch=1,
            grid=(wide,),
            in_specs=[
                whole(both.shape),
                pl.BlockSpec((1, width, block), lambda i, e: (e[0], 0, i)),
                pl.BlockSpec((1, 1, block), lambda i, e: (e[0], 0, i)),
                pl.BlockSpec((1, block, width), lambda i, e: (e[0], i, 0)),
            ],
            out_specs=[
                pl.BlockSpec((width, block), lambda i, e: (0, i)),
                pl.BlockSpec((1, block + 16, width), lambda i, e: (i, 0, 0)),
            ],
            scratch_shapes=[pltpu.VMEM((count, width), BF16)] * 2,
        ),
        out_shape=[
            jax.ShapeDtypeStruct((width, inner), BF16),
            jax.ShapeDtypeStruct((wide, block + 16, width), BF16),
        ],
        compiler_params=params("arbitrary"),
        cost_estimate=pl.CostEstimate(
            flops=8 * count * width * inner,
            bytes_accessed=8 * width * inner + 4 * count * width,
            transcendentals=count * inner,
        ),
        name="expert_weights",
    )(expert, both, w_in, b_in[:, None], w_out)


def hidden_kernel(blocks, place, cots, grads, hidden, context, gain_mix, d_hidden_out, weight_out, gain_out):
    i = pl.program_id(0)
    length, width = hidden.shape[1:]
    live = (place[0] + i < place[1]).astype(F32)
    rows = hidden[0]
    inverse = inverse_rms(rows)
    normed = rows * inverse
    grad = grads[...].astype(F32).reshape(length, width)
    d_normed = grad * gain_mix[...]
    d_hidden = cots[0].astype(F32) * live + inverse * (
        d_normed - normed * jnp.mean(d_normed * normed, axis=-1, keepdims=True)
    )
    d_hidden_out[0] = d_hidden
    gain = jnp.sum(grad * normed, axis=0, keepdims=True)
    d_low = d_hidden.astype(BF16)

    @pl.when(i == 0)
    def _():
        weight_out[...] = jnp.zeros_like(weight_out)
        gain_out[...] = jnp.zeros_like(gain_out)

    gain_out[0:1] += gain
    for j in range(blocks):
        weight_out[j] += mm_tn(context[0, :, j * LANES : (j + 1) * LANES], d_low)


def hidden_backward(place, cotangent, grads, hidden, context, gain_mix):
    spread, slots, part, width = grads.shape
    total, length, _ = cotangent.shape
    inner = context.shape[2]
    blocks = inner // LANES

    def own(i, place):
        return (jnp.minimum(place[0] + i, total - 1), 0, 0)

    def local(i, place):
        return (i, 0, 0)

    return pl.pallas_call(
        functools.partial(hidden_kernel, blocks),
        grid_spec=pltpu.PrefetchScalarGridSpec(
            num_scalar_prefetch=1,
            grid=(slots,),
            in_specs=[
                pl.BlockSpec((1, length, width), own),
                pl.BlockSpec((spread, 1, part, width), lambda i, place: (0, i, 0, 0)),
                pl.BlockSpec((1, length, width), local),
                pl.BlockSpec((1, length, inner), local),
                whole((1, width)),
            ],
            out_specs=[
                pl.BlockSpec((1, length, width), local),
                whole((blocks, LANES, width)),
                whole((8, width)),
            ],
        ),
        out_shape=[
            jax.ShapeDtypeStruct((slots, length, width), F32),
            jax.ShapeDtypeStruct((blocks, LANES, width), F32),
            jax.ShapeDtypeStruct((8, width), F32),
        ],
        compiler_params=params("arbitrary"),
        cost_estimate=pl.CostEstimate(
            flops=slots * 2 * length * width * inner,
            bytes_accessed=slots * length * width * 14,
            transcendentals=0,
        ),
        name="hidden_backward",
    )(place, cotangent, grads, hidden, context, gain_mix)


def attention_back_kernel(blocks, place, tokens, d_hidden, q_in, k_in, v_in, *refs):
    packs = refs[:blocks]
    gain_attn, d_tokens_out, weight_out, total, gain = refs[blocks:]
    i = pl.program_id(0)
    rows = tokens[0].astype(F32)
    length, width = rows.shape
    scale = float(HEAD_WIDTH) ** -0.5
    inverse = inverse_rms(rows)
    normed = rows * inverse
    entry = (normed * gain_attn[...]).astype(BF16)
    d_low = d_hidden[0].astype(BF16)
    causal = causal_mask(length)
    masks = head_masks(length)

    @pl.when(i == 0)
    def _():
        total[...] = jnp.zeros_like(total)
        gain[...] = jnp.zeros_like(gain)

    d_entry = jnp.zeros((length, width), F32)
    for j in range(blocks):
        at = slice(j * LANES, (j + 1) * LANES)
        q, k, v = q_in[0, :, at], k_in[0, :, at], v_in[0, :, at]
        d_context = mm(d_low, packs[j][:, 3 * LANES :]).astype(BF16)
        d_q = jnp.zeros((length, LANES), F32)
        d_k = jnp.zeros((length, LANES), F32)
        d_v = jnp.zeros((length, LANES), F32)
        for mask in masks:
            q_head = keep(mask, q)
            d_head = keep(mask, d_context)
            probs = causal_probs(q_head, k, causal)
            d_probs = mm_nt(d_head, v).astype(BF16).astype(F32)
            d_scores = probs * (d_probs - jnp.sum(probs * d_probs, axis=-1, keepdims=True))
            d_scores = d_scores.astype(BF16)
            d_v = d_v + mm_tn(probs.astype(BF16), d_head)
            d_q = d_q + mm(d_scores, keep(mask, k))
            d_k = d_k + mm_tn(d_scores, q_head)
        joint = jnp.concatenate([d_q * scale, d_k * scale, d_v], axis=1).astype(BF16)
        d_entry = d_entry + mm_nt(joint, packs[j][:, : 3 * LANES])
        grad = mm_tn(entry, joint)
        for c in range(3):
            total[j, c * width : (c + 1) * width] += grad[:, c * LANES : (c + 1) * LANES]
    d_entry = d_entry.astype(BF16).astype(F32)
    gain[0:1] += jnp.sum(d_entry * normed, axis=0, keepdims=True)
    d_normed = d_entry * gain_attn[...]
    d_tokens = d_hidden[0] + inverse * (
        d_normed - normed * jnp.mean(d_normed * normed, axis=-1, keepdims=True)
    )
    live = (place[0] + i < place[1]).astype(F32)
    d_tokens_out[0] = (d_tokens * live).astype(BF16)

    @pl.when(i == pl.num_programs(0) - 1)
    def _():
        height = 3 * width
        for j in range(blocks):
            weight_out[j, :height] = total[j].astype(BF16)
            weight_out[j, height:] = jnp.zeros((weight_out.shape[1] - height, LANES), BF16)
            tail = jnp.concatenate(
                [gain[0:1, c * LANES : (c + 1) * LANES] for c in range(width // LANES)]
                + [jnp.zeros((16 - width // LANES, LANES), F32)],
                axis=0,
            )
            weight_out[j, height : height + 16] = tail.astype(BF16)


def attention_backward(place, tokens, d_hidden, q, k, v, packs, gain_attn, extra):
    total, length, width = tokens.shape
    slots, _, inner = q.shape
    blocks = len(packs)

    def own(i, place):
        return (jnp.minimum(place[0] + i, total - 1), 0, 0)

    def local(i, place):
        return (i, 0, 0)

    return pl.pallas_call(
        functools.partial(attention_back_kernel, blocks),
        grid_spec=pltpu.PrefetchScalarGridSpec(
            num_scalar_prefetch=1,
            grid=(slots,),
            in_specs=[pl.BlockSpec((1, length, width), own), pl.BlockSpec((1, length, width), local)]
            + [pl.BlockSpec((1, length, inner), local)] * 3
            + [whole(p.shape) for p in packs]
            + [whole((1, width))],
            out_specs=[
                pl.BlockSpec((1, length, width), local),
                whole((blocks, 3 * width + extra, LANES)),
            ],
            scratch_shapes=[
                pltpu.VMEM((blocks, 3 * width, LANES), F32),
                pltpu.VMEM((8, width), F32),
            ],
        ),
        out_shape=[
            jax.ShapeDtypeStruct((slots, length, width), BF16),
            jax.ShapeDtypeStruct((blocks, 3 * width + extra, LANES), BF16),
        ],
        compiler_params=params("arbitrary"),
        cost_estimate=pl.CostEstimate(
            flops=slots * 2 * length * (7 * width * inner + 10 * length * inner),
            bytes_accessed=slots * length * width * 14 + 8 * width * inner * 2,
            transcendentals=slots * length * length * inner // HEAD_WIDTH,
        ),
        name="attention_backward",
    )(place, tokens, d_hidden, q, k, v, *packs, gain_attn)


def output_kernel(place, hidden, mixed, out):
    live = (place[0] + pl.program_id(0) < place[1]).astype(F32)
    rows = mixed[...].astype(F32).reshape(hidden.shape[1:])
    out[0] = (live * (hidden[0] + rows)).astype(BF16)


def layer_output(place, hidden, mixed):
    spread, slots, part, width = mixed.shape
    length = hidden.shape[1]
    return pl.pallas_call(
        output_kernel,
        grid_spec=pltpu.PrefetchScalarGridSpec(
            num_scalar_prefetch=1,
            grid=(slots,),
            in_specs=[
                pl.BlockSpec((1, length, width), lambda i, place: (i, 0, 0)),
                pl.BlockSpec((spread, 1, part, width), lambda i, place: (0, i, 0, 0)),
            ],
            out_specs=pl.BlockSpec((1, length, width), lambda i, place: (i, 0, 0)),
        ),
        out_shape=jax.ShapeDtypeStruct((slots, length, width), BF16),
        compiler_params=params("arbitrary"),
        cost_estimate=pl.CostEstimate(
            flops=slots * length * width * 3, bytes_accessed=slots * length * width * 8, transcendentals=0
        ),
        name="layer_output",
    )(place, hidden, mixed)


def swap_core(x):
    narrow = lax.axis_size("narrow")
    return lax.ppermute(x, "narrow", [(n, n ^ 1) for n in range(narrow)])


def from_chip(x, k):
    narrow = lax.axis_size("narrow")
    return lax.ppermute(x, "narrow", [((n + 2 * k) % narrow, n) for n in range(narrow)])


def to_chip(x, k):
    narrow = lax.axis_size("narrow")
    return lax.ppermute(x, "narrow", [(n, (n + 2 * k) % narrow) for n in range(narrow)])


def relative_narrow():
    narrow = lax.axis_size("narrow")
    me = lax.axis_index("narrow")
    chips = [lax.rem(me + 2 * k, narrow) for k in range(narrow // 2)]
    return chips + [lax.bitwise_xor(n, 1) for n in chips]


def gather_narrow(x):
    chips = [x] + [from_chip(x, k) for k in range(1, lax.axis_size("narrow") // 2)]
    return chips + [swap_core(piece) for piece in chips]


def scatter_narrow(x):
    chips = x.shape[0] // 2
    summed = x[:chips].astype(F32) + swap_core(x[chips:]).astype(F32)
    low = summed.astype(BF16)
    result = summed[0]
    for k in range(1, chips):
        result = result + to_chip(low[k], k).astype(F32)
    return result


def sum_wide(x):
    wide = lax.axis_size("wide")
    parts = x.astype(BF16).reshape(wide, x.shape[0] // wide, x.shape[1])
    parts = lax.all_to_all(parts, "wide", split_axis=0, concat_axis=0, tiled=True)
    part = jnp.sum(parts.astype(F32), axis=0).astype(BF16)
    parts = jnp.broadcast_to(part[None], parts.shape)
    parts = lax.all_to_all(parts, "wide", split_axis=0, concat_axis=0, tiled=True)
    return parts.reshape(x.shape).astype(F32)


def place_kernel(count, where, *refs):
    pieces, out, sems = refs[:count], refs[count], refs[count + 1]
    slots = pieces[0].shape[0]
    copies = [
        pltpu.make_async_copy(piece, out.at[pl.ds(where[j] * slots, slots)], sems.at[j])
        for j, piece in enumerate(pieces)
    ]
    for copy in copies:
        copy.start()
    for copy in copies:
        copy.wait()


def place_narrow(pieces, where):
    count = len(pieces)
    slots = pieces[0].shape[0]
    shape = (count * slots,) + pieces[0].shape[1:]
    size = pieces[0].size * 4 * count
    return pl.pallas_call(
        functools.partial(place_kernel, count),
        grid_spec=pltpu.PrefetchScalarGridSpec(
            num_scalar_prefetch=1,
            in_specs=[pl.BlockSpec(memory_space=pl.ANY)] * count,
            out_specs=pl.BlockSpec(memory_space=pl.ANY),
            scratch_shapes=[pltpu.SemaphoreType.DMA((count,))],
        ),
        out_shape=jax.ShapeDtypeStruct(shape, pieces[0].dtype),
        compiler_params=pltpu.CompilerParams(vmem_limit_bytes=1 << 20),
        cost_estimate=pl.CostEstimate(flops=0, bytes_accessed=size, transcendentals=0),
        name="place_narrow",
    )(where, *pieces)


def body(
    tokens,
    cotangent,
    counts,
    group_order,
    query_weight,
    key_weight,
    value_weight,
    output_weight,
    gain_attn,
    gain_mix,
    controller,
    w_in,
    b_in,
    w_out,
    b_out,
):
    slot_count, seq_len, model_width = tokens.shape
    wide, narrow = lax.axis_size("wide"), lax.axis_size("narrow")
    spread = wide * narrow
    wide_index, narrow_index = lax.axis_index("wide"), lax.axis_index("narrow")
    slots = -(-slot_count // narrow)
    part = seq_len // spread
    padded_part = -(-part // 8) * 8
    local_experts = w_in.shape[0]
    experts = local_experts * narrow
    share = wide // local_experts
    relative = jnp.stack(relative_narrow())
    head_columns = query_weight.shape[1]

    seq_ends = jnp.cumsum(counts)
    seq_starts = seq_ends - counts
    own_count = counts[wide_index]
    place = jnp.stack([narrow_index * slots, own_count]).astype(jnp.int32)
    slot_ids = jnp.arange(slots * narrow)
    slot_seqs = jnp.where(slot_ids[None] < counts[:, None], seq_starts[:, None] + slot_ids[None], -1)
    matches = slot_seqs.reshape(-1, 1) == group_order[None]
    slot_group = jnp.sum(jnp.where(matches, 1 + jnp.arange(group_order.shape[0]) // GROUP, 0), axis=1) - 1
    positions = jnp.arange(padded_part)
    row_code = jnp.where(slot_group[:, None] >= 0, slot_group[:, None] * padded_part + positions, -1)
    row_code = row_code.reshape(-1, 1).astype(jnp.int32)
    per_expert = GROUPS * padded_part
    col_code = (jnp.arange(experts * per_expert) % per_expert).astype(jnp.int32)[None]
    tile = jnp.repeat(jnp.eye(experts, dtype=BF16), per_expert, axis=1)

    pack = jnp.stack([query_weight, key_weight, value_weight, output_weight.T], axis=1)
    joined = LANES // head_columns
    packs = gather_narrow(pack.reshape(model_width, -1))
    if joined > 1:
        packs = [p.reshape(model_width, 4, head_columns) for p in packs]
        packs = [
            jnp.concatenate(packs[i : i + joined], axis=2).reshape(model_width, -1)
            for i in range(0, narrow, joined)
        ]
    controllers = jnp.stack(gather_narrow(controller.T))
    controllers = controllers[jnp.argsort(relative)].reshape(experts, model_width).T

    gain_attn_row, gain_mix_row = gain_attn[None], gain_mix[None]

    def own_slots(x):
        x = jnp.pad(x, ((0, slots * narrow - slot_count), (0, 0), (0, 0)))
        return lax.dynamic_slice_in_dim(x, narrow_index * slots, slots)

    def to_positions(x):
        x = lax.all_to_all(x, BOTH, split_axis=0, concat_axis=0, tiled=True)
        x = jnp.pad(x, ((0, 0), (0, 0), (0, padded_part - part), (0, 0)))
        return x.reshape(-1, model_width)

    def to_slots(x):
        x = x.reshape(spread, slots, padded_part, model_width)[:, :, :part]
        return lax.all_to_all(x, BOTH, split_axis=0, concat_axis=0, tiled=True)

    cot_sent = own_slots(cotangent).reshape(slots, spread, part, model_width).transpose(1, 0, 2, 3)
    cot_rows = to_positions(cot_sent)

    mix_sent, hidden, q, k, v, context = attention_forward(
        place, tokens, packs, gain_attn_row, gain_mix_row, slots, spread
    )
    mix_rows = to_positions(mix_sent)
    probs, spread_probs, both = mix_forward(
        padded_part, mix_rows, cot_rows, controllers, row_code, col_code, tile, narrow
    )

    both = both.reshape(narrow, 2, -1, padded_part, model_width)[:, :, :, :part]
    both = both.reshape(narrow, 2, -1, model_width)
    both = lax.all_to_all(both, "narrow", split_axis=0, concat_axis=0, tiled=True)
    rows = GROUPS * part
    by_expert = both.reshape(narrow, 2, local_experts, rows, model_width)
    if rows % 16 == 0:
        back = experts_at_positions(both, w_in, b_in, w_out, b_out)
    else:
        lines = by_expert.transpose(1, 2, 0, 3, 4).reshape(1, 2, -1, model_width)
        back = experts_at_positions(lines, w_in, b_in, w_out, b_out)
        back = back.reshape(2, local_experts, narrow, rows, model_width).transpose(2, 0, 1, 3, 4)
        back = back.reshape(both.shape)

    tokens_sent = by_expert.transpose(2, 0, 1, 3, 4).reshape(
        wide, narrow // share, 2, rows, model_width
    )
    tokens_all = lax.all_to_all(tokens_sent, "wide", split_axis=0, concat_axis=0, tiled=True)
    expert_index = (wide_index // share).astype(jnp.int32)[None]
    grad_in, grad_out = expert_weights(expert_index, tokens_all, w_in, b_in, w_out, wide)
    grad_in = lax.all_to_all(
        grad_in.reshape(wide, model_width // wide, -1), "wide", split_axis=0, concat_axis=0, tiled=True
    )
    hidden_units = w_in.shape[2]
    block = hidden_units // wide
    biases = grad_out[:, block : block + 2]
    grad_out = lax.all_to_all(grad_out[:, :block], "wide", split_axis=0, concat_axis=0, tiled=True)
    bias_out = biases[0, 0]
    bias_in = biases[:, 1, :block].reshape(-1)
    bias = jnp.concatenate([bias_in, bias_out])
    bias = lax.all_to_all(
        jnp.broadcast_to(bias[None, None], (wide, 1, bias.shape[0])),
        "wide",
        split_axis=0,
        concat_axis=0,
        tiled=True,
    )

    def over_share(x):
        x = x.astype(F32).reshape((local_experts, share) + x.shape[1:])
        return jnp.sum(x, axis=1)

    g_w_in, g_w_out = over_share(grad_in), over_share(grad_out)
    bias = over_share(bias)[:, 0]
    g_b_in, g_b_out = bias[:, :hidden_units], bias[:, hidden_units:]

    back = lax.all_to_all(back, "narrow", split_axis=0, concat_axis=0, tiled=True)
    back = back.reshape(narrow, 2, -1, part, model_width)
    back = jnp.pad(back, ((0, 0), (0, 0), (0, 0), (0, padded_part - part), (0, 0)))
    back = back.reshape(narrow, 2, -1, model_width)
    grad_rows, mixed_rows, grad_controller = mix_backward(
        padded_part, spread_probs, mix_rows, cot_rows, probs, back, controllers, row_code, col_code, tile
    )
    grads = to_slots(grad_rows)
    mixed = to_slots(mixed_rows)
    mixed_part = layer_output(place, hidden, mixed)
    mixed_part = place_narrow(gather_narrow(mixed_part), relative)[:slot_count]

    d_hidden, grad_output, grad_gain_mix = hidden_backward(
        place, cotangent, grads, hidden, context, gain_mix_row
    )
    grad_controller = grad_controller.reshape(narrow, local_experts, model_width)[relative]
    grad_output = grad_output.reshape(narrow, head_columns, model_width)
    gain_rows = jnp.broadcast_to(grad_gain_mix[None], (narrow,) + grad_gain_mix.shape)
    first = jnp.concatenate([grad_output, grad_controller, gain_rows], axis=1)
    height = first.shape[1]
    padding = -height % (16 * wide)
    first = jnp.pad(first, ((0, 0), (0, padding), (0, 0))).astype(BF16)
    first = sum_wide(scatter_narrow(first))
    output_weight_gradient = first[:head_columns]
    g_controller = first[head_columns : head_columns + local_experts].T
    g_gain_mix = first[head_columns + local_experts]

    extra = -(3 * model_width + 16) % (16 * wide) + 16
    d_tokens, second = attention_backward(
        place, tokens, d_hidden, q, k, v, packs, gain_attn_row, extra
    )
    d_tokens = place_narrow(gather_narrow(d_tokens), relative)[:slot_count]
    if joined > 1:
        tail = second[:, 3 * model_width :]
        second = second[:, : 3 * model_width].reshape(narrow // joined, 3 * model_width, joined, -1)
        second = second.transpose(0, 2, 1, 3).reshape(narrow, 3 * model_width, head_columns)
        second = jnp.pad(second, ((0, 0), (0, 0), (0, LANES - head_columns)))
        second = jnp.concatenate([second, jnp.repeat(tail, joined, axis=0)], axis=1)
    second = sum_wide(scatter_narrow(second))
    projections = second[: 3 * model_width, :head_columns].reshape(3, model_width, head_columns)
    g_gain_attn = second[3 * model_width : 3 * model_width + model_width // LANES].reshape(-1)

    return (
        mixed_part,
        d_tokens,
        projections[0],
        projections[1],
        projections[2],
        output_weight_gradient,
        g_gain_attn,
        g_gain_mix,
        g_controller,
        g_w_in,
        g_b_in,
        g_w_out,
        g_b_out,
    )


def solution(mesh):
    placed = (
        P("wide", None, None),
        P("wide", None, None),
        P(),
        P(),
        P(None, "narrow"),
        P(None, "narrow"),
        P(None, "narrow"),
        P("narrow", None),
        P(),
        P(),
        P(None, "narrow"),
        P("narrow", None, None),
        P("narrow", None),
        P("narrow", None, None),
        P("narrow", None),
    )
    return jax.shard_map(
        body,
        mesh=mesh,
        in_specs=placed,
        out_specs=(
            P("wide", None, None),
            P("wide", None, None),
            P(None, "narrow"),
            P(None, "narrow"),
            P(None, "narrow"),
            P("narrow", None),
            P(),
            P(),
            P(None, "narrow"),
            P("narrow", "wide", None),
            P("narrow", None),
            P("narrow", "wide", None),
            P("narrow", None),
        ),
        check_vma=False,
    )
```

```python
import functools

import jax
import jax.numpy as jnp
from jax import lax
from jax.experimental import pallas as pl
from jax.experimental.pallas import tpu as pltpu
from jax.sharding import PartitionSpec as P

HEAD_WIDTH = 64
GROUP = 32
GROUPS = 2
LANES = 128

EPSILON = 1e-05
NEGATIVE = -1e30
BOTH = ("wide", "narrow")
F32 = jnp.float32
BF16 = jnp.bfloat16
VMEM_LIMIT = 56 * 1024 * 1024


def mm(a, b):
    return lax.dot_general(a, b, (((1,), (0,)), ((), ())), preferred_element_type=F32)


def mm_nt(a, b):
    return lax.dot_general(a, b, (((1,), (1,)), ((), ())), preferred_element_type=F32)


def mm_tn(a, b):
    return lax.dot_general(a, b, (((0,), (0,)), ((), ())), preferred_element_type=F32)


def params(*semantics):
    return pltpu.CompilerParams(dimension_semantics=semantics or None, vmem_limit_bytes=VMEM_LIMIT)


def whole(shape):
    zeros = (0,) * len(shape)
    return pl.BlockSpec(tuple(shape), lambda *_: zeros)


def head_masks(rows):
    lane = lax.broadcasted_iota(jnp.int32, (rows, LANES), 1)
    return [(lane >= h * HEAD_WIDTH) & (lane < (h + 1) * HEAD_WIDTH) for h in range(LANES // HEAD_WIDTH)]


def keep(mask, rows):
    return jnp.where(mask, rows, jnp.zeros_like(rows))


def causal_probs(query_head, keys, causal):
    scores = mm_nt(query_head, keys) * (float(HEAD_WIDTH) ** -0.5)
    scores = jnp.where(causal, scores, NEGATIVE)
    powers = jnp.exp(scores - jnp.max(scores, axis=-1, keepdims=True))
    return powers / jnp.sum(powers, axis=-1, keepdims=True)


def causal_mask(length):
    return lax.broadcasted_iota(jnp.int32, (length, length), 0) >= lax.broadcasted_iota(
        jnp.int32, (length, length), 1
    )


def inverse_rms(rows):
    return lax.rsqrt(jnp.mean(rows * rows, axis=-1, keepdims=True) + EPSILON)


def attention_kernel(blocks, place, tokens, *refs):
    packs = refs[:blocks]
    gain_attn, gain_mix, mix_out, hidden_out, q_out, k_out, v_out, context_out = refs[blocks:]
    rows = tokens[0].astype(F32)
    length, width = rows.shape
    entry = (rows * inverse_rms(rows) * gain_attn[...]).astype(BF16)
    causal = causal_mask(length)
    masks = head_masks(length)
    attention = jnp.zeros((length, width), F32)
    for j in range(blocks):
        at = slice(j * LANES, (j + 1) * LANES)
        joint = mm(entry, packs[j][:, : 3 * LANES]).astype(BF16)
        q, k, v = (joint[:, i * LANES : (i + 1) * LANES] for i in range(3))
        context = jnp.zeros((length, LANES), F32)
        for mask in masks:
            probs = causal_probs(keep(mask, q), k, causal)
            context = context + mm(probs.astype(BF16), keep(mask, v))
        context = context.astype(BF16)
        attention = attention + mm_nt(context, packs[j][:, 3 * LANES :])
        q_out[0, :, at] = q
        k_out[0, :, at] = k
        v_out[0, :, at] = v
        context_out[0, :, at] = context
    hidden = rows + attention
    mixed = hidden * inverse_rms(hidden) * gain_mix[...]
    mix_out[...] = mixed.reshape(mix_out.shape).astype(BF16)
    hidden_out[0] = hidden


def attention_forward(place, tokens, packs, gain_attn, gain_mix, slots, spread):
    total, length, width = tokens.shape
    inner = packs[0].shape[1] // 4 * len(packs)
    part = length // spread

    def own(i, place):
        return (jnp.minimum(place[0] + i, total - 1), 0, 0)

    def local(i, place):
        return (i, 0, 0)

    saved = jax.ShapeDtypeStruct((slots, length, inner), BF16)
    return pl.pallas_call(
        functools.partial(attention_kernel, len(packs)),
        grid_spec=pltpu.PrefetchScalarGridSpec(
            num_scalar_prefetch=1,
            grid=(slots,),
            in_specs=[pl.BlockSpec((1, length, width), own)]
            + [whole(p.shape) for p in packs]
            + [whole((1, width))] * 2,
            out_specs=[
                pl.BlockSpec((spread, 1, part, width), lambda i, place: (0, i, 0, 0)),
                pl.BlockSpec((1, length, width), local),
            ]
            + [pl.BlockSpec((1, length, inner), local)] * 4,
        ),
        out_shape=[
            jax.ShapeDtypeStruct((spread, slots, part, width), BF16),
            jax.ShapeDtypeStruct((slots, length, width), F32),
        ]
        + [saved] * 4,
        compiler_params=params("arbitrary"),
        cost_estimate=pl.CostEstimate(
            flops=slots * 2 * length * (4 * width * inner + 4 * length * inner),
            bytes_accessed=slots * length * width * 16 + 4 * width * inner * 2,
            transcendentals=slots * length * length * inner // HEAD_WIDTH,
        ),
        name="attention_forward",
    )(place, tokens, *packs, gain_attn, gain_mix)


def slot_softmax(logits, codes, part):
    experts = logits.shape[1]
    logits = logits.reshape(-1, part, experts)
    codes = jnp.broadcast_to(codes, (codes.shape[0], experts)).reshape(-1, part, experts)
    total = jnp.zeros_like(logits)
    for g in range(GROUPS):
        inside = (codes >= g * part) & (codes < (g + 1) * part)
        held = jnp.where(inside, logits, NEGATIVE)
        powers = jnp.where(inside, jnp.exp(held - jnp.max(held, axis=0, keepdims=True)), 0.0)
        total = total + powers / jnp.sum(powers, axis=0, keepdims=True)
    return total.reshape(-1, experts)


def group_totals(terms, codes, part):
    experts = terms.shape[1]
    terms = terms.reshape(-1, part, experts)
    codes = jnp.broadcast_to(codes, (codes.shape[0], experts)).reshape(-1, part, experts)
    total = jnp.zeros_like(terms)
    for g in range(GROUPS):
        inside = (codes >= g * part) & (codes < (g + 1) * part)
        total = jnp.where(inside, jnp.sum(jnp.where(inside, terms, 0.0), axis=0, keepdims=True), total)
    return total.reshape(-1, experts)


def mix_kernel(part, relative, rows, cots, controller, row_code, col_code, tile, probs_out, spread_out, *refs):
    sent, (merged, grads) = refs[:-2], refs[-2:]
    held = rows[...]
    probs = slot_softmax(mm(held, controller[...]), row_code[...], part)
    probs_out[...] = probs
    wide = mm(probs.astype(BF16), tile[...])
    spread = jnp.where(row_code[...] == col_code[...], wide, 0.0).astype(BF16)
    spread_out[...] = spread
    block = sent[0].shape[1]
    merged[...] = mm_tn(spread, held).astype(BF16)
    grads[...] = mm_tn(spread, cots[...]).astype(BF16)
    for j, out in enumerate(sent):
        at = pl.ds(pl.multiple_of(relative[j] * block, block), block)
        out[0] = merged[at]
        out[1] = grads[at]


def mix_forward(part, relative, rows, cots, controller, row_code, col_code, tile, narrow):
    count, width = rows.shape
    experts, columns = tile.shape
    block = columns // narrow
    return pl.pallas_call(
        functools.partial(mix_kernel, part),
        grid_spec=pltpu.PrefetchScalarGridSpec(
            num_scalar_prefetch=1,
            grid=(1,),
            in_specs=[whole(x.shape) for x in (rows, cots, controller, row_code, col_code, tile)],
            out_specs=[whole((count, experts)), whole((count, columns))]
            + [whole((2, block, width))] * narrow,
            scratch_shapes=[pltpu.VMEM((columns, width), BF16)] * 2,
        ),
        out_shape=[
            jax.ShapeDtypeStruct((count, experts), F32),
            jax.ShapeDtypeStruct((count, columns), BF16),
        ]
        + [jax.ShapeDtypeStruct((2, block, width), BF16)] * narrow,
        compiler_params=params("arbitrary"),
        cost_estimate=pl.CostEstimate(
            flops=4 * count * columns * width,
            bytes_accessed=6 * count * width * 2,
            transcendentals=count * experts * 2,
        ),
        name="mix_forward",
    )(relative, rows, cots, controller, row_code, col_code, tile)


def unmix_kernel(
    part, narrow, relative, spread, rows, cots, probs, controller, row_code, col_code, tile, *refs
):
    back, (grad_out, mixed_out, gain_out, outs, grads) = refs[:narrow], refs[narrow:]
    block = back[0].shape[1]
    for j, piece in enumerate(back):
        at = pl.ds(pl.multiple_of(relative[j] * block, block), block)
        outs[at] = piece[0]
        grads[at] = piece[1]
    held = rows[...]
    pairs = (mm_nt(cots[...], outs[...]) + mm_nt(held, grads[...])).astype(BF16)
    pairs = jnp.where(row_code[...] == col_code[...], pairs, jnp.zeros_like(pairs))
    d_weights = mm_nt(pairs, tile[...])
    p = probs[...]
    d_logits = (p * (d_weights - group_totals(p * d_weights, row_code[...], part))).astype(BF16)
    grad_out[...] = (mm(spread[...], grads[...]) + mm_nt(d_logits, controller[...])).astype(BF16)
    mixed_out[...] = mm(spread[...], outs[...]).astype(BF16)
    gain_out[...] = mm_tn(d_logits, held)


def mix_backward(part, relative, spread, rows, cots, probs, back, controller, row_code, col_code, tile):
    count, width = rows.shape
    experts, columns = tile.shape
    operands = (spread, rows, cots, probs, controller, row_code, col_code, tile) + tuple(back)
    outs = [
        jax.ShapeDtypeStruct((count, width), BF16),
        jax.ShapeDtypeStruct((count, width), BF16),
        jax.ShapeDtypeStruct((experts, width), F32),
    ]
    return pl.pallas_call(
        functools.partial(unmix_kernel, part, len(back)),
        grid_spec=pltpu.PrefetchScalarGridSpec(
            num_scalar_prefetch=1,
            grid=(1,),
            in_specs=[whole(x.shape) for x in operands],
            out_specs=[whole(x.shape) for x in outs],
            scratch_shapes=[pltpu.VMEM((columns, width), BF16)] * 2,
        ),
        out_shape=outs,
        compiler_params=params("arbitrary"),
        cost_estimate=pl.CostEstimate(
            flops=8 * count * columns * width,
            bytes_accessed=8 * count * width * 2,
            transcendentals=0,
        ),
        name="mix_backward",
    )(relative, *operands)


GELU_SLOPE = 0.7978845608028654
GELU_CUBE = 0.044715


def gelu_pair(x):
    square = x * x
    bend = jnp.tanh(GELU_SLOPE * x * (1.0 + GELU_CUBE * square))
    gate = 0.5 * (1.0 + bend)
    slope = gate + 0.5 * x * (1.0 - bend * bend) * (GELU_SLOPE * (1.0 + 3.0 * GELU_CUBE * square))
    return x * gate, slope


def expert_kernel(count, *refs):
    both, (w_in, b_in, w_out, b_out), sent = refs[:count], refs[count : count + 4], refs[count + 4 :]
    rows = both[0].shape[1]
    merged = jnp.concatenate([x[0] for x in both], axis=0)
    grads = jnp.concatenate([x[1] for x in both], axis=0)
    act, slope = gelu_pair(mm(merged, w_in[0]) + b_in[0])
    outs = mm(act.astype(BF16), w_out[0]) + b_out[0]
    d_pre = (mm_nt(grads, w_out[0]) * slope).astype(BF16)
    d_merged = mm_nt(d_pre, w_in[0])
    for j, out in enumerate(sent):
        at = slice(j * rows, (j + 1) * rows)
        out[0] = outs[at].astype(BF16)
        out[1] = d_merged[at].astype(BF16)


def experts_at_positions(both, w_in, b_in, w_out, b_out):
    _, count, width = both[0].shape
    experts, _, inner = w_in.shape
    sources = len(both)
    tokens = pl.BlockSpec((2, count // experts, width), lambda e: (0, e, 0))
    return pl.pallas_call(
        functools.partial(expert_kernel, sources),
        grid=(experts,),
        in_specs=[tokens] * sources
        + [
            pl.BlockSpec((1, width, inner), lambda e: (e, 0, 0)),
            pl.BlockSpec((1, 1, inner), lambda e: (e, 0, 0)),
            pl.BlockSpec((1, inner, width), lambda e: (e, 0, 0)),
            pl.BlockSpec((1, 1, width), lambda e: (e, 0, 0)),
        ],
        out_specs=[tokens] * sources,
        out_shape=[jax.ShapeDtypeStruct(x.shape, BF16) for x in both],
        compiler_params=params("arbitrary"),
        cost_estimate=pl.CostEstimate(
            flops=8 * sources * count * width * inner,
            bytes_accessed=4 * experts * width * inner + 4 * sources * count * width * 2,
            transcendentals=sources * count * inner,
        ),
        name="experts",
    )(*both, w_in, b_in[:, None], w_out, b_out[:, None])


def weight_kernel(units, where, both, w_in, b_in, w_out, g_in, g_out, bias_out, merged, grads, total):
    i = pl.program_id(1)
    width = both.shape[-1]
    half, unit = where[0], where[1]
    span = total.shape[0]
    block = w_out.shape[1]

    @pl.when(i == 0)
    def _():
        merged[...] = both[:, 0, :, 0].reshape(merged.shape)
        grads[...] = both[:, 0, :, 1].reshape(grads.shape)
        bias_out[...] = jnp.zeros_like(bias_out)
        sums = jnp.sum(grads[...].astype(F32), axis=0, keepdims=True)
        bias_out[0, 1:2, :width] = sums

    act, slope = gelu_pair(mm(merged[...], w_in[0]) + b_in[0])
    d_pre = (mm_nt(grads[...], w_out[0]) * slope).astype(BF16)
    bias_out[0, 0:1, pl.ds(pl.multiple_of(i * block, block), block)] = jnp.sum(
        d_pre.astype(F32), axis=0, keepdims=True
    )
    total[...] = mm_tn(merged[:, pl.ds(pl.multiple_of(half * span, span), span)], d_pre)
    rows = span // units
    for d in range(units):
        at = pl.ds(pl.multiple_of(lax.bitwise_xor(unit, d) * rows, rows), rows)
        g_in[d, 0] = total[at].astype(BF16)

    @pl.when((i >= half * units) & (i < (half + 1) * units))
    def _():
        g_out[0, 0] = mm_tn(act.astype(BF16), grads[...]).astype(BF16)


def expert_weights(where, first, both, w_in, b_in, w_out, wide, units):
    sources, held, inner_sources, _, rows, width = both.shape
    inner = w_in.shape[2]
    block = inner // wide
    count = sources * inner_sources * rows
    span = width * units // wide

    def out_block(p, i, where, first):
        return (lax.bitwise_xor(jnp.clip(i - where[0] * units, 0, units - 1), where[1]), p, 0, 0)

    return pl.pallas_call(
        lambda where, first, *refs: weight_kernel(units, where, *refs),
        grid_spec=pltpu.PrefetchScalarGridSpec(
            num_scalar_prefetch=2,
            grid=(held, wide),
            in_specs=[
                pl.BlockSpec(
                    (sources, 1, inner_sources, 2, rows, width), lambda p, i, w, f: (0, p, 0, 0, 0, 0)
                ),
                pl.BlockSpec((1, width, block), lambda p, i, w, f: (f[0] + p, 0, i)),
                pl.BlockSpec((1, 1, block), lambda p, i, w, f: (f[0] + p, 0, i)),
                pl.BlockSpec((1, block, width), lambda p, i, w, f: (f[0] + p, i, 0)),
            ],
            out_specs=[
                pl.BlockSpec((units, 1, span // units, block), lambda p, i, w, f: (0, p, 0, i)),
                pl.BlockSpec((1, 1, block, width), out_block),
                pl.BlockSpec((1, 8, inner), lambda p, i, w, f: (p, 0, 0)),
            ],
            scratch_shapes=[pltpu.VMEM((count, width), BF16)] * 2 + [pltpu.VMEM((span, block), F32)],
        ),
        out_shape=[
            jax.ShapeDtypeStruct((units, held, span // units, inner), BF16),
            jax.ShapeDtypeStruct((units, held, block, width), BF16),
            jax.ShapeDtypeStruct((held, 8, inner), F32),
        ],
        compiler_params=params("arbitrary", "arbitrary"),
        cost_estimate=pl.CostEstimate(
            flops=held * 6 * count * width * inner,
            bytes_accessed=held * (8 * width * inner + 4 * count * width),
            transcendentals=held * count * inner,
        ),
        name="expert_weights",
    )(where, first, both, w_in, b_in[:, None], w_out)


def attention_back_kernel(blocks, place, tokens, cots, grads, hidden, q_in, k_in, v_in, context, *refs):
    packs = refs[:blocks]
    gain_attn, gain_mix, d_tokens_out, weight_out, total, gains = refs[blocks:]
    i = pl.program_id(0)
    length, width = hidden.shape[1:]
    scale = float(HEAD_WIDTH) ** -0.5
    live = (place[0] + i < place[1]).astype(F32)

    @pl.when(i == 0)
    def _():
        total[...] = jnp.zeros_like(total)
        gains[...] = jnp.zeros_like(gains)

    rows = hidden[0]
    inverse = inverse_rms(rows)
    normed = rows * inverse
    grad = grads[...].astype(F32).reshape(length, width)
    gains[1:2] += jnp.sum(grad * normed, axis=0, keepdims=True)
    d_normed = grad * gain_mix[...]
    d_hidden = cots[0].astype(F32) * live + inverse * (
        d_normed - normed * jnp.mean(d_normed * normed, axis=-1, keepdims=True)
    )
    d_low = d_hidden.astype(BF16)

    rows = tokens[0].astype(F32)
    inverse = inverse_rms(rows)
    normed = rows * inverse
    entry = (normed * gain_attn[...]).astype(BF16)
    causal = causal_mask(length)
    masks = head_masks(length)
    d_entry = jnp.zeros((length, width), F32)
    for j in range(blocks):
        at = slice(j * LANES, (j + 1) * LANES)
        q, k, v = q_in[0, :, at], k_in[0, :, at], v_in[0, :, at]
        d_context = mm(d_low, packs[j][:, 3 * LANES :]).astype(BF16)
        d_q = jnp.zeros((length, LANES), F32)
        d_k = jnp.zeros((length, LANES), F32)
        d_v = jnp.zeros((length, LANES), F32)
        for mask in masks:
            q_head = keep(mask, q)
            d_head = keep(mask, d_context)
            probs = causal_probs(q_head, k, causal)
            d_probs = mm_nt(d_head, v).astype(BF16).astype(F32)
            d_scores = probs * (d_probs - jnp.sum(probs * d_probs, axis=-1, keepdims=True))
            d_scores = d_scores.astype(BF16)
            d_v = d_v + mm_tn(probs.astype(BF16), d_head)
            d_q = d_q + mm(d_scores, keep(mask, k))
            d_k = d_k + mm_tn(d_scores, q_head)
        joint = jnp.concatenate([d_q * scale, d_k * scale, d_v], axis=1).astype(BF16)
        d_entry = d_entry + mm_nt(joint, packs[j][:, : 3 * LANES])
        grad = mm_tn(entry, joint)
        for c in range(3):
            total[j, c * width : (c + 1) * width] += grad[:, c * LANES : (c + 1) * LANES]
        total[j, 3 * width : 4 * width] += mm_tn(d_low, context[0, :, at])
    d_entry = d_entry.astype(BF16).astype(F32)
    gains[0:1] += jnp.sum(d_entry * normed, axis=0, keepdims=True)
    d_normed = d_entry * gain_attn[...]
    d_tokens = d_hidden + inverse * (
        d_normed - normed * jnp.mean(d_normed * normed, axis=-1, keepdims=True)
    )
    d_tokens_out[0] = (d_tokens * live).astype(BF16)

    @pl.when(i == pl.num_programs(0) - 1)
    def _():
        height = 4 * width
        pieces = width // LANES
        tail = [gains[r : r + 1, c * LANES : (c + 1) * LANES] for r in range(2) for c in range(pieces)]
        tail = jnp.concatenate(tail + [jnp.zeros((16 - 2 * pieces, LANES), F32)], axis=0).astype(BF16)
        for j in range(blocks):
            weight_out[j, :height] = total[j].astype(BF16)
            weight_out[j, height:] = tail


def attention_backward(place, tokens, cotangent, grads, hidden, q, k, v, context, packs, gain_attn, gain_mix):
    total, length, width = tokens.shape
    spread, slots, part, _ = grads.shape
    inner = q.shape[2]
    blocks = len(packs)

    def own(i, place):
        return (jnp.minimum(place[0] + i, total - 1), 0, 0)

    def local(i, place):
        return (i, 0, 0)

    return pl.pallas_call(
        functools.partial(attention_back_kernel, blocks),
        grid_spec=pltpu.PrefetchScalarGridSpec(
            num_scalar_prefetch=1,
            grid=(slots,),
            in_specs=[
                pl.BlockSpec((1, length, width), own),
                pl.BlockSpec((1, length, width), own),
                pl.BlockSpec((spread, 1, part, width), lambda i, place: (0, i, 0, 0)),
                pl.BlockSpec((1, length, width), local),
            ]
            + [pl.BlockSpec((1, length, inner), local)] * 4
            + [whole(p.shape) for p in packs]
            + [whole((1, width))] * 2,
            out_specs=[
                pl.BlockSpec((1, length, width), local),
                whole((blocks, 4 * width + 16, LANES)),
            ],
            scratch_shapes=[
                pltpu.VMEM((blocks, 4 * width, LANES), F32),
                pltpu.VMEM((8, width), F32),
            ],
        ),
        out_shape=[
            jax.ShapeDtypeStruct((slots, length, width), BF16),
            jax.ShapeDtypeStruct((blocks, 4 * width + 16, LANES), BF16),
        ],
        compiler_params=params("arbitrary"),
        cost_estimate=pl.CostEstimate(
            flops=slots * 2 * length * (8 * width * inner + 10 * length * inner),
            bytes_accessed=slots * length * width * 18 + 8 * width * inner * 2,
            transcendentals=slots * length * length * inner // HEAD_WIDTH,
        ),
        name="attention_backward",
    )(place, tokens, cotangent, grads, hidden, q, k, v, context, *packs, gain_attn, gain_mix)


def output_kernel(place, hidden, mixed, out):
    live = (place[0] + pl.program_id(0) < place[1]).astype(F32)
    rows = mixed[...].astype(F32).reshape(hidden.shape[1:])
    out[0] = (live * (hidden[0] + rows)).astype(BF16)


def layer_output(place, hidden, mixed):
    spread, slots, part, width = mixed.shape
    length = hidden.shape[1]
    return pl.pallas_call(
        output_kernel,
        grid_spec=pltpu.PrefetchScalarGridSpec(
            num_scalar_prefetch=1,
            grid=(slots,),
            in_specs=[
                pl.BlockSpec((1, length, width), lambda i, place: (i, 0, 0)),
                pl.BlockSpec((spread, 1, part, width), lambda i, place: (0, i, 0, 0)),
            ],
            out_specs=pl.BlockSpec((1, length, width), lambda i, place: (i, 0, 0)),
        ),
        out_shape=jax.ShapeDtypeStruct((slots, length, width), BF16),
        compiler_params=params("arbitrary"),
        cost_estimate=pl.CostEstimate(
            flops=slots * length * width * 3, bytes_accessed=slots * length * width * 8, transcendentals=0
        ),
        name="layer_output",
    )(place, hidden, mixed)


def swap_core(x):
    narrow = lax.axis_size("narrow")
    return lax.ppermute(x, "narrow", [(n, n ^ 1) for n in range(narrow)])


def from_chip(x, k):
    narrow = lax.axis_size("narrow")
    return lax.ppermute(x, "narrow", [((n + 2 * k) % narrow, n) for n in range(narrow)])


def to_chip(x, k):
    narrow = lax.axis_size("narrow")
    return lax.ppermute(x, "narrow", [(n, (n + 2 * k) % narrow) for n in range(narrow)])


def relative_narrow():
    narrow = lax.axis_size("narrow")
    me = lax.axis_index("narrow")
    chips = [lax.rem(me + 2 * k, narrow) for k in range(narrow // 2)]
    return chips + [lax.bitwise_xor(n, 1) for n in chips]


def gather_narrow(x):
    chips = [x] + [from_chip(x, k) for k in range(1, lax.axis_size("narrow") // 2)]
    return chips + [swap_core(piece) for piece in chips]


def scatter_narrow(x):
    chips = x.shape[0] // 2
    summed = x[:chips].astype(F32) + swap_core(x[chips:]).astype(F32)
    low = summed.astype(BF16)
    result = summed[0]
    for k in range(1, chips):
        result = result + to_chip(low[k], k).astype(F32)
    return result


def sum_wide(x):
    wide = lax.axis_size("wide")
    parts = x.astype(BF16).reshape(wide, x.shape[0] // wide, x.shape[1])
    parts = lax.all_to_all(parts, "wide", split_axis=0, concat_axis=0, tiled=True)
    part = jnp.sum(parts.astype(F32), axis=0).astype(BF16)
    parts = jnp.broadcast_to(part[None], parts.shape)
    parts = lax.all_to_all(parts, "wide", split_axis=0, concat_axis=0, tiled=True)
    return parts.reshape(x.shape).astype(F32)


def to_relative(x, j):
    narrow = lax.axis_size("narrow")
    k, other = j % (narrow // 2), j // (narrow // 2)
    return lax.ppermute(x, "narrow", [(n, ((n + 2 * k) % narrow) ^ other) for n in range(narrow)])


def from_relative(x, j):
    narrow = lax.axis_size("narrow")
    k, other = j % (narrow // 2), j // (narrow // 2)
    return lax.ppermute(x, "narrow", [(((n + 2 * k) % narrow) ^ other, n) for n in range(narrow)])


def to_unit(x, d):
    wide = lax.axis_size("wide")
    return lax.ppermute(x, "wide", [(w, w ^ d) for w in range(wide)])


def place_kernel(count, where, *refs):
    out = refs[count]
    for j in range(count):

        @pl.when(pl.program_id(0) == j)
        def _(j=j):
            out[...] = refs[j][...].astype(out.dtype)


def place_blocks(pieces, where, dtype):
    count = len(pieces)
    shape = pieces[0].shape
    zeros = (0,) * (len(shape) - 1)
    return pl.pallas_call(
        functools.partial(place_kernel, count),
        grid_spec=pltpu.PrefetchScalarGridSpec(
            num_scalar_prefetch=1,
            grid=(count,),
            in_specs=[whole(shape)] * count,
            out_specs=pl.BlockSpec(shape, lambda i, where: (where[i],) + zeros),
        ),
        out_shape=jax.ShapeDtypeStruct((count * shape[0],) + shape[1:], dtype),
        compiler_params=params("arbitrary"),
        cost_estimate=pl.CostEstimate(
            flops=0, bytes_accessed=pieces[0].size * 8 * count, transcendentals=0
        ),
        name="place_blocks",
    )(where, *pieces)


def body(
    tokens,
    cotangent,
    counts,
    group_order,
    query_weight,
    key_weight,
    value_weight,
    output_weight,
    gain_attn,
    gain_mix,
    controller,
    w_in,
    b_in,
    w_out,
    b_out,
):
    slot_count, seq_len, model_width = tokens.shape
    wide, narrow = lax.axis_size("wide"), lax.axis_size("narrow")
    spread = wide * narrow
    wide_index, narrow_index = lax.axis_index("wide"), lax.axis_index("narrow")
    slots = -(-slot_count // narrow)
    part = seq_len // spread
    padded_part = -(-part // 8) * 8
    local_experts = w_in.shape[0]
    experts = local_experts * narrow
    relative = jnp.stack(relative_narrow())
    head_columns = query_weight.shape[1]

    seq_ends = jnp.cumsum(counts)
    seq_starts = seq_ends - counts
    own_count = counts[wide_index]
    place = jnp.stack([narrow_index * slots, own_count]).astype(jnp.int32)
    slot_ids = jnp.arange(slots * narrow)
    slot_seqs = jnp.where(slot_ids[None] < counts[:, None], seq_starts[:, None] + slot_ids[None], -1)
    matches = slot_seqs.reshape(-1, 1) == group_order[None]
    slot_group = jnp.sum(jnp.where(matches, 1 + jnp.arange(group_order.shape[0]) // GROUP, 0), axis=1) - 1
    positions = jnp.arange(padded_part)
    row_code = jnp.where(slot_group[:, None] >= 0, slot_group[:, None] * padded_part + positions, -1)
    row_code = row_code.reshape(-1, 1).astype(jnp.int32)
    per_expert = GROUPS * padded_part
    col_code = (jnp.arange(experts * per_expert) % per_expert).astype(jnp.int32)[None]
    tile = jnp.repeat(jnp.eye(experts, dtype=BF16), per_expert, axis=1)

    pack = jnp.stack([query_weight, key_weight, value_weight, output_weight.T], axis=1)
    joined = LANES // head_columns
    packs = gather_narrow(pack.reshape(model_width, -1))
    if joined > 1:
        packs = [p.reshape(model_width, 4, head_columns) for p in packs]
        packs = [
            jnp.concatenate(packs[i : i + joined], axis=2).reshape(model_width, -1)
            for i in range(0, narrow, joined)
        ]
    controllers = jnp.stack(gather_narrow(controller.T))
    controllers = controllers[jnp.argsort(relative)].reshape(experts, model_width).T

    gain_attn_row, gain_mix_row = gain_attn[None], gain_mix[None]

    def own_slots(x):
        x = jnp.pad(x, ((0, slots * narrow - slot_count), (0, 0), (0, 0)))
        return lax.dynamic_slice_in_dim(x, narrow_index * slots, slots)

    def to_positions(x):
        x = lax.all_to_all(x, BOTH, split_axis=0, concat_axis=0, tiled=True)
        x = jnp.pad(x, ((0, 0), (0, 0), (0, padded_part - part), (0, 0)))
        return x.reshape(-1, model_width)

    def to_slots(x):
        x = x.reshape(spread, slots, padded_part, model_width)[:, :, :part]
        return lax.all_to_all(x, BOTH, split_axis=0, concat_axis=0, tiled=True)

    cot_sent = own_slots(cotangent).reshape(slots, spread, part, model_width).transpose(1, 0, 2, 3)
    cot_rows = to_positions(cot_sent)

    mix_sent, hidden, q, k, v, context = attention_forward(
        place, tokens, packs, gain_attn_row, gain_mix_row, slots, spread
    )
    mix_rows = to_positions(mix_sent)
    probs, spread_probs, *both = mix_forward(
        padded_part, relative, mix_rows, cot_rows, controllers, row_code, col_code, tile, narrow
    )

    def trim(x):
        return x.reshape(2, -1, padded_part, model_width)[:, :, :part].reshape(2, -1, model_width)

    def untrim(x):
        x = x.reshape(2, -1, part, model_width)
        x = jnp.pad(x, ((0, 0), (0, 0), (0, padded_part - part), (0, 0)))
        return x.reshape(2, -1, model_width)

    both = [trim(x) for x in both]
    both = both[:1] + [to_relative(x, j) for j, x in enumerate(both) if j]
    rows = GROUPS * part
    by_expert = jnp.stack(both).reshape(narrow, 2, local_experts, rows, model_width)
    halves = 2 if wide % 4 == 0 else 1
    units = wide // halves
    held, share = max(local_experts // units, 1), max(units // local_experts, 1)
    unit = lax.rem(wide_index, units)
    tokens_sent = by_expert.transpose(2, 0, 1, 3, 4).reshape(
        units, held, narrow // share, 2, rows, model_width
    )
    tokens_sent = jnp.concatenate([tokens_sent] * halves)
    tokens_sent, both = lax.optimization_barrier((tokens_sent, both))
    tokens_all = lax.all_to_all(tokens_sent, "wide", split_axis=0, concat_axis=0, tiled=True)
    if rows % 16 == 0:
        back = experts_at_positions(both, w_in, b_in, w_out, b_out)
    else:
        lines = by_expert.transpose(1, 2, 0, 3, 4).reshape(2, -1, model_width)
        (back,) = experts_at_positions([lines], w_in, b_in, w_out, b_out)
        back = back.reshape(2, local_experts, narrow, rows, model_width).transpose(2, 0, 1, 3, 4)
        back = list(back.reshape(narrow, 2, -1, model_width))

    where = jnp.stack([wide_index // units, unit]).astype(jnp.int32)
    first = (unit * held // share).astype(jnp.int32)[None]
    grad_in, grad_out, bias = expert_weights(
        where, first, tokens_all, w_in, b_in, w_out, wide, units
    )

    back = [untrim(x if j == 0 else from_relative(x, j)) for j, x in enumerate(back)]
    grad_rows, mixed_rows, grad_controller = mix_backward(
        padded_part, relative, spread_probs, mix_rows, cot_rows, probs, back, controllers, row_code, col_code, tile
    )
    grads = to_slots(grad_rows)
    mixed_rows, grad_in, grad_out, bias, grads = lax.optimization_barrier(
        (mixed_rows, grad_in, grad_out, bias, grads)
    )
    mixed = to_slots(mixed_rows)

    def by_unit(pieces, dtype):
        pieces = [pieces[0]] + [to_unit(pieces[d], d) for d in range(1, units)]
        order = lax.bitwise_xor(unit, jnp.arange(units))
        if share == 1:
            return place_blocks(pieces, order, dtype)
        pieces = jnp.stack(pieces)[order].astype(F32)
        return jnp.sum(pieces.reshape((local_experts, share) + pieces.shape[2:]), axis=1)

    g_w_in, g_w_out = by_unit(grad_in, F32), by_unit(grad_out, F32)
    bias = by_unit([bias] * units, F32)
    g_b_in, g_b_out = bias[:, 0], bias[:, 1, :model_width]

    mixed_part = layer_output(place, hidden, mixed)
    mixed_part = place_blocks(gather_narrow(mixed_part), relative, BF16)[:slot_count]

    d_tokens, weights = attention_backward(
        place, tokens, cotangent, grads, hidden, q, k, v, context, packs, gain_attn_row, gain_mix_row
    )
    d_tokens = place_blocks(gather_narrow(d_tokens), relative, BF16)[:slot_count]
    height = 4 * model_width
    if joined > 1:
        tail = weights[:, height:]
        weights = weights[:, :height].reshape(narrow // joined, height, joined, -1)
        weights = weights.transpose(0, 2, 1, 3).reshape(narrow, height, head_columns)
        weights = jnp.pad(weights, ((0, 0), (0, 0), (0, LANES - head_columns)))
        weights = jnp.concatenate([weights, jnp.repeat(tail, joined, axis=0)], axis=1)
    grad_controller = grad_controller.astype(BF16).reshape(narrow, -1, LANES)[relative]
    end = height + 16 + grad_controller.shape[1]
    weights = jnp.concatenate([weights, grad_controller], axis=1)
    weights = jnp.pad(weights, ((0, 0), (0, -end % (16 * wide)), (0, 0)))
    weights = sum_wide(scatter_narrow(weights))
    projections = weights[:height, :head_columns].reshape(4, model_width, head_columns)
    pieces = model_width // LANES
    g_gain_attn = weights[height : height + pieces].reshape(-1)
    g_gain_mix = weights[height + pieces : height + 2 * pieces].reshape(-1)
    g_controller = weights[height + 16 : end].reshape(local_experts, model_width).T
    output_weight_gradient = projections[3].T

    return (
        mixed_part,
        d_tokens,
        projections[0],
        projections[1],
        projections[2],
        output_weight_gradient,
        g_gain_attn,
        g_gain_mix,
        g_controller,
        g_w_in,
        g_b_in,
        g_w_out,
        g_b_out,
    )


def solution(mesh):
    placed = (
        P("wide", None, None),
        P("wide", None, None),
        P(),
        P(),
        P(None, "narrow"),
        P(None, "narrow"),
        P(None, "narrow"),
        P("narrow", None),
        P(),
        P(),
        P(None, "narrow"),
        P("narrow", None, None),
        P("narrow", None),
        P("narrow", None, None),
        P("narrow", None),
    )
    return jax.shard_map(
        body,
        mesh=mesh,
        in_specs=placed,
        out_specs=(
            P("wide", None, None),
            P("wide", None, None),
            P(None, "narrow"),
            P(None, "narrow"),
            P(None, "narrow"),
            P("narrow", None),
            P(),
            P(),
            P(None, "narrow"),
            P("narrow", "wide", None),
            P("narrow", None),
            P("narrow", "wide", None),
            P("narrow", None),
        ),
        check_vma=False,
    )
```

```python
import functools

import jax
import jax.numpy as jnp
from jax import lax
from jax.experimental import pallas as pl
from jax.experimental.pallas import tpu as pltpu
from jax.sharding import PartitionSpec as P

HEAD_WIDTH = 64
GROUP = 32
GROUPS = 2
LANES = 128

EPSILON = 1e-05
NEGATIVE = -1e30
BOTH = ("wide", "narrow")
F32 = jnp.float32
BF16 = jnp.bfloat16
VMEM_LIMIT = 56 * 1024 * 1024


def mm(a, b):
    return lax.dot_general(a, b, (((1,), (0,)), ((), ())), preferred_element_type=F32)


def mm_nt(a, b):
    return lax.dot_general(a, b, (((1,), (1,)), ((), ())), preferred_element_type=F32)


def mm_tn(a, b):
    return lax.dot_general(a, b, (((0,), (0,)), ((), ())), preferred_element_type=F32)


def params(*semantics):
    return pltpu.CompilerParams(dimension_semantics=semantics or None, vmem_limit_bytes=VMEM_LIMIT)


def whole(shape):
    zeros = (0,) * len(shape)
    return pl.BlockSpec(tuple(shape), lambda *_: zeros)


def head_masks(rows):
    lane = lax.broadcasted_iota(jnp.int32, (rows, LANES), 1)
    return [(lane >= h * HEAD_WIDTH) & (lane < (h + 1) * HEAD_WIDTH) for h in range(LANES // HEAD_WIDTH)]


def keep(mask, rows):
    return jnp.where(mask, rows, jnp.zeros_like(rows))


def causal_probs(query_head, keys, causal):
    scores = mm_nt(query_head, keys) * (float(HEAD_WIDTH) ** -0.5)
    scores = jnp.where(causal, scores, NEGATIVE)
    powers = jnp.exp(scores - jnp.max(scores, axis=-1, keepdims=True))
    return powers * (1.0 / jnp.sum(powers, axis=-1, keepdims=True))


def causal_mask(length):
    return lax.broadcasted_iota(jnp.int32, (length, length), 0) >= lax.broadcasted_iota(
        jnp.int32, (length, length), 1
    )


def inverse_rms(rows):
    return lax.rsqrt(jnp.mean(rows * rows, axis=-1, keepdims=True) + EPSILON)


def attend(entry, packs, causal, masks, joint_out, context_out):
    attention = None
    for j, pack in enumerate(packs):
        joint = mm(entry, pack[:, : 3 * LANES]).astype(BF16)
        joint_out[0, :, j * 3 * LANES : (j + 1) * 3 * LANES] = joint
        q, k, v = (joint[:, i * LANES : (i + 1) * LANES] for i in range(3))
        context = None
        for mask in masks:
            probs = causal_probs(keep(mask, q), k, causal)
            term = mm(probs.astype(BF16), keep(mask, v))
            context = term if context is None else context + term
        context = context.astype(BF16)
        context_out[0, :, j * LANES : (j + 1) * LANES] = context
        term = mm_nt(context, pack[:, 3 * LANES :])
        attention = term if attention is None else attention + term
    return attention


def near_kernel(blocks, place, tokens, *refs):
    packs, (gain_attn, partial_out, joint_out, context_out) = refs[:blocks], refs[blocks:]
    rows = tokens[0].astype(F32)
    entry = (rows * inverse_rms(rows) * gain_attn[...]).astype(BF16)
    length = rows.shape[0]
    partial_out[0] = rows + attend(
        entry, packs, causal_mask(length), head_masks(length), joint_out, context_out
    )


def far_kernel(blocks, place, tokens, partial, *refs):
    packs = refs[:blocks]
    gain_attn, gain_mix, mix_out, hidden_out, joint_out, context_out = refs[blocks:]
    rows = tokens[0].astype(F32)
    entry = (rows * inverse_rms(rows) * gain_attn[...]).astype(BF16)
    length = rows.shape[0]
    hidden = partial[0] + attend(
        entry, packs, causal_mask(length), head_masks(length), joint_out, context_out
    )
    mixed = hidden * inverse_rms(hidden) * gain_mix[...]
    mix_out[...] = mixed.reshape(mix_out.shape).astype(BF16)
    hidden_out[0] = hidden


def local_block(i, place):
    return (i, 0, 0)


def attention_near(place, tokens, packs, gain_attn, slots):
    total, length, width = tokens.shape
    inner = len(packs) * LANES
    return pl.pallas_call(
        functools.partial(near_kernel, len(packs)),
        grid_spec=pltpu.PrefetchScalarGridSpec(
            num_scalar_prefetch=1,
            grid=(slots,),
            in_specs=[
                pl.BlockSpec((1, length, width), lambda i, place: (jnp.minimum(place[0] + i, total - 1), 0, 0))
            ]
            + [whole(p.shape) for p in packs]
            + [whole((1, width))],
            out_specs=[
                pl.BlockSpec((1, length, width), local_block),
                pl.BlockSpec((1, length, 3 * inner), local_block),
                pl.BlockSpec((1, length, inner), local_block),
            ],
        ),
        out_shape=[
            jax.ShapeDtypeStruct((slots, length, width), F32),
            jax.ShapeDtypeStruct((slots, length, 3 * inner), BF16),
            jax.ShapeDtypeStruct((slots, length, inner), BF16),
        ],
        compiler_params=params("arbitrary"),
        cost_estimate=pl.CostEstimate(
            flops=slots * 2 * length * (4 * width * inner + 4 * length * inner),
            bytes_accessed=slots * length * (width * 6 + inner * 8) + 8 * width * inner,
            transcendentals=slots * length * length * inner // HEAD_WIDTH,
        ),
        name="attention_near",
    )(place, tokens, *packs, gain_attn)


def attention_far(place, tokens, partial, packs, gain_attn, gain_mix, slots, spread):
    total, length, width = tokens.shape
    inner = len(packs) * LANES
    part = length // spread
    return pl.pallas_call(
        functools.partial(far_kernel, len(packs)),
        grid_spec=pltpu.PrefetchScalarGridSpec(
            num_scalar_prefetch=1,
            grid=(slots,),
            in_specs=[
                pl.BlockSpec((1, length, width), lambda i, place: (jnp.minimum(place[0] + i, total - 1), 0, 0)),
                pl.BlockSpec((1, length, width), local_block),
            ]
            + [whole(p.shape) for p in packs]
            + [whole((1, width))] * 2,
            out_specs=[
                pl.BlockSpec((spread, 1, part, width), lambda i, place: (0, i, 0, 0)),
                pl.BlockSpec((1, length, width), local_block),
                pl.BlockSpec((1, length, 3 * inner), local_block),
                pl.BlockSpec((1, length, inner), local_block),
            ],
        ),
        out_shape=[
            jax.ShapeDtypeStruct((spread, slots, part, width), BF16),
            jax.ShapeDtypeStruct((slots, length, width), F32),
            jax.ShapeDtypeStruct((slots, length, 3 * inner), BF16),
            jax.ShapeDtypeStruct((slots, length, inner), BF16),
        ],
        compiler_params=params("arbitrary"),
        cost_estimate=pl.CostEstimate(
            flops=slots * 2 * length * (4 * width * inner + 4 * length * inner),
            bytes_accessed=slots * length * (width * 12 + inner * 8) + 8 * width * inner,
            transcendentals=slots * length * length * inner // HEAD_WIDTH,
        ),
        name="attention_far",
    )(place, tokens, partial, *packs, gain_attn, gain_mix)


def pack_kernel(query, key, value, output, out):
    width = query.shape[1]
    for i, ref in enumerate((query, key, value)):
        out[:, i * width : (i + 1) * width] = ref[...]
    out[:, 3 * width :] = output[...].T


def pack_weights(query, key, value, output):
    width, columns = query.shape
    if columns % LANES:
        return jnp.concatenate([query, key, value, output.T], axis=1)
    return pl.pallas_call(
        pack_kernel,
        out_shape=jax.ShapeDtypeStruct((width, 4 * columns), BF16),
        compiler_params=params(),
        cost_estimate=pl.CostEstimate(flops=0, bytes_accessed=16 * width * columns, transcendentals=0),
        name="pack_weights",
    )(query, key, value, output)


def slot_softmax(logits, codes, part):
    experts = logits.shape[1]
    logits = logits.reshape(-1, part, experts)
    codes = jnp.broadcast_to(codes, (codes.shape[0], experts)).reshape(-1, part, experts)
    total = jnp.zeros_like(logits)
    for g in range(GROUPS):
        inside = (codes >= g * part) & (codes < (g + 1) * part)
        held = jnp.where(inside, logits, NEGATIVE)
        powers = jnp.where(inside, jnp.exp(held - jnp.max(held, axis=0, keepdims=True)), 0.0)
        total = total + powers / jnp.sum(powers, axis=0, keepdims=True)
    return total.reshape(-1, experts)


def group_totals(terms, codes, part):
    experts = terms.shape[1]
    terms = terms.reshape(-1, part, experts)
    codes = jnp.broadcast_to(codes, (codes.shape[0], experts)).reshape(-1, part, experts)
    total = jnp.zeros_like(terms)
    for g in range(GROUPS):
        inside = (codes >= g * part) & (codes < (g + 1) * part)
        total = jnp.where(inside, jnp.sum(jnp.where(inside, terms, 0.0), axis=0, keepdims=True), total)
    return total.reshape(-1, experts)


def mix_kernel(part, relative, rows, cots, controller, row_code, col_code, tile, probs_out, spread_out, *refs):
    sent, (merged, grads) = refs[:-2], refs[-2:]
    held = rows[...]
    probs = slot_softmax(mm(held, controller[...]), row_code[...], part)
    probs_out[...] = probs
    wide = mm(probs.astype(BF16), tile[...])
    spread = jnp.where(row_code[...] == col_code[...], wide, 0.0).astype(BF16)
    spread_out[...] = spread
    count, _, lines, _ = sent[0].shape
    merged[...] = mm_tn(spread, held).astype(BF16)
    grads[...] = mm_tn(spread, cots[...]).astype(BF16)
    for j, out in enumerate(sent):
        for e in range(count):
            at = pl.ds(pl.multiple_of((relative[j] * count + e) * lines, lines), lines)
            out[e, 0] = merged[at]
            out[e, 1] = grads[at]


def mix_forward(part, relative, rows, cots, controller, row_code, col_code, tile, narrow):
    count, width = rows.shape
    experts, columns = tile.shape
    sent = (experts // narrow, 2, columns // experts, width)
    return pl.pallas_call(
        functools.partial(mix_kernel, part),
        grid_spec=pltpu.PrefetchScalarGridSpec(
            num_scalar_prefetch=1,
            grid=(1,),
            in_specs=[whole(x.shape) for x in (rows, cots, controller, row_code, col_code, tile)],
            out_specs=[whole((count, experts)), whole((count, columns))]
            + [whole(sent)] * narrow,
            scratch_shapes=[pltpu.VMEM((columns, width), BF16)] * 2,
        ),
        out_shape=[
            jax.ShapeDtypeStruct((count, experts), F32),
            jax.ShapeDtypeStruct((count, columns), BF16),
        ]
        + [jax.ShapeDtypeStruct(sent, BF16)] * narrow,
        compiler_params=params("arbitrary"),
        cost_estimate=pl.CostEstimate(
            flops=4 * count * columns * width,
            bytes_accessed=6 * count * width * 2,
            transcendentals=count * experts * 2,
        ),
        name="mix_forward",
    )(relative, rows, cots, controller, row_code, col_code, tile)


def unmix_kernel(
    part, narrow, relative, spread, rows, cots, probs, controller, row_code, col_code, tile, *refs
):
    back, (grad_out, mixed_out, gain_out, outs, grads) = refs[:narrow], refs[narrow:]
    count, _, lines, _ = back[0].shape
    for j, piece in enumerate(back):
        for e in range(count):
            at = pl.ds(pl.multiple_of((relative[j] * count + e) * lines, lines), lines)
            outs[at] = piece[e, 0]
            grads[at] = piece[e, 1]
    held = rows[...]
    pairs = (mm_nt(cots[...], outs[...]) + mm_nt(held, grads[...])).astype(BF16)
    pairs = jnp.where(row_code[...] == col_code[...], pairs, jnp.zeros_like(pairs))
    d_weights = mm_nt(pairs, tile[...])
    p = probs[...]
    d_logits = (p * (d_weights - group_totals(p * d_weights, row_code[...], part))).astype(BF16)
    grad_out[...] = (mm(spread[...], grads[...]) + mm_nt(d_logits, controller[...])).astype(BF16)
    mixed_out[...] = mm(spread[...], outs[...]).astype(BF16)
    gain_out[...] = mm_tn(d_logits, held)


def mix_backward(part, relative, spread, rows, cots, probs, back, controller, row_code, col_code, tile):
    count, width = rows.shape
    experts, columns = tile.shape
    operands = (spread, rows, cots, probs, controller, row_code, col_code, tile) + tuple(back)
    outs = [
        jax.ShapeDtypeStruct((count, width), BF16),
        jax.ShapeDtypeStruct((count, width), BF16),
        jax.ShapeDtypeStruct((experts, width), F32),
    ]
    return pl.pallas_call(
        functools.partial(unmix_kernel, part, len(back)),
        grid_spec=pltpu.PrefetchScalarGridSpec(
            num_scalar_prefetch=1,
            grid=(1,),
            in_specs=[whole(x.shape) for x in operands],
            out_specs=[whole(x.shape) for x in outs],
            scratch_shapes=[pltpu.VMEM((columns, width), BF16)] * 2,
        ),
        out_shape=outs,
        compiler_params=params("arbitrary"),
        cost_estimate=pl.CostEstimate(
            flops=8 * count * columns * width,
            bytes_accessed=8 * count * width * 2,
            transcendentals=0,
        ),
        name="mix_backward",
    )(relative, *operands)


GELU_SLOPE = 0.7978845608028654
GELU_CUBE = 0.044715


def gelu_pair(x):
    square = x * x
    bend = jnp.tanh(GELU_SLOPE * x * (1.0 + GELU_CUBE * square))
    gate = 0.5 * (1.0 + bend)
    slope = gate + 0.5 * x * (1.0 - bend * bend) * (GELU_SLOPE * (1.0 + 3.0 * GELU_CUBE * square))
    return x * gate, slope


def expert_kernel(count, *refs):
    both, (w_in, b_in, w_out, b_out), sent = refs[:count], refs[count : count + 4], refs[count + 4 :]
    rows = both[0].shape[2]
    merged = jnp.concatenate([x[0, 0] for x in both], axis=0)
    grads = jnp.concatenate([x[0, 1] for x in both], axis=0)
    act, slope = gelu_pair(mm(merged, w_in[0]) + b_in[0])
    outs = mm(act.astype(BF16), w_out[0]) + b_out[0]
    d_pre = (mm_nt(grads, w_out[0]) * slope).astype(BF16)
    d_merged = mm_nt(d_pre, w_in[0])
    for j, out in enumerate(sent):
        at = slice(j * rows, (j + 1) * rows)
        out[0, 0] = outs[at].astype(BF16)
        out[0, 1] = d_merged[at].astype(BF16)


def experts_at_positions(both, w_in, b_in, w_out, b_out):
    experts, _, rows, width = both[0].shape
    inner = w_in.shape[2]
    sources, count = len(both), experts * rows
    tokens = pl.BlockSpec((1, 2, rows, width), lambda e: (e, 0, 0, 0))
    return pl.pallas_call(
        functools.partial(expert_kernel, sources),
        grid=(experts,),
        in_specs=[tokens] * sources
        + [
            pl.BlockSpec((1, width, inner), lambda e: (e, 0, 0)),
            pl.BlockSpec((1, 1, inner), lambda e: (e, 0, 0)),
            pl.BlockSpec((1, inner, width), lambda e: (e, 0, 0)),
            pl.BlockSpec((1, 1, width), lambda e: (e, 0, 0)),
        ],
        out_specs=[tokens] * sources,
        out_shape=[jax.ShapeDtypeStruct(x.shape, BF16) for x in both],
        compiler_params=params("arbitrary"),
        cost_estimate=pl.CostEstimate(
            flops=8 * sources * count * width * inner,
            bytes_accessed=4 * experts * width * inner + 4 * sources * count * width * 2,
            transcendentals=sources * count * inner,
        ),
        name="experts",
    )(*both, w_in, b_in[:, None], w_out, b_out[:, None])


def weight_kernel(units, where, first, both, w_in, b_in, w_out, *refs):
    refs, (merged, grads, turned, total) = refs[:-4], refs[-4:]
    outs = list(refs[: units - 1]) + [refs[units - 1 :]]
    p, i = pl.program_id(0), pl.program_id(1)
    half, unit = where[0], where[1]
    width = both.shape[-1]
    block = w_out.shape[1]
    span = turned.shape[0]
    rows = span // units
    fold = width // block
    height = refs[0].shape[1]

    def put(lines, at, values, d=None):
        for u in range(units) if d is None else [d]:
            if u < units - 1:
                outs[u][p, lines, at] = values
            else:
                for expert, out in enumerate(outs[u]):

                    @pl.when(p == expert)
                    def _(out=out):
                        out[0, lines, at] = values

    @pl.when(i == 0)
    def _():
        merged[...] = both[:, :, 0, 0].reshape(merged.shape)
        grads[...] = both[:, :, 0, 1].reshape(grads.shape)
        turned[...] = merged[:, pl.ds(pl.multiple_of(half * span, span), span)].T
        sums = jnp.sum(grads[...].astype(F32), axis=0, keepdims=True).astype(BF16)
        put(slice(height - 16, height), slice(0, width), jnp.zeros((16, width), BF16))
        put(slice(height - 1, height), slice(0, width), sums)

    act, slope = gelu_pair(mm(merged[...], w_in[0]) + b_in[0])
    d_pre = (mm_nt(grads[...], w_out[0]) * slope).astype(BF16)
    bias = jnp.sum(d_pre.astype(F32), axis=0, keepdims=True).astype(BF16)
    total[...] = mm(turned[...], d_pre)
    for part in range(fold):

        @pl.when(lax.rem(i, fold) == part)
        def _(part=part):
            at = slice(part * block, (part + 1) * block)
            base = pl.ds(pl.multiple_of(i // fold * rows, rows), rows)
            for d in range(units):
                own = pl.multiple_of(lax.bitwise_xor(unit, d) * rows, rows)
                put(base, at, total[pl.ds(own, rows)].astype(BF16), d)

    for step in range(pl.num_programs(1)):

        @pl.when(i == step)
        def _(step=step):
            line = height - 16 + step // fold
            put(slice(line, line + 1), slice(step % fold * block, (step % fold + 1) * block), bias)

    @pl.when((i >= half * units) & (i < (half + 1) * units))
    def _():
        grad = mm_tn(act.astype(BF16), grads[...]).astype(BF16)
        start = height - 16 - block
        for d in range(units):

            @pl.when(i - half * units == lax.bitwise_xor(unit, d))
            def _(d=d):
                put(slice(start, start + block), slice(0, width), grad, d)


def expert_weights(where, first, both, w_in, b_in, w_out, wide, units):
    sources, inner_sources, held, _, rows, width = both.shape
    inner = w_in.shape[2]
    block = inner // wide
    count = sources * inner_sources * rows
    span = width * units // wide
    height = inner // width * (width // wide) + block + 16
    shapes = [(held, height, width)] * (units - 1) + [(1, height, width)] * held
    return pl.pallas_call(
        functools.partial(weight_kernel, units),
        grid_spec=pltpu.PrefetchScalarGridSpec(
            num_scalar_prefetch=2,
            grid=(held, wide),
            in_specs=[
                pl.BlockSpec(
                    (sources, inner_sources, 1, 2, rows, width), lambda p, i, w, f: (0, 0, p, 0, 0, 0)
                ),
                pl.BlockSpec((1, width, block), lambda p, i, w, f: (f[0] + p, 0, i)),
                pl.BlockSpec((1, 1, block), lambda p, i, w, f: (f[0] + p, 0, i)),
                pl.BlockSpec((1, block, width), lambda p, i, w, f: (f[0] + p, i, 0)),
            ],
            out_specs=[whole(x) for x in shapes],
            scratch_shapes=[pltpu.VMEM((count, width), BF16)] * 2
            + [pltpu.VMEM((span, count), BF16), pltpu.VMEM((span, block), F32)],
        ),
        out_shape=[jax.ShapeDtypeStruct(x, BF16) for x in shapes],
        compiler_params=params("arbitrary", "arbitrary"),
        cost_estimate=pl.CostEstimate(
            flops=held * 6 * count * width * inner,
            bytes_accessed=held * (8 * width * inner + 4 * count * width),
            transcendentals=held * count * inner,
        ),
        name="expert_weights",
    )(where, first, both, w_in, b_in[:, None], w_out)


def owner_kernel(units, held, where, *refs):
    pieces, (g_in, g_out, bias) = refs[:-3], refs[-3:]
    rows, block = g_in.shape[1], g_out.shape[1]
    width = g_out.shape[2]
    start = pieces[0].shape[1] - 16 - block
    for d in range(units):
        for p in range(held):

            @pl.when((pl.program_id(0) == d) & (pl.program_id(1) == p))
            def _(d=d, p=p):
                ref, e = (pieces[d], p) if d < units - 1 else (pieces[d + p], 0)
                for c in range(g_in.shape[2] // width):
                    at = slice(c * width, (c + 1) * width)
                    g_in[0, :, at] = ref[e, c * rows : (c + 1) * rows].astype(F32)
                g_out[0] = ref[e, start : start + block].astype(F32)
                bias[0] = ref[e, start + block :].astype(F32)


def owned_weights(pieces, where, inner, wide, units):
    width = pieces[0].shape[2]
    held = len(pieces) - units + 1
    count = units * held
    shapes = [(1, width // wide, inner), (1, inner // wide, width), (1, 16, width)]
    return pl.pallas_call(
        functools.partial(owner_kernel, units, held),
        grid_spec=pltpu.PrefetchScalarGridSpec(
            num_scalar_prefetch=1,
            grid=(units, held),
            in_specs=[whole(x.shape) for x in pieces],
            out_specs=[pl.BlockSpec(x, lambda d, p, where: (where[d] * held + p, 0, 0)) for x in shapes],
        ),
        out_shape=[jax.ShapeDtypeStruct((count,) + x[1:], F32) for x in shapes],
        compiler_params=params("arbitrary", "arbitrary"),
        cost_estimate=pl.CostEstimate(
            flops=0, bytes_accessed=sum(x.size for x in pieces) * 6, transcendentals=0
        ),
        name="owned_weights",
    )(where, *pieces)


def attend_back(entry, d_low, packs, joint_in, context_in, causal, masks, total):
    width = entry.shape[1]
    scale = float(HEAD_WIDTH) ** -0.5
    d_entry = None
    for j, pack in enumerate(packs):
        base = j * 3 * LANES
        q, k, v = (joint_in[0, :, base + i * LANES : base + (i + 1) * LANES] for i in range(3))
        context = context_in[0, :, j * LANES : (j + 1) * LANES]
        d_context = mm(d_low, pack[:, 3 * LANES :]).astype(BF16)
        d_q, d_k, d_v = [], [], []
        for mask in masks:
            q_head = keep(mask, q)
            d_head = keep(mask, d_context)
            probs = causal_probs(q_head, k, causal)
            d_probs = mm_nt(d_head, v).astype(BF16).astype(F32)
            d_scores = probs * (d_probs - jnp.sum(probs * d_probs, axis=-1, keepdims=True))
            d_scores = d_scores.astype(BF16)
            d_v.append(mm_tn(probs.astype(BF16), d_head))
            d_q.append(mm(d_scores, keep(mask, k)))
            d_k.append(mm_tn(d_scores, q_head))
        joint = [sum(d_q) * scale, sum(d_k) * scale, sum(d_v)]
        joint = jnp.concatenate(joint, axis=1).astype(BF16)
        term = mm_nt(joint, pack[:, : 3 * LANES])
        d_entry = term if d_entry is None else d_entry + term
        grad = mm_tn(entry, joint)
        for c in range(3):
            total[j, c * width : (c + 1) * width] += grad[:, c * LANES : (c + 1) * LANES]
        grad = mm_tn(context, d_low)
        for c in range(width // LANES):
            at = slice(3 * width + c * LANES, 3 * width + (c + 1) * LANES)
            total[j, at] += grad[:, c * LANES : (c + 1) * LANES]
    return d_entry


def store_weights(total, controllers, outs, lanes, gains=None):
    height = total.shape[1]
    for o, out in enumerate(outs):
        j, at = divmod(o, LANES // lanes)
        piece = total[j].astype(BF16)
        if lanes < LANES:
            own = slice(at * lanes, (at + 1) * lanes)
            split = height // 4 * 3
            piece = [jnp.pad(piece[:split, own], ((0, 0), (0, LANES - lanes)))] + [
                jnp.pad(piece[c : c + LANES][own], ((0, LANES - lanes), (0, 0)))
                for c in range(split, height, LANES)
            ]
            piece = jnp.concatenate(piece, axis=0)
        out[:height] = piece
        tail = [controllers[o]]
        if gains is not None:
            tail.append(gains)
        left = out.shape[0] - height - sum(x.shape[0] for x in tail)
        out[height:] = jnp.concatenate(tail + [jnp.zeros((left, LANES), BF16)], axis=0)


def back_far_kernel(blocks, lanes, place, tokens, cots, grads, hidden, joint, context, *refs):
    packs, (gain_attn, gain_mix, controllers), refs = refs[:blocks], refs[blocks : blocks + 3], refs[blocks + 3 :]
    (partial_out, d_hidden_out, gain_out), outs, total = refs[:3], refs[3:-1], refs[-1]
    i = pl.program_id(0)
    length, width = hidden.shape[1:]
    live = (place[0] + i < place[1]).astype(F32)

    @pl.when(i == 0)
    def _():
        total[...] = jnp.zeros_like(total)
        gain_out[...] = jnp.zeros_like(gain_out)

    rows = hidden[0]
    inverse = inverse_rms(rows)
    normed = rows * inverse
    grad = grads[...].astype(F32).reshape(length, width)
    gain_out[0:1] += jnp.sum(grad * normed, axis=0, keepdims=True)
    d_normed = grad * gain_mix[...]
    d_hidden = cots[0].astype(F32) * live + inverse * (
        d_normed - normed * jnp.mean(d_normed * normed, axis=-1, keepdims=True)
    )
    d_hidden_out[0] = d_hidden
    rows = tokens[0].astype(F32)
    entry = (rows * inverse_rms(rows) * gain_attn[...]).astype(BF16)
    partial_out[0] = attend_back(
        entry, d_hidden.astype(BF16), packs, joint, context, causal_mask(length), head_masks(length), total
    )

    @pl.when(i == pl.num_programs(0) - 1)
    def _():
        store_weights(total, controllers, outs, lanes)


def back_near_kernel(blocks, lanes, place, tokens, d_hidden, partial, joint, context, *refs):
    packs, (gain_attn, gain_in, controllers), refs = refs[:blocks], refs[blocks : blocks + 3], refs[blocks + 3 :]
    d_tokens_out, outs, (total, gain) = refs[0], refs[1:-2], refs[-2:]
    i = pl.program_id(0)
    length, width = d_hidden.shape[1:]

    @pl.when(i == 0)
    def _():
        total[...] = jnp.zeros_like(total)
        gain[...] = jnp.zeros_like(gain)

    rows = tokens[0].astype(F32)
    inverse = inverse_rms(rows)
    normed = rows * inverse
    entry = (normed * gain_attn[...]).astype(BF16)
    d_entry = partial[0] + attend_back(
        entry, d_hidden[0].astype(BF16), packs, joint, context, causal_mask(length), head_masks(length), total
    )
    d_entry = d_entry.astype(BF16).astype(F32)
    gain[0:1] += jnp.sum(d_entry * normed, axis=0, keepdims=True)
    d_normed = d_entry * gain_attn[...]
    d_tokens = d_hidden[0] + inverse * (
        d_normed - normed * jnp.mean(d_normed * normed, axis=-1, keepdims=True)
    )
    live = (place[0] + i < place[1]).astype(F32)
    d_tokens_out[0] = (d_tokens * live).astype(BF16)

    @pl.when(i == pl.num_programs(0) - 1)
    def _():
        pieces = width // LANES
        tail = [x[0:1, c * LANES : (c + 1) * LANES] for x in (gain, gain_in) for c in range(pieces)]
        tail.append(jnp.zeros((16 - 2 * pieces, LANES), F32))
        store_weights(total, controllers, outs, lanes, jnp.concatenate(tail, axis=0).astype(BF16))


def attention_back_far(
    place, tokens, cotangent, grads, hidden, joint, context, packs, gain_attn, gain_mix, controllers, height
):
    total, length, width = tokens.shape
    spread, slots, part, _ = grads.shape
    inner = context.shape[2]
    blocks = len(packs)
    count = controllers.shape[0]

    def own(i, place):
        return (jnp.minimum(place[0] + i, total - 1), 0, 0)

    rows = pl.BlockSpec((1, length, width), local_block)
    return pl.pallas_call(
        functools.partial(back_far_kernel, blocks, inner // count),
        grid_spec=pltpu.PrefetchScalarGridSpec(
            num_scalar_prefetch=1,
            grid=(slots,),
            in_specs=[
                pl.BlockSpec((1, length, width), own),
                pl.BlockSpec((1, length, width), own),
                pl.BlockSpec((spread, 1, part, width), lambda i, place: (0, i, 0, 0)),
                rows,
                pl.BlockSpec((1, length, 3 * inner), local_block),
                pl.BlockSpec((1, length, inner), local_block),
            ]
            + [whole(p.shape) for p in packs]
            + [whole((1, width))] * 2
            + [whole(controllers.shape)],
            out_specs=[rows, rows, whole((8, width))] + [whole((height, LANES))] * count,
            scratch_shapes=[pltpu.VMEM((blocks, 4 * width, LANES), F32)],
        ),
        out_shape=[
            jax.ShapeDtypeStruct((slots, length, width), F32),
            jax.ShapeDtypeStruct((slots, length, width), F32),
            jax.ShapeDtypeStruct((8, width), F32),
        ]
        + [jax.ShapeDtypeStruct((height, LANES), BF16)] * count,
        compiler_params=params("arbitrary"),
        cost_estimate=pl.CostEstimate(
            flops=0,
            bytes_accessed=slots * length * (width * 18 + inner * 8) + 16 * width * inner,
            transcendentals=slots * length * length * inner // HEAD_WIDTH,
        ),
        name="attention_back_far",
    )(place, tokens, cotangent, grads, hidden, joint, context, *packs, gain_attn, gain_mix, controllers)


def attention_back_near(
    place, tokens, d_hidden, partial, joint, context, packs, gain_attn, gain_in, controllers, height
):
    total, length, width = tokens.shape
    slots, _, inner = context.shape
    blocks = len(packs)
    count = controllers.shape[0]

    def own(i, place):
        return (jnp.minimum(place[0] + i, total - 1), 0, 0)

    rows = pl.BlockSpec((1, length, width), local_block)
    return pl.pallas_call(
        functools.partial(back_near_kernel, blocks, inner // count),
        grid_spec=pltpu.PrefetchScalarGridSpec(
            num_scalar_prefetch=1,
            grid=(slots,),
            in_specs=[
                pl.BlockSpec((1, length, width), own),
                rows,
                rows,
                pl.BlockSpec((1, length, 3 * inner), local_block),
                pl.BlockSpec((1, length, inner), local_block),
            ]
            + [whole(p.shape) for p in packs]
            + [whole((1, width)), whole((8, width)), whole(controllers.shape)],
            out_specs=[rows] + [whole((height, LANES))] * count,
            scratch_shapes=[
                pltpu.VMEM((blocks, 4 * width, LANES), F32),
                pltpu.VMEM((8, width), F32),
            ],
        ),
        out_shape=[
            jax.ShapeDtypeStruct((slots, length, width), BF16),
        ]
        + [jax.ShapeDtypeStruct((height, LANES), BF16)] * count,
        compiler_params=params("arbitrary"),
        cost_estimate=pl.CostEstimate(
            flops=0,
            bytes_accessed=slots * length * (width * 12 + inner * 8) + 16 * width * inner,
            transcendentals=slots * length * length * inner // HEAD_WIDTH,
        ),
        name="attention_back_near",
    )(place, tokens, d_hidden, partial, joint, context, *packs, gain_attn, gain_in, controllers)


def output_kernel(place, hidden, mixed, out):
    live = (place[0] + pl.program_id(0) < place[1]).astype(F32)
    rows = mixed[...].astype(F32).reshape(hidden.shape[1:])
    out[0] = (live * (hidden[0] + rows)).astype(BF16)


def layer_output(place, hidden, mixed):
    spread, slots, part, width = mixed.shape
    length = hidden.shape[1]
    return pl.pallas_call(
        output_kernel,
        grid_spec=pltpu.PrefetchScalarGridSpec(
            num_scalar_prefetch=1,
            grid=(slots,),
            in_specs=[
                pl.BlockSpec((1, length, width), lambda i, place: (i, 0, 0)),
                pl.BlockSpec((spread, 1, part, width), lambda i, place: (0, i, 0, 0)),
            ],
            out_specs=pl.BlockSpec((1, length, width), lambda i, place: (i, 0, 0)),
        ),
        out_shape=jax.ShapeDtypeStruct((slots, length, width), BF16),
        compiler_params=params("arbitrary"),
        cost_estimate=pl.CostEstimate(
            flops=slots * length * width * 3, bytes_accessed=slots * length * width * 8, transcendentals=0
        ),
        name="layer_output",
    )(place, hidden, mixed)


def swap_core(x):
    narrow = lax.axis_size("narrow")
    return lax.ppermute(x, "narrow", [(n, n ^ 1) for n in range(narrow)])


def from_chip(x, k):
    narrow = lax.axis_size("narrow")
    return lax.ppermute(x, "narrow", [((n + 2 * k) % narrow, n) for n in range(narrow)])


def to_chip(x, k):
    narrow = lax.axis_size("narrow")
    return lax.ppermute(x, "narrow", [(n, (n + 2 * k) % narrow) for n in range(narrow)])


def relative_narrow():
    narrow = lax.axis_size("narrow")
    me = lax.axis_index("narrow")
    return [lax.bitwise_xor(lax.rem(me + 2 * (j // 2), narrow), j % 2) for j in range(narrow)]


def gather_narrow(x):
    blocks = []
    for k in range(lax.axis_size("narrow") // 2):
        piece = from_chip(x, k) if k else x
        blocks += [piece, swap_core(piece)]
    return blocks


def far_sums(pieces):
    pairs = [(pieces[2 * k], swap_core(pieces[2 * k + 1])) for k in range(len(pieces) // 2)]
    return [(x.astype(F32) + y.astype(F32)).astype(BF16) for x, y in pairs]


def sum_wide(x, *others):
    wide = lax.axis_size("wide")
    parts = x.astype(BF16).reshape(wide, x.shape[0] // wide, x.shape[1])
    parts = lax.all_to_all(parts, "wide", split_axis=0, concat_axis=0, tiled=True)
    part = jnp.sum(parts.astype(F32), axis=0).astype(BF16)
    part, others = lax.optimization_barrier((part, others))
    parts = jnp.broadcast_to(part[None], parts.shape)
    parts = lax.all_to_all(parts, "wide", split_axis=0, concat_axis=0, tiled=True)
    return parts.reshape(x.shape).astype(F32), others


def to_relative(x, j):
    narrow = lax.axis_size("narrow")
    k, other = j // 2, j % 2
    return lax.ppermute(x, "narrow", [(n, ((n + 2 * k) % narrow) ^ other) for n in range(narrow)])


def from_relative(x, j):
    narrow = lax.axis_size("narrow")
    k, other = j // 2, j % 2
    return lax.ppermute(x, "narrow", [(((n + 2 * k) % narrow) ^ other, n) for n in range(narrow)])


def to_unit(x, d):
    wide = lax.axis_size("wide")
    return lax.ppermute(x, "wide", [(w, w ^ d) for w in range(wide)])


def place_kernel(count, where, *refs):
    out = refs[count]
    for j in range(count):

        @pl.when(pl.program_id(0) == j)
        def _(j=j):
            out[...] = refs[j][...].astype(out.dtype)


def place_blocks(pieces, where, dtype):
    count = len(pieces)
    shape = pieces[0].shape
    zeros = (0,) * (len(shape) - 1)
    return pl.pallas_call(
        functools.partial(place_kernel, count),
        grid_spec=pltpu.PrefetchScalarGridSpec(
            num_scalar_prefetch=1,
            grid=(count,),
            in_specs=[whole(shape)] * count,
            out_specs=pl.BlockSpec(shape, lambda i, where: (where[i],) + zeros),
        ),
        out_shape=jax.ShapeDtypeStruct((count * shape[0],) + shape[1:], dtype),
        compiler_params=params("arbitrary"),
        cost_estimate=pl.CostEstimate(
            flops=0, bytes_accessed=pieces[0].size * 8 * count, transcendentals=0
        ),
        name="place_blocks",
    )(where, *pieces)


def body(
    tokens,
    cotangent,
    counts,
    group_order,
    query_weight,
    key_weight,
    value_weight,
    output_weight,
    gain_attn,
    gain_mix,
    controller,
    w_in,
    b_in,
    w_out,
    b_out,
):
    slot_count, seq_len, model_width = tokens.shape
    wide, narrow = lax.axis_size("wide"), lax.axis_size("narrow")
    spread = wide * narrow
    wide_index, narrow_index = lax.axis_index("wide"), lax.axis_index("narrow")
    slots = -(-slot_count // narrow)
    part = seq_len // spread
    padded_part = -(-part // 8) * 8
    local_experts = w_in.shape[0]
    experts = local_experts * narrow
    relative = jnp.stack(relative_narrow())
    head_columns = query_weight.shape[1]

    seq_ends = jnp.cumsum(counts)
    seq_starts = seq_ends - counts
    own_count = counts[wide_index]
    place = jnp.stack([narrow_index * slots, own_count]).astype(jnp.int32)
    slot_ids = jnp.arange(slots * narrow)
    slot_seqs = jnp.where(slot_ids[None] < counts[:, None], seq_starts[:, None] + slot_ids[None], -1)
    matches = slot_seqs.reshape(-1, 1) == group_order[None]
    slot_group = jnp.sum(jnp.where(matches, 1 + jnp.arange(group_order.shape[0]) // GROUP, 0), axis=1) - 1
    positions = jnp.arange(padded_part)
    row_code = jnp.where(slot_group[:, None] >= 0, slot_group[:, None] * padded_part + positions, -1)
    row_code = row_code.reshape(-1, 1).astype(jnp.int32)
    per_expert = GROUPS * padded_part
    col_code = (jnp.arange(experts * per_expert) % per_expert).astype(jnp.int32)[None]
    tile = jnp.repeat(jnp.eye(experts, dtype=BF16), per_expert, axis=1)

    pack = pack_weights(query_weight, key_weight, value_weight, output_weight)
    packs = [pack, swap_core(pack)]
    far_packs = [from_chip(pack, k) for k in range(1, narrow // 2)]
    joined = LANES // head_columns

    def join(packs):
        if joined == 1:
            return packs
        packs = [p.reshape(model_width, 4, head_columns) for p in packs]
        return [
            jnp.concatenate(packs[i : i + joined], axis=2).reshape(model_width, -1)
            for i in range(0, len(packs), joined)
        ]

    controllers = jnp.stack(gather_narrow(controller.T))
    controllers = controllers[jnp.argsort(relative)].reshape(experts, model_width).T

    gain_attn_row, gain_mix_row = gain_attn[None], gain_mix[None]

    def to_positions(x):
        x = lax.all_to_all(x, BOTH, split_axis=0, concat_axis=0, tiled=True)
        x = jnp.pad(x, ((0, 0), (0, 0), (0, padded_part - part), (0, 0)))
        return x.reshape(-1, model_width)

    def to_slots(x):
        x = x.reshape(spread, slots, padded_part, model_width)[:, :, :part]
        return lax.all_to_all(x, BOTH, split_axis=0, concat_axis=0, tiled=True)

    cots, *packs = lax.optimization_barrier((cotangent, *packs))
    cots = jnp.pad(cots, ((0, slots * narrow - slot_count), (0, 0), (0, 0)))
    cots = cots.reshape(slots * narrow, wide, narrow, part, model_width)
    cots = lax.dynamic_index_in_dim(cots, narrow_index, axis=2, keepdims=False).transpose(1, 0, 2, 3)
    cots = lax.all_to_all(cots, "wide", split_axis=0, concat_axis=0, tiled=True)
    cots = jnp.pad(cots, ((0, 0), (0, 0), (0, padded_part - part), (0, 0)))
    cot_rows = cots.reshape(-1, model_width)

    packs = join(packs)
    partial, joint_near, context_near = attention_near(place, tokens, packs, gain_attn_row, slots)
    partial, far_packs = lax.optimization_barrier((partial, far_packs))
    far_packs = join([x for piece in far_packs for x in (piece, swap_core(piece))])
    mix_sent, hidden, joint_far, context_far = attention_far(
        place, tokens, partial, far_packs, gain_attn_row, gain_mix_row, slots, spread
    )
    mix_rows = to_positions(mix_sent)
    probs, spread_probs, *both = mix_forward(
        padded_part, relative, mix_rows, cot_rows, controllers, row_code, col_code, tile, narrow
    )

    rows = GROUPS * part

    def trim(x):
        x = x.reshape(local_experts, 2, GROUPS, padded_part, model_width)[:, :, :, :part]
        return x.reshape(local_experts, 2, rows, model_width)

    def untrim(x):
        x = x.reshape(local_experts, 2, GROUPS, part, model_width)
        x = jnp.pad(x, ((0, 0), (0, 0), (0, 0), (0, padded_part - part), (0, 0)))
        return x.reshape(local_experts, 2, -1, model_width)

    both = [trim(x) for x in both]
    both = both[:1] + [to_relative(x, j) for j, x in enumerate(both) if j]
    halves = 2 if wide % 4 == 0 else 1
    units = wide // halves
    held, share = max(local_experts // units, 1), max(units // local_experts, 1)
    unit = lax.rem(wide_index, units)
    shape = (held, 2, rows, model_width)
    tokens_sent = jnp.stack(both).reshape((share, narrow // share, units // share) + shape)
    tokens_sent = tokens_sent.transpose(2, 0, 1, 3, 4, 5, 6).reshape((units, narrow // share) + shape)
    tokens_sent = jnp.concatenate([tokens_sent] * halves)
    tokens_sent, both = lax.optimization_barrier((tokens_sent, both))
    tokens_all = lax.all_to_all(tokens_sent, "wide", split_axis=0, concat_axis=0, tiled=True)
    if rows % 16 == 0:
        back = experts_at_positions(both, w_in, b_in, w_out, b_out)
    else:
        lines = jnp.stack(both, axis=2).reshape(local_experts, 2, narrow * rows, model_width)
        (back,) = experts_at_positions([lines], w_in, b_in, w_out, b_out)
        back = back.reshape(local_experts, 2, narrow, rows, model_width)
        back = [back[:, :, j] for j in range(narrow)]

    where = jnp.stack([wide_index // units, unit]).astype(jnp.int32)
    first = (unit * held // share).astype(jnp.int32)[None]
    expert_grads = expert_weights(where, first, tokens_all, w_in, b_in, w_out, wide, units)

    back = [untrim(x if j == 0 else from_relative(x, j)) for j, x in enumerate(back)]
    grad_rows, mixed_rows, grad_controller = mix_backward(
        padded_part, relative, spread_probs, mix_rows, cot_rows, probs, back, controllers, row_code, col_code, tile
    )
    grads = to_slots(grad_rows)
    mixed_rows, expert_grads, grads = lax.optimization_barrier((mixed_rows, expert_grads, grads))
    mixed = to_slots(mixed_rows)

    expert_grads = list(expert_grads[:1]) + [
        to_unit(x, min(d, units - 1)) for d, x in enumerate(expert_grads) if d
    ]

    height = 4 * model_width
    grad_controller = grad_controller.astype(BF16).reshape(narrow, -1, LANES)[relative]
    end = height + grad_controller.shape[1]
    rows_sent = -(-(end + 16) // (16 * wide)) * 16 * wide
    partial, d_hidden, gain_mix_part, *far = attention_back_far(
        place,
        tokens,
        cotangent,
        grads,
        hidden,
        joint_far,
        context_far,
        far_packs,
        gain_attn_row,
        gain_mix_row,
        grad_controller[2:],
        rows_sent,
    )
    partial, far = lax.optimization_barrier((partial, far_sums(far)))
    far = sum([to_chip(x, k + 1).astype(F32) for k, x in enumerate(far)], 0.0)
    d_tokens, kept, sent = attention_back_near(
        place,
        tokens,
        d_hidden,
        partial,
        joint_near,
        context_near,
        packs,
        gain_attn_row,
        gain_mix_part,
        grad_controller[:2],
        rows_sent,
    )
    d_tokens, kept, sent, mixed, expert_grads[:3] = lax.optimization_barrier(
        (d_tokens, kept, sent, mixed, expert_grads[:3])
    )
    weights = kept.astype(F32) + swap_core(sent).astype(F32) + far
    weights, expert_grads = sum_wide(weights, *expert_grads)
    gains = weights[end : end + 16].astype(BF16)
    gains = sum([to_chip(gains, k).astype(F32) for k in range(1, narrow // 2)], gains.astype(F32))
    projections = weights[: 3 * model_width, :head_columns].reshape(3, model_width, head_columns)
    output_weight_gradient = weights[3 * model_width : height].reshape(-1, LANES, LANES)[:, :head_columns]
    output_weight_gradient = output_weight_gradient.transpose(1, 0, 2).reshape(head_columns, -1)
    g_controller = weights[height:end].reshape(local_experts, model_width).T
    pieces = model_width // LANES
    g_gain_attn = gains[:pieces].reshape(-1)
    g_gain_mix = gains[pieces : 2 * pieces].reshape(-1)

    d_tokens = place_blocks(gather_narrow(d_tokens), relative, BF16)[:slot_count]
    mixed_part = layer_output(place, hidden, mixed)
    mixed_part = place_blocks(gather_narrow(mixed_part), relative, BF16)[:slot_count]

    order = lax.bitwise_xor(unit, jnp.arange(units))
    g_w_in, g_w_out, bias = owned_weights(expert_grads, order, w_in.shape[2], wide, units)

    def over_share(x):
        return jnp.sum(x.reshape((local_experts, share) + x.shape[1:]), axis=1)

    g_w_in, g_w_out, bias = (over_share(x) for x in (g_w_in, g_w_out, bias))
    g_b_in = bias[:, : w_in.shape[2] // model_width].reshape(local_experts, -1)
    g_b_out = bias[:, -1]

    return (
        mixed_part,
        d_tokens,
        projections[0],
        projections[1],
        projections[2],
        output_weight_gradient,
        g_gain_attn,
        g_gain_mix,
        g_controller,
        g_w_in,
        g_b_in,
        g_w_out,
        g_b_out,
    )


def solution(mesh):
    placed = (
        P("wide", None, None),
        P("wide", None, None),
        P(),
        P(),
        P(None, "narrow"),
        P(None, "narrow"),
        P(None, "narrow"),
        P("narrow", None),
        P(),
        P(),
        P(None, "narrow"),
        P("narrow", None, None),
        P("narrow", None),
        P("narrow", None, None),
        P("narrow", None),
    )
    return jax.shard_map(
        body,
        mesh=mesh,
        in_specs=placed,
        out_specs=(
            P("wide", None, None),
            P("wide", None, None),
            P(None, "narrow"),
            P(None, "narrow"),
            P(None, "narrow"),
            P("narrow", None),
            P(),
            P(),
            P(None, "narrow"),
            P("narrow", "wide", None),
            P("narrow", None),
            P("narrow", "wide", None),
            P("narrow", None),
        ),
        check_vma=False,
    )
```

```python
import functools

import jax
import jax.numpy as jnp
from jax import lax
from jax.experimental import pallas as pl
from jax.experimental.pallas import tpu as pltpu
from jax.sharding import PartitionSpec as P

HEAD_WIDTH = 64
GROUP = 32
GROUPS = 2
LANES = 128

EPSILON = 1e-05
NEGATIVE = -1e30
BOTH = ("wide", "narrow")
F32 = jnp.float32
BF16 = jnp.bfloat16
VMEM_LIMIT = 56 * 1024 * 1024


def mm(a, b):
    return lax.dot_general(a, b, (((1,), (0,)), ((), ())), preferred_element_type=F32)


def mm_nt(a, b):
    return lax.dot_general(a, b, (((1,), (1,)), ((), ())), preferred_element_type=F32)


def mm_tn(a, b):
    return lax.dot_general(a, b, (((0,), (0,)), ((), ())), preferred_element_type=F32)


def params(*semantics):
    return pltpu.CompilerParams(dimension_semantics=semantics or None, vmem_limit_bytes=VMEM_LIMIT)


def whole(shape):
    zeros = (0,) * len(shape)
    return pl.BlockSpec(tuple(shape), lambda *_: zeros)


def head_masks(rows):
    lane = lax.broadcasted_iota(jnp.int32, (rows, LANES), 1)
    return [(lane >= h * HEAD_WIDTH) & (lane < (h + 1) * HEAD_WIDTH) for h in range(LANES // HEAD_WIDTH)]


def keep(mask, rows):
    return jnp.where(mask, rows, jnp.zeros_like(rows))


def causal_probs(query_head, keys, causal):
    scores = mm_nt(query_head, keys) * (float(HEAD_WIDTH) ** -0.5)
    scores = jnp.where(causal, scores, NEGATIVE)
    powers = jnp.exp(scores - jnp.max(scores, axis=-1, keepdims=True))
    return powers * (1.0 / jnp.sum(powers, axis=-1, keepdims=True))


def causal_mask(length):
    return lax.broadcasted_iota(jnp.int32, (length, length), 0) >= lax.broadcasted_iota(
        jnp.int32, (length, length), 1
    )


def inverse_rms(rows):
    return lax.rsqrt(jnp.mean(rows * rows, axis=-1, keepdims=True) + EPSILON)


def attend(entry, packs, causal, masks, joint_out, context_out):
    attention = None
    for j, pack in enumerate(packs):
        joint = mm(entry, pack[:, : 3 * LANES]).astype(BF16)
        joint_out[0, :, j * 3 * LANES : (j + 1) * 3 * LANES] = joint
        q, k, v = (joint[:, i * LANES : (i + 1) * LANES] for i in range(3))
        context = None
        for mask in masks:
            probs = causal_probs(keep(mask, q), k, causal)
            term = mm(probs.astype(BF16), keep(mask, v))
            context = term if context is None else context + term
        context = context.astype(BF16)
        context_out[0, :, j * LANES : (j + 1) * LANES] = context
        term = mm_nt(context, pack[:, 3 * LANES :])
        attention = term if attention is None else attention + term
    return attention


def near_kernel(blocks, place, tokens, *refs):
    packs, (gain_attn, partial_out, joint_out, context_out) = refs[:blocks], refs[blocks:]
    rows = tokens[0].astype(F32)
    entry = (rows * inverse_rms(rows) * gain_attn[...]).astype(BF16)
    length = rows.shape[0]
    partial_out[0] = rows + attend(
        entry, packs, causal_mask(length), head_masks(length), joint_out, context_out
    )


def far_kernel(blocks, place, tokens, partial, *refs):
    packs = refs[:blocks]
    gain_attn, gain_mix, mix_out, hidden_out, joint_out, context_out = refs[blocks:]
    rows = tokens[0].astype(F32)
    entry = (rows * inverse_rms(rows) * gain_attn[...]).astype(BF16)
    length = rows.shape[0]
    hidden = partial[0] + attend(
        entry, packs, causal_mask(length), head_masks(length), joint_out, context_out
    )
    mixed = hidden * inverse_rms(hidden) * gain_mix[...]
    mix_out[...] = mixed.reshape(mix_out.shape).astype(BF16)
    hidden_out[0] = hidden


def local_block(i, place):
    return (i, 0, 0)


def attention_near(place, tokens, packs, gain_attn, slots):
    total, length, width = tokens.shape
    inner = len(packs) * LANES
    return pl.pallas_call(
        functools.partial(near_kernel, len(packs)),
        grid_spec=pltpu.PrefetchScalarGridSpec(
            num_scalar_prefetch=1,
            grid=(slots,),
            in_specs=[
                pl.BlockSpec((1, length, width), lambda i, place: (jnp.minimum(place[0] + i, total - 1), 0, 0))
            ]
            + [whole(p.shape) for p in packs]
            + [whole((1, width))],
            out_specs=[
                pl.BlockSpec((1, length, width), local_block),
                pl.BlockSpec((1, length, 3 * inner), local_block),
                pl.BlockSpec((1, length, inner), local_block),
            ],
        ),
        out_shape=[
            jax.ShapeDtypeStruct((slots, length, width), F32),
            jax.ShapeDtypeStruct((slots, length, 3 * inner), BF16),
            jax.ShapeDtypeStruct((slots, length, inner), BF16),
        ],
        compiler_params=params("arbitrary"),
        cost_estimate=pl.CostEstimate(
            flops=slots * 2 * length * (4 * width * inner + 4 * length * inner),
            bytes_accessed=slots * length * (width * 6 + inner * 8) + 8 * width * inner,
            transcendentals=slots * length * length * inner // HEAD_WIDTH,
        ),
        name="attention_near",
    )(place, tokens, *packs, gain_attn)


def attention_far(place, tokens, partial, packs, gain_attn, gain_mix, slots, spread):
    total, length, width = tokens.shape
    inner = len(packs) * LANES
    part = length // spread
    return pl.pallas_call(
        functools.partial(far_kernel, len(packs)),
        grid_spec=pltpu.PrefetchScalarGridSpec(
            num_scalar_prefetch=1,
            grid=(slots,),
            in_specs=[
                pl.BlockSpec((1, length, width), lambda i, place: (jnp.minimum(place[0] + i, total - 1), 0, 0)),
                pl.BlockSpec((1, length, width), local_block),
            ]
            + [whole(p.shape) for p in packs]
            + [whole((1, width))] * 2,
            out_specs=[
                pl.BlockSpec((spread, 1, part, width), lambda i, place: (0, i, 0, 0)),
                pl.BlockSpec((1, length, width), local_block),
                pl.BlockSpec((1, length, 3 * inner), local_block),
                pl.BlockSpec((1, length, inner), local_block),
            ],
        ),
        out_shape=[
            jax.ShapeDtypeStruct((spread, slots, part, width), BF16),
            jax.ShapeDtypeStruct((slots, length, width), F32),
            jax.ShapeDtypeStruct((slots, length, 3 * inner), BF16),
            jax.ShapeDtypeStruct((slots, length, inner), BF16),
        ],
        compiler_params=params("arbitrary"),
        cost_estimate=pl.CostEstimate(
            flops=slots * 2 * length * (4 * width * inner + 4 * length * inner),
            bytes_accessed=slots * length * (width * 12 + inner * 8) + 8 * width * inner,
            transcendentals=slots * length * length * inner // HEAD_WIDTH,
        ),
        name="attention_far",
    )(place, tokens, partial, *packs, gain_attn, gain_mix)


def pack_kernel(query, key, value, output, out):
    width = query.shape[1]
    for i, ref in enumerate((query, key, value)):
        out[:, i * width : (i + 1) * width] = ref[...]
    out[:, 3 * width :] = output[...].T


def pack_weights(query, key, value, output):
    width, columns = query.shape
    if columns % LANES:
        return jnp.concatenate([query, key, value, output.T], axis=1)
    return pl.pallas_call(
        pack_kernel,
        out_shape=jax.ShapeDtypeStruct((width, 4 * columns), BF16),
        compiler_params=params(),
        cost_estimate=pl.CostEstimate(flops=0, bytes_accessed=16 * width * columns, transcendentals=0),
        name="pack_weights",
    )(query, key, value, output)


def slot_softmax(logits, codes, part):
    experts = logits.shape[1]
    logits = logits.reshape(-1, part, experts)
    codes = jnp.broadcast_to(codes, (codes.shape[0], experts)).reshape(-1, part, experts)
    total = jnp.zeros_like(logits)
    for g in range(GROUPS):
        inside = (codes >= g * part) & (codes < (g + 1) * part)
        held = jnp.where(inside, logits, NEGATIVE)
        powers = jnp.where(inside, jnp.exp(held - jnp.max(held, axis=0, keepdims=True)), 0.0)
        total = total + powers / jnp.sum(powers, axis=0, keepdims=True)
    return total.reshape(-1, experts)


def group_totals(terms, codes, part):
    experts = terms.shape[1]
    terms = terms.reshape(-1, part, experts)
    codes = jnp.broadcast_to(codes, (codes.shape[0], experts)).reshape(-1, part, experts)
    total = jnp.zeros_like(terms)
    for g in range(GROUPS):
        inside = (codes >= g * part) & (codes < (g + 1) * part)
        total = jnp.where(inside, jnp.sum(jnp.where(inside, terms, 0.0), axis=0, keepdims=True), total)
    return total.reshape(-1, experts)


def mix_kernel(part, relative, rows, cots, controller, row_code, col_code, tile, probs_out, spread_out, *refs):
    sent, (merged, grads) = refs[:-2], refs[-2:]
    held = rows[...]
    probs = slot_softmax(mm(held, controller[...]), row_code[...], part)
    probs_out[...] = probs
    wide = mm(probs.astype(BF16), tile[...])
    spread = jnp.where(row_code[...] == col_code[...], wide, 0.0).astype(BF16)
    spread_out[...] = spread
    count, _, lines, _ = sent[0].shape
    merged[...] = mm_tn(spread, held).astype(BF16)
    grads[...] = mm_tn(spread, cots[...]).astype(BF16)
    for j, out in enumerate(sent):
        for e in range(count):
            at = pl.ds(pl.multiple_of((relative[j] * count + e) * lines, lines), lines)
            out[e, 0] = merged[at]
            out[e, 1] = grads[at]


def mix_forward(part, relative, rows, cots, controller, row_code, col_code, tile, narrow):
    count, width = rows.shape
    experts, columns = tile.shape
    sent = (experts // narrow, 2, columns // experts, width)
    return pl.pallas_call(
        functools.partial(mix_kernel, part),
        grid_spec=pltpu.PrefetchScalarGridSpec(
            num_scalar_prefetch=1,
            grid=(1,),
            in_specs=[whole(x.shape) for x in (rows, cots, controller, row_code, col_code, tile)],
            out_specs=[whole((count, experts)), whole((count, columns))]
            + [whole(sent)] * narrow,
            scratch_shapes=[pltpu.VMEM((columns, width), BF16)] * 2,
        ),
        out_shape=[
            jax.ShapeDtypeStruct((count, experts), F32),
            jax.ShapeDtypeStruct((count, columns), BF16),
        ]
        + [jax.ShapeDtypeStruct(sent, BF16)] * narrow,
        compiler_params=params("arbitrary"),
        cost_estimate=pl.CostEstimate(
            flops=4 * count * columns * width,
            bytes_accessed=6 * count * width * 2,
            transcendentals=count * experts * 2,
        ),
        name="mix_forward",
    )(relative, rows, cots, controller, row_code, col_code, tile)


def unmix_kernel(
    part, narrow, relative, spread, rows, cots, probs, controller, row_code, col_code, tile, *refs
):
    back, (sent, gain_out, outs, grads) = refs[:narrow], refs[narrow:]
    count, _, lines, _ = back[0].shape
    for j, piece in enumerate(back):
        for e in range(count):
            at = pl.ds(pl.multiple_of((relative[j] * count + e) * lines, lines), lines)
            outs[at] = piece[e, 0]
            grads[at] = piece[e, 1]
    held = rows[...]
    pairs = (mm_nt(cots[...], outs[...]) + mm_nt(held, grads[...])).astype(BF16)
    pairs = jnp.where(row_code[...] == col_code[...], pairs, jnp.zeros_like(pairs))
    d_weights = mm_nt(pairs, tile[...])
    p = probs[...]
    d_logits = (p * (d_weights - group_totals(p * d_weights, row_code[...], part))).astype(BF16)
    shape = (sent.shape[0],) + sent.shape[2:]
    grad = mm(spread[...], grads[...]) + mm_nt(d_logits, controller[...])
    sent[:, 0] = grad.reshape(shape).astype(BF16)
    sent[:, 1] = mm(spread[...], outs[...]).reshape(shape).astype(BF16)
    gain_out[...] = mm_tn(d_logits, held)


def mix_backward(part, relative, spread, rows, cots, probs, back, controller, row_code, col_code, tile, devices):
    count, width = rows.shape
    experts, columns = tile.shape
    operands = (spread, rows, cots, probs, controller, row_code, col_code, tile) + tuple(back)
    outs = [
        jax.ShapeDtypeStruct((devices, 2, count // devices, width), BF16),
        jax.ShapeDtypeStruct((experts, width), F32),
    ]
    return pl.pallas_call(
        functools.partial(unmix_kernel, part, len(back)),
        grid_spec=pltpu.PrefetchScalarGridSpec(
            num_scalar_prefetch=1,
            grid=(1,),
            in_specs=[whole(x.shape) for x in operands],
            out_specs=[whole(x.shape) for x in outs],
            scratch_shapes=[pltpu.VMEM((columns, width), BF16)] * 2,
        ),
        out_shape=outs,
        compiler_params=params("arbitrary"),
        cost_estimate=pl.CostEstimate(
            flops=8 * count * columns * width,
            bytes_accessed=8 * count * width * 2,
            transcendentals=0,
        ),
        name="mix_backward",
    )(relative, *operands)


GELU_SLOPE = 0.7978845608028654
GELU_CUBE = 0.044715


def gelu_pair(x):
    square = x * x
    bend = jnp.tanh(GELU_SLOPE * x * (1.0 + GELU_CUBE * square))
    gate = 0.5 * (1.0 + bend)
    slope = gate + 0.5 * x * (1.0 - bend * bend) * (GELU_SLOPE * (1.0 + 3.0 * GELU_CUBE * square))
    return x * gate, slope


def expert_kernel(count, *refs):
    both, (w_in, b_in, w_out, b_out), sent = refs[:count], refs[count : count + 4], refs[count + 4 :]
    rows = both[0].shape[2]
    merged = jnp.concatenate([x[0, 0] for x in both], axis=0)
    grads = jnp.concatenate([x[0, 1] for x in both], axis=0)
    act, slope = gelu_pair(mm(merged, w_in[0]) + b_in[0])
    outs = mm(act.astype(BF16), w_out[0]) + b_out[0]
    d_pre = (mm_nt(grads, w_out[0]) * slope).astype(BF16)
    d_merged = mm_nt(d_pre, w_in[0])
    for j, out in enumerate(sent):
        at = slice(j * rows, (j + 1) * rows)
        out[0, 0] = outs[at].astype(BF16)
        out[0, 1] = d_merged[at].astype(BF16)


def experts_at_positions(both, w_in, b_in, w_out, b_out):
    experts, _, rows, width = both[0].shape
    inner = w_in.shape[2]
    sources, count = len(both), experts * rows
    tokens = pl.BlockSpec((1, 2, rows, width), lambda e: (e, 0, 0, 0))
    return pl.pallas_call(
        functools.partial(expert_kernel, sources),
        grid=(experts,),
        in_specs=[tokens] * sources
        + [
            pl.BlockSpec((1, width, inner), lambda e: (e, 0, 0)),
            pl.BlockSpec((1, 1, inner), lambda e: (e, 0, 0)),
            pl.BlockSpec((1, inner, width), lambda e: (e, 0, 0)),
            pl.BlockSpec((1, 1, width), lambda e: (e, 0, 0)),
        ],
        out_specs=[tokens] * sources,
        out_shape=[jax.ShapeDtypeStruct(x.shape, BF16) for x in both],
        compiler_params=params("arbitrary"),
        cost_estimate=pl.CostEstimate(
            flops=8 * sources * count * width * inner,
            bytes_accessed=4 * experts * width * inner + 4 * sources * count * width * 2,
            transcendentals=sources * count * inner,
        ),
        name="experts",
    )(*both, w_in, b_in[:, None], w_out, b_out[:, None])


def weight_kernel(units, where, both, w_in, b_in, w_out, *refs):
    outs, (merged, grads, turned, total) = refs[:units], refs[units:]
    i, half, unit = pl.program_id(0), where[0], where[1]
    steps = pl.num_programs(0)
    width = both.shape[-1]
    span = turned.shape[0]
    rows = span // units
    height = outs[0].shape[0]
    block = height - 16 - steps * rows
    slices = width // block

    @pl.when(i == 0)
    def _():
        merged[...] = both[:, :, 0, 0].reshape(merged.shape)
        grads[...] = both[:, :, 0, 1].reshape(grads.shape)
        turned[...] = merged[:, pl.ds(pl.multiple_of(half * span, span), span)].T
        sums = jnp.sum(grads[...].astype(F32), axis=0, keepdims=True).astype(BF16)
        for out in outs:
            out[height - 16 :] = jnp.zeros((16, width), BF16)
            out[height - 1 :] = sums

    act, slope = gelu_pair(mm(merged[...], w_in[0]) + b_in[0])
    d_pre = (mm_nt(grads[...], w_out[0]) * slope).astype(BF16)
    bias = jnp.sum(d_pre.astype(F32), axis=0, keepdims=True).astype(BF16)
    total[...] = mm(turned[...], d_pre)
    base = pl.ds(pl.multiple_of(i * rows, rows), rows)
    for d, out in enumerate(outs):
        own = pl.ds(pl.multiple_of(lax.bitwise_xor(unit, d) * rows, rows), rows)
        out[base] = total[own].astype(BF16)
    for step in range(steps):

        @pl.when(i == step)
        def _(step=step):
            for out in outs:
                out[height - 16 + step : height - 15 + step] = bias

    @pl.when(i // (steps // 2) == half)
    def _():
        grad = mm_tn(act.astype(BF16), grads[...]).astype(BF16)
        first = (i - half * (steps // 2)) * slices
        for s in range(slices):
            for d, out in enumerate(outs):

                @pl.when(first + s == lax.bitwise_xor(unit, d))
                def _(s=s, out=out):
                    out[height - 16 - block : height - 16] = grad[s * block : (s + 1) * block]


def expert_weights(where, expert, p, both, w_in, b_in, w_out, wide, units):
    sources, inner_sources, _, _, rows, width = both.shape
    inner = w_in.shape[2]
    count = sources * inner_sources * rows
    span = width * units // wide
    height = inner // width * (width // wide) + inner // wide + 16
    return pl.pallas_call(
        lambda where, expert, *refs: weight_kernel(units, where, *refs),
        grid_spec=pltpu.PrefetchScalarGridSpec(
            num_scalar_prefetch=2,
            grid=(inner // width,),
            in_specs=[
                pl.BlockSpec(
                    (sources, inner_sources, 1, 2, rows, width), lambda i, w, e: (0, 0, p, 0, 0, 0)
                ),
                pl.BlockSpec((1, width, width), lambda i, w, e: (e[0], 0, i)),
                pl.BlockSpec((1, 1, width), lambda i, w, e: (e[0], 0, i)),
                pl.BlockSpec((1, width, width), lambda i, w, e: (e[0], i, 0)),
            ],
            out_specs=[whole((height, width))] * units,
            scratch_shapes=[pltpu.VMEM((count, width), BF16)] * 2
            + [pltpu.VMEM((span, count), BF16), pltpu.VMEM((span, width), F32)],
        ),
        out_shape=[jax.ShapeDtypeStruct((height, width), BF16)] * units,
        compiler_params=params("arbitrary"),
        cost_estimate=pl.CostEstimate(
            flops=6 * count * width * inner,
            bytes_accessed=8 * width * inner + 4 * count * width,
            transcendentals=count * inner,
        ),
        name="expert_weights",
    )(where, expert, both, w_in, b_in[:, None], w_out)


def owner_kernel(where, *refs):
    pieces, (g_in, g_out, bias) = refs[:-3], refs[-3:]
    rows, block = g_in.shape[1], g_out.shape[1]
    width = g_out.shape[2]
    start = pieces[0].shape[0] - 16 - block
    for j, piece in enumerate(pieces):

        @pl.when(pl.program_id(0) == j)
        def _(piece=piece):
            for c in range(g_in.shape[2] // width):
                g_in[0, :, c * width : (c + 1) * width] = piece[c * rows : (c + 1) * rows].astype(F32)
            g_out[0] = piece[start : start + block].astype(F32)
            bias[0] = piece[start + block :].astype(F32)


def owned_weights(pieces, where, inner, wide):
    count = len(pieces)
    width = pieces[0].shape[1]
    shapes = [(1, width // wide, inner), (1, inner // wide, width), (1, 16, width)]
    return pl.pallas_call(
        owner_kernel,
        grid_spec=pltpu.PrefetchScalarGridSpec(
            num_scalar_prefetch=1,
            grid=(count,),
            in_specs=[whole(x.shape) for x in pieces],
            out_specs=[pl.BlockSpec(x, lambda j, where: (where[j], 0, 0)) for x in shapes],
        ),
        out_shape=[jax.ShapeDtypeStruct((count,) + x[1:], F32) for x in shapes],
        compiler_params=params("arbitrary"),
        cost_estimate=pl.CostEstimate(
            flops=0, bytes_accessed=sum(x.size for x in pieces) * 6, transcendentals=0
        ),
        name="owned_weights",
    )(where, *pieces)


def attend_back(entry, d_low, packs, joint_in, context_in, causal, masks, total):
    width = entry.shape[1]
    scale = float(HEAD_WIDTH) ** -0.5
    d_entry = None
    for j, pack in enumerate(packs):
        base = j * 3 * LANES
        q, k, v = (joint_in[0, :, base + i * LANES : base + (i + 1) * LANES] for i in range(3))
        context = context_in[0, :, j * LANES : (j + 1) * LANES]
        d_context = mm(d_low, pack[:, 3 * LANES :]).astype(BF16)
        d_q, d_k, d_v = [], [], []
        for mask in masks:
            q_head = keep(mask, q)
            d_head = keep(mask, d_context)
            probs = causal_probs(q_head, k, causal)
            d_probs = mm_nt(d_head, v).astype(BF16).astype(F32)
            d_scores = probs * (d_probs - jnp.sum(probs * d_probs, axis=-1, keepdims=True))
            d_scores = d_scores.astype(BF16)
            d_v.append(mm_tn(probs.astype(BF16), d_head))
            d_q.append(mm(d_scores, keep(mask, k)))
            d_k.append(mm_tn(d_scores, q_head))
        joint = [sum(d_q) * scale, sum(d_k) * scale, sum(d_v)]
        joint = jnp.concatenate(joint, axis=1).astype(BF16)
        term = mm_nt(joint, pack[:, : 3 * LANES])
        d_entry = term if d_entry is None else d_entry + term
        grad = mm_tn(entry, joint)
        for c in range(3):
            total[j, c * width : (c + 1) * width] += grad[:, c * LANES : (c + 1) * LANES]
        grad = mm_tn(context, d_low)
        for c in range(width // LANES):
            at = slice(3 * width + c * LANES, 3 * width + (c + 1) * LANES)
            total[j, at] += grad[:, c * LANES : (c + 1) * LANES]
    return d_entry


def store_weights(total, controllers, outs, lanes, gains=None):
    height = total.shape[1]
    for o, out in enumerate(outs):
        j, at = divmod(o, LANES // lanes)
        piece = total[j].astype(BF16)
        if lanes < LANES:
            own = slice(at * lanes, (at + 1) * lanes)
            split = height // 4 * 3
            piece = [jnp.pad(piece[:split, own], ((0, 0), (0, LANES - lanes)))] + [
                jnp.pad(piece[c : c + LANES][own], ((0, LANES - lanes), (0, 0)))
                for c in range(split, height, LANES)
            ]
            piece = jnp.concatenate(piece, axis=0)
        out[:height] = piece
        tail = [controllers[o]]
        if gains is not None:
            tail.append(gains)
        left = out.shape[0] - height - sum(x.shape[0] for x in tail)
        out[height:] = jnp.concatenate(tail + [jnp.zeros((left, LANES), BF16)], axis=0)


def back_far_kernel(blocks, lanes, place, tokens, cots, grads, mixed, hidden, joint, context, *refs):
    packs, (gain_attn, gain_mix, controllers), refs = refs[:blocks], refs[blocks : blocks + 3], refs[blocks + 3 :]
    (partial_out, d_hidden_out, mixed_out, gain_out), outs, total = refs[:4], refs[4:-1], refs[-1]
    i = pl.program_id(0)
    length, width = hidden.shape[1:]
    live = (place[0] + i < place[1]).astype(F32)

    @pl.when(i == 0)
    def _():
        total[...] = jnp.zeros_like(total)
        gain_out[...] = jnp.zeros_like(gain_out)

    rows = hidden[0]
    inverse = inverse_rms(rows)
    normed = rows * inverse
    grad = grads[...].astype(F32).reshape(length, width)
    gain_out[0:1] += jnp.sum(grad * normed, axis=0, keepdims=True)
    d_normed = grad * gain_mix[...]
    d_hidden = cots[0].astype(F32) * live + inverse * (
        d_normed - normed * jnp.mean(d_normed * normed, axis=-1, keepdims=True)
    )
    d_hidden_out[0] = d_hidden
    mixed_out[0] = (live * (hidden[0] + mixed[...].astype(F32).reshape(length, width))).astype(BF16)
    rows = tokens[0].astype(F32)
    entry = (rows * inverse_rms(rows) * gain_attn[...]).astype(BF16)
    partial_out[0] = attend_back(
        entry, d_hidden.astype(BF16), packs, joint, context, causal_mask(length), head_masks(length), total
    )

    @pl.when(i == pl.num_programs(0) - 1)
    def _():
        store_weights(total, controllers, outs, lanes)


def back_near_kernel(blocks, lanes, place, tokens, d_hidden, partial, joint, context, *refs):
    packs, (gain_attn, gain_in, controllers), refs = refs[:blocks], refs[blocks : blocks + 3], refs[blocks + 3 :]
    d_tokens_out, outs, (total, gain) = refs[0], refs[1:-2], refs[-2:]
    i = pl.program_id(0)
    length, width = d_hidden.shape[1:]

    @pl.when(i == 0)
    def _():
        total[...] = jnp.zeros_like(total)
        gain[...] = jnp.zeros_like(gain)

    rows = tokens[0].astype(F32)
    inverse = inverse_rms(rows)
    normed = rows * inverse
    entry = (normed * gain_attn[...]).astype(BF16)
    d_entry = partial[0] + attend_back(
        entry, d_hidden[0].astype(BF16), packs, joint, context, causal_mask(length), head_masks(length), total
    )
    d_entry = d_entry.astype(BF16).astype(F32)
    gain[0:1] += jnp.sum(d_entry * normed, axis=0, keepdims=True)
    d_normed = d_entry * gain_attn[...]
    d_tokens = d_hidden[0] + inverse * (
        d_normed - normed * jnp.mean(d_normed * normed, axis=-1, keepdims=True)
    )
    live = (place[0] + i < place[1]).astype(F32)
    d_tokens_out[0] = (d_tokens * live).astype(BF16)

    @pl.when(i == pl.num_programs(0) - 1)
    def _():
        pieces = width // LANES
        tail = [x[0:1, c * LANES : (c + 1) * LANES] for x in (gain, gain_in) for c in range(pieces)]
        tail.append(jnp.zeros((16 - 2 * pieces, LANES), F32))
        store_weights(total, controllers, outs, lanes, jnp.concatenate(tail, axis=0).astype(BF16))


def attention_back_far(
    place, tokens, cotangent, back, hidden, joint, context, packs, gain_attn, gain_mix, controllers, height
):
    total, length, width = tokens.shape
    slots = hidden.shape[0]
    spread, part = back.shape[0], back.shape[2] // slots
    inner = context.shape[2]
    blocks = len(packs)
    count = controllers.shape[0]

    def own(i, place):
        return (jnp.minimum(place[0] + i, total - 1), 0, 0)

    rows = pl.BlockSpec((1, length, width), local_block)
    return pl.pallas_call(
        functools.partial(back_far_kernel, blocks, inner // count),
        grid_spec=pltpu.PrefetchScalarGridSpec(
            num_scalar_prefetch=1,
            grid=(slots,),
            in_specs=[
                pl.BlockSpec((1, length, width), own),
                pl.BlockSpec((1, length, width), own),
                pl.BlockSpec((spread, 1, part, width), lambda i, place: (0, 0, i, 0)),
                pl.BlockSpec((spread, 1, part, width), lambda i, place: (0, 1, i, 0)),
                rows,
                pl.BlockSpec((1, length, 3 * inner), local_block),
                pl.BlockSpec((1, length, inner), local_block),
            ]
            + [whole(p.shape) for p in packs]
            + [whole((1, width))] * 2
            + [whole(controllers.shape)],
            out_specs=[rows, rows, rows, whole((8, width))] + [whole((height, LANES))] * count,
            scratch_shapes=[pltpu.VMEM((blocks, 4 * width, LANES), F32)],
        ),
        out_shape=[
            jax.ShapeDtypeStruct((slots, length, width), F32),
            jax.ShapeDtypeStruct((slots, length, width), F32),
            jax.ShapeDtypeStruct((slots, length, width), BF16),
            jax.ShapeDtypeStruct((8, width), F32),
        ]
        + [jax.ShapeDtypeStruct((height, LANES), BF16)] * count,
        compiler_params=params("arbitrary"),
        cost_estimate=pl.CostEstimate(
            flops=0,
            bytes_accessed=slots * length * (width * 18 + inner * 8) + 16 * width * inner,
            transcendentals=slots * length * length * inner // HEAD_WIDTH,
        ),
        name="attention_back_far",
    )(place, tokens, cotangent, back, back, hidden, joint, context, *packs, gain_attn, gain_mix, controllers)


def attention_back_near(
    place, tokens, d_hidden, partial, joint, context, packs, gain_attn, gain_in, controllers, height
):
    total, length, width = tokens.shape
    slots, _, inner = context.shape
    blocks = len(packs)
    count = controllers.shape[0]

    def own(i, place):
        return (jnp.minimum(place[0] + i, total - 1), 0, 0)

    rows = pl.BlockSpec((1, length, width), local_block)
    return pl.pallas_call(
        functools.partial(back_near_kernel, blocks, inner // count),
        grid_spec=pltpu.PrefetchScalarGridSpec(
            num_scalar_prefetch=1,
            grid=(slots,),
            in_specs=[
                pl.BlockSpec((1, length, width), own),
                rows,
                rows,
                pl.BlockSpec((1, length, 3 * inner), local_block),
                pl.BlockSpec((1, length, inner), local_block),
            ]
            + [whole(p.shape) for p in packs]
            + [whole((1, width)), whole((8, width)), whole(controllers.shape)],
            out_specs=[rows] + [whole((height, LANES))] * count,
            scratch_shapes=[
                pltpu.VMEM((blocks, 4 * width, LANES), F32),
                pltpu.VMEM((8, width), F32),
            ],
        ),
        out_shape=[
            jax.ShapeDtypeStruct((slots, length, width), BF16),
        ]
        + [jax.ShapeDtypeStruct((height, LANES), BF16)] * count,
        compiler_params=params("arbitrary"),
        cost_estimate=pl.CostEstimate(
            flops=0,
            bytes_accessed=slots * length * (width * 12 + inner * 8) + 16 * width * inner,
            transcendentals=slots * length * length * inner // HEAD_WIDTH,
        ),
        name="attention_back_near",
    )(place, tokens, d_hidden, partial, joint, context, *packs, gain_attn, gain_in, controllers)


def swap_core(x):
    narrow = lax.axis_size("narrow")
    return lax.ppermute(x, "narrow", [(n, n ^ 1) for n in range(narrow)])


def from_chip(x, k):
    narrow = lax.axis_size("narrow")
    return lax.ppermute(x, "narrow", [((n + 2 * k) % narrow, n) for n in range(narrow)])


def to_chip(x, k):
    narrow = lax.axis_size("narrow")
    return lax.ppermute(x, "narrow", [(n, (n + 2 * k) % narrow) for n in range(narrow)])


def relative_narrow():
    narrow = lax.axis_size("narrow")
    me = lax.axis_index("narrow")
    return [lax.bitwise_xor(lax.rem(me + 2 * (j // 2), narrow), j % 2) for j in range(narrow)]


def gather_narrow(x):
    blocks = []
    for k in range(lax.axis_size("narrow") // 2):
        piece = from_chip(x, k) if k else x
        blocks += [piece, swap_core(piece)]
    return blocks


def far_sums(pieces):
    pairs = [(pieces[2 * k], swap_core(pieces[2 * k + 1])) for k in range(len(pieces) // 2)]
    return [(x.astype(F32) + y.astype(F32)).astype(BF16) for x, y in pairs]


def after(x, *others):
    return lax.optimization_barrier((x, others))[0]


def wide_parts(x):
    wide = lax.axis_size("wide")
    parts = x.astype(BF16).reshape(wide, x.shape[0] // wide, x.shape[1])
    parts = lax.all_to_all(parts, "wide", split_axis=0, concat_axis=0, tiled=True)
    return jnp.sum(parts.astype(F32), axis=0).astype(BF16)


def from_parts(part):
    parts = jnp.broadcast_to(part[None], (lax.axis_size("wide"),) + part.shape)
    parts = lax.all_to_all(parts, "wide", split_axis=0, concat_axis=0, tiled=True)
    return parts.reshape(-1, part.shape[-1]).astype(F32)


def to_relative(x, j):
    narrow = lax.axis_size("narrow")
    k, other = j // 2, j % 2
    return lax.ppermute(x, "narrow", [(n, ((n + 2 * k) % narrow) ^ other) for n in range(narrow)])


def from_relative(x, j):
    narrow = lax.axis_size("narrow")
    k, other = j // 2, j % 2
    return lax.ppermute(x, "narrow", [(((n + 2 * k) % narrow) ^ other, n) for n in range(narrow)])


def to_unit(x, d):
    wide = lax.axis_size("wide")
    return lax.ppermute(x, "wide", [(w, w ^ d) for w in range(wide)])


def place_kernel(where, *refs):
    pieces, out = refs[:-1], refs[-1]
    for j, piece in enumerate(pieces):

        @pl.when(pl.program_id(0) == j)
        def _(piece=piece):
            out[...] = piece[...]


def place_blocks(pieces, where):
    count = len(pieces)
    shape = pieces[0].shape
    return pl.pallas_call(
        place_kernel,
        grid_spec=pltpu.PrefetchScalarGridSpec(
            num_scalar_prefetch=1,
            grid=(count,),
            in_specs=[whole(shape)] * count,
            out_specs=pl.BlockSpec(shape, lambda j, where: (where[j], 0, 0)),
        ),
        out_shape=jax.ShapeDtypeStruct((count * shape[0],) + shape[1:], pieces[0].dtype),
        compiler_params=params("arbitrary"),
        cost_estimate=pl.CostEstimate(
            flops=0, bytes_accessed=pieces[0].size * 4 * count, transcendentals=0
        ),
        name="place_blocks",
    )(where, *pieces)


def body(
    tokens,
    cotangent,
    counts,
    group_order,
    query_weight,
    key_weight,
    value_weight,
    output_weight,
    gain_attn,
    gain_mix,
    controller,
    w_in,
    b_in,
    w_out,
    b_out,
):
    slot_count, seq_len, model_width = tokens.shape
    wide, narrow = lax.axis_size("wide"), lax.axis_size("narrow")
    spread = wide * narrow
    wide_index, narrow_index = lax.axis_index("wide"), lax.axis_index("narrow")
    slots = -(-slot_count // narrow)
    part = seq_len // spread
    padded_part = -(-part // 8) * 8
    local_experts = w_in.shape[0]
    experts = local_experts * narrow
    relative = jnp.stack(relative_narrow())
    head_columns = query_weight.shape[1]

    seq_ends = jnp.cumsum(counts)
    seq_starts = seq_ends - counts
    own_count = counts[wide_index]
    place = jnp.stack([narrow_index * slots, own_count]).astype(jnp.int32)
    slot_ids = jnp.arange(slots * narrow)
    slot_seqs = jnp.where(slot_ids[None] < counts[:, None], seq_starts[:, None] + slot_ids[None], -1)
    matches = slot_seqs.reshape(-1, 1) == group_order[None]
    slot_group = jnp.sum(jnp.where(matches, 1 + jnp.arange(group_order.shape[0]) // GROUP, 0), axis=1) - 1
    positions = jnp.arange(padded_part)
    row_code = jnp.where(slot_group[:, None] >= 0, slot_group[:, None] * padded_part + positions, -1)
    row_code = row_code.reshape(-1, 1).astype(jnp.int32)
    per_expert = GROUPS * padded_part
    col_code = (jnp.arange(experts * per_expert) % per_expert).astype(jnp.int32)[None]
    tile = jnp.repeat(jnp.eye(experts, dtype=BF16), per_expert, axis=1)

    pack = pack_weights(query_weight, key_weight, value_weight, output_weight)
    packs = [pack, swap_core(pack)]
    far_packs = [from_chip(pack, k) for k in range(1, narrow // 2)]
    joined = LANES // head_columns

    def join(packs):
        if joined == 1:
            return packs
        packs = [p.reshape(model_width, 4, head_columns) for p in packs]
        return [
            jnp.concatenate(packs[i : i + joined], axis=2).reshape(model_width, -1)
            for i in range(0, len(packs), joined)
        ]

    controllers = jnp.stack(gather_narrow(controller.T))
    controllers = controllers[jnp.argsort(relative)].reshape(experts, model_width).T

    gain_attn_row, gain_mix_row = gain_attn[None], gain_mix[None]

    def to_positions(x):
        x = lax.all_to_all(x, BOTH, split_axis=0, concat_axis=0, tiled=True)
        x = jnp.pad(x, ((0, 0), (0, 0), (0, padded_part - part), (0, 0)))
        return x.reshape(-1, model_width)

    def to_slots(x):
        x = x.reshape(spread, 2, slots, padded_part, model_width)[:, :, :, :part]
        x = x.reshape(spread, 2, slots * part, model_width)
        return lax.all_to_all(x, BOTH, split_axis=0, concat_axis=0, tiled=True)

    cots, *packs = lax.optimization_barrier((cotangent, *packs))
    cots = jnp.pad(cots, ((0, slots * narrow - slot_count), (0, 0), (0, 0)))
    cots = cots.reshape(slots * narrow, wide, narrow, part, model_width)
    cots = lax.dynamic_index_in_dim(cots, narrow_index, axis=2, keepdims=False).transpose(1, 0, 2, 3)
    cots = lax.all_to_all(cots, "wide", split_axis=0, concat_axis=0, tiled=True)
    cots = jnp.pad(cots, ((0, 0), (0, 0), (0, padded_part - part), (0, 0)))
    cot_rows = cots.reshape(-1, model_width)

    packs = join(packs)
    partial, joint_near, context_near = attention_near(place, tokens, packs, gain_attn_row, slots)
    partial, far_packs = lax.optimization_barrier((partial, far_packs))
    far_packs = join([x for piece in far_packs for x in (piece, swap_core(piece))])
    mix_sent, hidden, joint_far, context_far = attention_far(
        place, tokens, partial, far_packs, gain_attn_row, gain_mix_row, slots, spread
    )
    mix_rows = to_positions(mix_sent)
    probs, spread_probs, *both = mix_forward(
        padded_part, relative, mix_rows, cot_rows, controllers, row_code, col_code, tile, narrow
    )

    rows = GROUPS * part

    def trim(x):
        x = x.reshape(local_experts, 2, GROUPS, padded_part, model_width)[:, :, :, :part]
        return x.reshape(local_experts, 2, rows, model_width)

    def untrim(x):
        x = x.reshape(local_experts, 2, GROUPS, part, model_width)
        x = jnp.pad(x, ((0, 0), (0, 0), (0, 0), (0, padded_part - part), (0, 0)))
        return x.reshape(local_experts, 2, -1, model_width)

    both = [trim(x) for x in both]
    both = both[:1] + [to_relative(x, j) for j, x in enumerate(both) if j]
    halves = 2 if wide % 4 == 0 else 1
    units = wide // halves
    held, share = max(local_experts // units, 1), max(units // local_experts, 1)
    unit = lax.rem(wide_index, units)
    shape = (held, 2, rows, model_width)
    tokens_sent = jnp.stack(both).reshape((share, narrow // share, units // share) + shape)
    tokens_sent = tokens_sent.transpose(2, 0, 1, 3, 4, 5, 6).reshape((units, narrow // share) + shape)
    tokens_sent = jnp.concatenate([tokens_sent] * halves)
    tokens_sent, both = lax.optimization_barrier((tokens_sent, both))
    tokens_all = lax.all_to_all(tokens_sent, "wide", split_axis=0, concat_axis=0, tiled=True)
    if rows % 16 == 0:
        back = experts_at_positions(both, w_in, b_in, w_out, b_out)
    else:
        lines = jnp.stack(both, axis=2).reshape(local_experts, 2, narrow * rows, model_width)
        (back,) = experts_at_positions([lines], w_in, b_in, w_out, b_out)
        back = back.reshape(local_experts, 2, narrow, rows, model_width)
        back = [back[:, :, j] for j in range(narrow)]

    where = jnp.stack([wide_index // units, unit]).astype(jnp.int32)
    first = (unit * held // share).astype(jnp.int32)
    expert_grads = [
        expert_weights(where, (first + p)[None], p, tokens_all, w_in, b_in, w_out, wide, units)
        for p in range(held)
    ]

    back = [untrim(x if j == 0 else from_relative(x, j)) for j, x in enumerate(back)]
    slot_rows, grad_controller = mix_backward(
        padded_part,
        relative,
        spread_probs,
        mix_rows,
        cot_rows,
        probs,
        back,
        controllers,
        row_code,
        col_code,
        tile,
        spread,
    )
    slot_rows = to_slots(slot_rows)
    expert_grads = [[x[0]] + [to_unit(x[d], d) for d in range(1, units)] for x in expert_grads]
    slot_rows = after(slot_rows, expert_grads[0][:-1], [x[0] for x in expert_grads])

    height = 4 * model_width
    grad_controller = grad_controller.astype(BF16).reshape(narrow, -1, LANES)[relative]
    end = height + grad_controller.shape[1]
    rows_sent = -(-(end + 16) // (16 * wide)) * 16 * wide
    partial, d_hidden, mixed_part, gain_mix_part, *far = attention_back_far(
        place,
        tokens,
        cotangent,
        slot_rows,
        hidden,
        joint_far,
        context_far,
        far_packs,
        gain_attn_row,
        gain_mix_row,
        grad_controller[2:],
        rows_sent,
    )
    early = [x[1:-1] for x in expert_grads[1:]]
    far, early = lax.optimization_barrier((far, early))
    for x, pieces in zip(expert_grads[1:], early):
        x[1:-1] = pieces
    partial, far = lax.optimization_barrier((partial, far_sums(far)))
    far = sum([to_chip(x, k + 1).astype(F32) for k, x in enumerate(far)], 0.0)
    d_tokens, kept, sent = attention_back_near(
        place,
        tokens,
        d_hidden,
        partial,
        joint_near,
        context_near,
        packs,
        gain_attn_row,
        gain_mix_part,
        grad_controller[:2],
        rows_sent,
    )
    d_tokens, kept, sent, far, expert_grads[0][-1] = lax.optimization_barrier(
        (d_tokens, kept, sent, far, expert_grads[0][-1])
    )
    weights = kept.astype(F32) + swap_core(sent).astype(F32) + far
    part_sums = wide_parts(weights)

    d_tokens = [d_tokens] + [from_chip(d_tokens, k) for k in range(1, narrow // 2)]
    swapped = [swap_core(d_tokens[0]), swap_core(mixed_part)]
    mixed_part, d_tokens[1:], swapped, expert_grads = lax.optimization_barrier(
        (mixed_part, d_tokens[1:], swapped, expert_grads)
    )
    mixed_part = [mixed_part] + [from_chip(mixed_part, k) for k in range(1, narrow // 2)]
    order = lax.bitwise_xor(unit, jnp.arange(units)) * held
    order = (order[None] + jnp.arange(held)[:, None]).reshape(-1)
    pieces = [piece for x in expert_grads for piece in x]
    g_w_in, g_w_out, bias = owned_weights(pieces, order, w_in.shape[2], wide)
    swapped = swapped + [swap_core(x) for x in d_tokens[1:]]
    part_sums, bias, swapped = lax.optimization_barrier((part_sums, bias, swapped))

    def placed(pieces, others):
        pieces = [x for pair in zip(pieces, others) for x in pair]
        return place_blocks(pieces, relative)[:slot_count]

    d_tokens = placed(d_tokens, swapped[:1] + swapped[2:])
    mixed_part[1:], d_tokens = lax.optimization_barrier((mixed_part[1:], d_tokens))
    mixed_part = placed(mixed_part, swapped[1:2] + [swap_core(x) for x in mixed_part[1:]])
    weights = from_parts(part_sums)
    gains = weights[end : end + 16].astype(BF16)
    gains = sum([to_chip(gains, k).astype(F32) for k in range(1, narrow // 2)], gains.astype(F32))
    projections = weights[: 3 * model_width, :head_columns].reshape(3, model_width, head_columns)
    output_weight_gradient = weights[3 * model_width : height].reshape(-1, LANES, LANES)[:, :head_columns]
    output_weight_gradient = output_weight_gradient.transpose(1, 0, 2).reshape(head_columns, -1)
    g_controller = weights[height:end].reshape(local_experts, model_width).T
    lines = model_width // LANES
    g_gain_attn = gains[:lines].reshape(-1)
    g_gain_mix = gains[lines : 2 * lines].reshape(-1)

    def over_share(x):
        return jnp.sum(x.reshape((local_experts, share) + x.shape[1:]), axis=1)

    g_w_in, g_w_out, bias = (over_share(x) for x in (g_w_in, g_w_out, bias))
    g_b_in = bias[:, : w_in.shape[2] // model_width].reshape(local_experts, -1)
    g_b_out = bias[:, -1]

    return (
        mixed_part,
        d_tokens,
        projections[0],
        projections[1],
        projections[2],
        output_weight_gradient,
        g_gain_attn,
        g_gain_mix,
        g_controller,
        g_w_in,
        g_b_in,
        g_w_out,
        g_b_out,
    )


def solution(mesh):
    placed = (
        P("wide", None, None),
        P("wide", None, None),
        P(),
        P(),
        P(None, "narrow"),
        P(None, "narrow"),
        P(None, "narrow"),
        P("narrow", None),
        P(),
        P(),
        P(None, "narrow"),
        P("narrow", None, None),
        P("narrow", None),
        P("narrow", None, None),
        P("narrow", None),
    )
    return jax.shard_map(
        body,
        mesh=mesh,
        in_specs=placed,
        out_specs=(
            P("wide", None, None),
            P("wide", None, None),
            P(None, "narrow"),
            P(None, "narrow"),
            P(None, "narrow"),
            P("narrow", None),
            P(),
            P(),
            P(None, "narrow"),
            P("narrow", "wide", None),
            P("narrow", None),
            P("narrow", "wide", None),
            P("narrow", None),
        ),
        check_vma=False,
    )
```

```python
import functools

import jax
import jax.numpy as jnp
from jax import lax
from jax.experimental import pallas as pl
from jax.experimental.pallas import tpu as pltpu
from jax.sharding import PartitionSpec as P

HEAD_WIDTH = 64
GROUP = 32
GROUPS = 2
LANES = 128

EPSILON = 1e-05
NEGATIVE = -1e30
BOTH = ("wide", "narrow")
F32 = jnp.float32
BF16 = jnp.bfloat16
VMEM_LIMIT = 56 * 1024 * 1024


def mm(a, b):
    return lax.dot_general(a, b, (((1,), (0,)), ((), ())), preferred_element_type=F32)


def mm_nt(a, b):
    return lax.dot_general(a, b, (((1,), (1,)), ((), ())), preferred_element_type=F32)


def mm_tn(a, b):
    return lax.dot_general(a, b, (((0,), (0,)), ((), ())), preferred_element_type=F32)


def params(*semantics):
    return pltpu.CompilerParams(dimension_semantics=semantics or None, vmem_limit_bytes=VMEM_LIMIT)


def whole(shape):
    zeros = (0,) * len(shape)
    return pl.BlockSpec(tuple(shape), lambda *_: zeros)


def head_masks(rows):
    lane = lax.broadcasted_iota(jnp.int32, (rows, LANES), 1)
    return [(lane >= h * HEAD_WIDTH) & (lane < (h + 1) * HEAD_WIDTH) for h in range(LANES // HEAD_WIDTH)]


def keep(mask, rows):
    return jnp.where(mask, rows, jnp.zeros_like(rows))


def causal_probs(query_head, keys, causal):
    scores = mm_nt(query_head, keys) * (float(HEAD_WIDTH) ** -0.5)
    scores = jnp.where(causal, scores, NEGATIVE)
    powers = jnp.exp(scores - jnp.max(scores, axis=-1, keepdims=True))
    return powers * (1.0 / jnp.sum(powers, axis=-1, keepdims=True))


def causal_mask(length):
    return lax.broadcasted_iota(jnp.int32, (length, length), 0) >= lax.broadcasted_iota(
        jnp.int32, (length, length), 1
    )


def inverse_rms(rows):
    return lax.rsqrt(jnp.mean(rows * rows, axis=-1, keepdims=True) + EPSILON)


def attend(entry, packs, causal, masks, joint_out, context_out):
    attention = None
    for j, pack in enumerate(packs):
        joint = mm(entry, pack[:, : 3 * LANES]).astype(BF16)
        joint_out[0, :, j * 3 * LANES : (j + 1) * 3 * LANES] = joint
        q, k, v = (joint[:, i * LANES : (i + 1) * LANES] for i in range(3))
        context = None
        for mask in masks:
            probs = causal_probs(keep(mask, q), k, causal)
            term = mm(probs.astype(BF16), keep(mask, v))
            context = term if context is None else context + term
        context = context.astype(BF16)
        context_out[0, :, j * LANES : (j + 1) * LANES] = context
        term = mm_nt(context, pack[:, 3 * LANES :])
        attention = term if attention is None else attention + term
    return attention


def near_kernel(blocks, place, tokens, *refs):
    packs, (gain_attn, partial_out, joint_out, context_out) = refs[:blocks], refs[blocks:]
    rows = tokens[0].astype(F32)
    entry = (rows * inverse_rms(rows) * gain_attn[...]).astype(BF16)
    length = rows.shape[0]
    partial_out[0] = rows + attend(
        entry, packs, causal_mask(length), head_masks(length), joint_out, context_out
    )


def far_kernel(blocks, place, tokens, partial, *refs):
    packs = refs[:blocks]
    gain_attn, gain_mix, mix_out, hidden_out, joint_out, context_out = refs[blocks:]
    rows = tokens[0].astype(F32)
    entry = (rows * inverse_rms(rows) * gain_attn[...]).astype(BF16)
    length = rows.shape[0]
    hidden = partial[0] + attend(
        entry, packs, causal_mask(length), head_masks(length), joint_out, context_out
    )
    mixed = hidden * inverse_rms(hidden) * gain_mix[...]
    mix_out[...] = mixed.reshape(mix_out.shape).astype(BF16)
    hidden_out[0] = hidden


def local_block(i, place):
    return (i, 0, 0)


def attention_near(place, tokens, packs, gain_attn, slots):
    total, length, width = tokens.shape
    inner = len(packs) * LANES
    return pl.pallas_call(
        functools.partial(near_kernel, len(packs)),
        grid_spec=pltpu.PrefetchScalarGridSpec(
            num_scalar_prefetch=1,
            grid=(slots,),
            in_specs=[
                pl.BlockSpec((1, length, width), lambda i, place: (jnp.minimum(place[0] + i, total - 1), 0, 0))
            ]
            + [whole(p.shape) for p in packs]
            + [whole((1, width))],
            out_specs=[
                pl.BlockSpec((1, length, width), local_block),
                pl.BlockSpec((1, length, 3 * inner), local_block),
                pl.BlockSpec((1, length, inner), local_block),
            ],
        ),
        out_shape=[
            jax.ShapeDtypeStruct((slots, length, width), F32),
            jax.ShapeDtypeStruct((slots, length, 3 * inner), BF16),
            jax.ShapeDtypeStruct((slots, length, inner), BF16),
        ],
        compiler_params=params("arbitrary"),
        cost_estimate=pl.CostEstimate(
            flops=slots * 2 * length * (4 * width * inner + 4 * length * inner),
            bytes_accessed=slots * length * (width * 6 + inner * 8) + 8 * width * inner,
            transcendentals=slots * length * length * inner // HEAD_WIDTH,
        ),
        name="attention_near",
    )(place, tokens, *packs, gain_attn)


def attention_far(place, tokens, partial, packs, gain_attn, gain_mix, slots, spread):
    total, length, width = tokens.shape
    inner = len(packs) * LANES
    part = length // spread
    return pl.pallas_call(
        functools.partial(far_kernel, len(packs)),
        grid_spec=pltpu.PrefetchScalarGridSpec(
            num_scalar_prefetch=1,
            grid=(slots,),
            in_specs=[
                pl.BlockSpec((1, length, width), lambda i, place: (jnp.minimum(place[0] + i, total - 1), 0, 0)),
                pl.BlockSpec((1, length, width), local_block),
            ]
            + [whole(p.shape) for p in packs]
            + [whole((1, width))] * 2,
            out_specs=[
                pl.BlockSpec((spread, 1, part, width), lambda i, place: (0, i, 0, 0)),
                pl.BlockSpec((1, length, width), local_block),
                pl.BlockSpec((1, length, 3 * inner), local_block),
                pl.BlockSpec((1, length, inner), local_block),
            ],
        ),
        out_shape=[
            jax.ShapeDtypeStruct((spread, slots, part, width), BF16),
            jax.ShapeDtypeStruct((slots, length, width), F32),
            jax.ShapeDtypeStruct((slots, length, 3 * inner), BF16),
            jax.ShapeDtypeStruct((slots, length, inner), BF16),
        ],
        compiler_params=params("arbitrary"),
        cost_estimate=pl.CostEstimate(
            flops=slots * 2 * length * (4 * width * inner + 4 * length * inner),
            bytes_accessed=slots * length * (width * 12 + inner * 8) + 8 * width * inner,
            transcendentals=slots * length * length * inner // HEAD_WIDTH,
        ),
        name="attention_far",
    )(place, tokens, partial, *packs, gain_attn, gain_mix)


def pack_kernel(query, key, value, output, out):
    width = query.shape[1]
    for i, ref in enumerate((query, key, value)):
        out[:, i * width : (i + 1) * width] = ref[...]
    out[:, 3 * width :] = output[...].T


def pack_weights(query, key, value, output):
    width, columns = query.shape
    if columns % LANES:
        return jnp.concatenate([query, key, value, output.T], axis=1)
    return pl.pallas_call(
        pack_kernel,
        out_shape=jax.ShapeDtypeStruct((width, 4 * columns), BF16),
        compiler_params=params(),
        cost_estimate=pl.CostEstimate(flops=0, bytes_accessed=16 * width * columns, transcendentals=0),
        name="pack_weights",
    )(query, key, value, output)


def slot_softmax(logits, codes, part):
    experts = logits.shape[1]
    logits = logits.reshape(-1, part, experts)
    codes = jnp.broadcast_to(codes, (codes.shape[0], experts)).reshape(-1, part, experts)
    total = jnp.zeros_like(logits)
    for g in range(GROUPS):
        inside = (codes >= g * part) & (codes < (g + 1) * part)
        held = jnp.where(inside, logits, NEGATIVE)
        powers = jnp.where(inside, jnp.exp(held - jnp.max(held, axis=0, keepdims=True)), 0.0)
        total = total + powers / jnp.sum(powers, axis=0, keepdims=True)
    return total.reshape(-1, experts)


def group_totals(terms, codes, part):
    experts = terms.shape[1]
    terms = terms.reshape(-1, part, experts)
    codes = jnp.broadcast_to(codes, (codes.shape[0], experts)).reshape(-1, part, experts)
    total = jnp.zeros_like(terms)
    for g in range(GROUPS):
        inside = (codes >= g * part) & (codes < (g + 1) * part)
        total = jnp.where(inside, jnp.sum(jnp.where(inside, terms, 0.0), axis=0, keepdims=True), total)
    return total.reshape(-1, experts)


def mix_kernel(part, relative, rows, cots, controller, row_code, col_code, tile, probs_out, spread_out, *refs):
    sent, (merged, grads) = refs[:-2], refs[-2:]
    held = rows[...]
    probs = slot_softmax(mm(held, controller[...]), row_code[...], part)
    probs_out[...] = probs
    wide = mm(probs.astype(BF16), tile[...])
    spread = jnp.where(row_code[...] == col_code[...], wide, 0.0).astype(BF16)
    spread_out[...] = spread
    count, _, lines, _ = sent[0].shape
    merged[...] = mm_tn(spread, held).astype(BF16)
    grads[...] = mm_tn(spread, cots[...]).astype(BF16)
    for j, out in enumerate(sent):
        for e in range(count):
            at = pl.ds(pl.multiple_of((relative[j] * count + e) * lines, lines), lines)
            out[e, 0] = merged[at]
            out[e, 1] = grads[at]


def mix_forward(part, relative, rows, cots, controller, row_code, col_code, tile, narrow):
    count, width = rows.shape
    experts, columns = tile.shape
    sent = (experts // narrow, 2, columns // experts, width)
    return pl.pallas_call(
        functools.partial(mix_kernel, part),
        grid_spec=pltpu.PrefetchScalarGridSpec(
            num_scalar_prefetch=1,
            grid=(1,),
            in_specs=[whole(x.shape) for x in (rows, cots, controller, row_code, col_code, tile)],
            out_specs=[whole((count, experts)), whole((count, columns))]
            + [whole(sent)] * narrow,
            scratch_shapes=[pltpu.VMEM((columns, width), BF16)] * 2,
        ),
        out_shape=[
            jax.ShapeDtypeStruct((count, experts), F32),
            jax.ShapeDtypeStruct((count, columns), BF16),
        ]
        + [jax.ShapeDtypeStruct(sent, BF16)] * narrow,
        compiler_params=params("arbitrary"),
        cost_estimate=pl.CostEstimate(
            flops=4 * count * columns * width,
            bytes_accessed=6 * count * width * 2,
            transcendentals=count * experts * 2,
        ),
        name="mix_forward",
    )(relative, rows, cots, controller, row_code, col_code, tile)


def unmix_kernel(
    part, narrow, relative, spread, rows, cots, probs, controller, row_code, col_code, tile, *refs
):
    back, (sent, gain_out, outs, grads) = refs[:narrow], refs[narrow:]
    count, _, lines, _ = back[0].shape
    for j, piece in enumerate(back):
        for e in range(count):
            at = pl.ds(pl.multiple_of((relative[j] * count + e) * lines, lines), lines)
            outs[at] = piece[e, 0]
            grads[at] = piece[e, 1]
    held = rows[...]
    pairs = (mm_nt(cots[...], outs[...]) + mm_nt(held, grads[...])).astype(BF16)
    pairs = jnp.where(row_code[...] == col_code[...], pairs, jnp.zeros_like(pairs))
    d_weights = mm_nt(pairs, tile[...])
    p = probs[...]
    d_logits = (p * (d_weights - group_totals(p * d_weights, row_code[...], part))).astype(BF16)
    shape = (sent.shape[0],) + sent.shape[2:]
    grad = mm(spread[...], grads[...]) + mm_nt(d_logits, controller[...])
    sent[:, 0] = grad.reshape(shape).astype(BF16)
    sent[:, 1] = mm(spread[...], outs[...]).reshape(shape).astype(BF16)
    gain_out[...] = mm_tn(d_logits, held)


def mix_backward(part, relative, spread, rows, cots, probs, back, controller, row_code, col_code, tile, devices):
    count, width = rows.shape
    experts, columns = tile.shape
    operands = (spread, rows, cots, probs, controller, row_code, col_code, tile) + tuple(back)
    outs = [
        jax.ShapeDtypeStruct((devices, 2, count // devices, width), BF16),
        jax.ShapeDtypeStruct((experts, width), F32),
    ]
    return pl.pallas_call(
        functools.partial(unmix_kernel, part, len(back)),
        grid_spec=pltpu.PrefetchScalarGridSpec(
            num_scalar_prefetch=1,
            grid=(1,),
            in_specs=[whole(x.shape) for x in operands],
            out_specs=[whole(x.shape) for x in outs],
            scratch_shapes=[pltpu.VMEM((columns, width), BF16)] * 2,
        ),
        out_shape=outs,
        compiler_params=params("arbitrary"),
        cost_estimate=pl.CostEstimate(
            flops=8 * count * columns * width,
            bytes_accessed=8 * count * width * 2,
            transcendentals=0,
        ),
        name="mix_backward",
    )(relative, *operands)


GELU_SLOPE = 0.7978845608028654
GELU_CUBE = 0.044715


def gelu_pair(x):
    square = x * x
    bend = jnp.tanh(GELU_SLOPE * x * (1.0 + GELU_CUBE * square))
    gate = 0.5 * (1.0 + bend)
    slope = gate + 0.5 * x * (1.0 - bend * bend) * (GELU_SLOPE * (1.0 + 3.0 * GELU_CUBE * square))
    return x * gate, slope


def expert_kernel(count, *refs):
    both, (w_in, b_in, w_out, b_out), sent = refs[:count], refs[count : count + 4], refs[count + 4 :]
    rows = both[0].shape[2]
    merged = jnp.concatenate([x[0, 0] for x in both], axis=0)
    grads = jnp.concatenate([x[0, 1] for x in both], axis=0)
    act, slope = gelu_pair(mm(merged, w_in[0]) + b_in[0])
    outs = mm(act.astype(BF16), w_out[0]) + b_out[0]
    d_pre = (mm_nt(grads, w_out[0]) * slope).astype(BF16)
    d_merged = mm_nt(d_pre, w_in[0])
    for j, out in enumerate(sent):
        at = slice(j * rows, (j + 1) * rows)
        out[0, 0] = outs[at].astype(BF16)
        out[0, 1] = d_merged[at].astype(BF16)


def experts_at_positions(both, w_in, b_in, w_out, b_out):
    experts, _, rows, width = both[0].shape
    inner = w_in.shape[2]
    sources, count = len(both), experts * rows
    tokens = pl.BlockSpec((1, 2, rows, width), lambda e: (e, 0, 0, 0))
    return pl.pallas_call(
        functools.partial(expert_kernel, sources),
        grid=(experts,),
        in_specs=[tokens] * sources
        + [
            pl.BlockSpec((1, width, inner), lambda e: (e, 0, 0)),
            pl.BlockSpec((1, 1, inner), lambda e: (e, 0, 0)),
            pl.BlockSpec((1, inner, width), lambda e: (e, 0, 0)),
            pl.BlockSpec((1, 1, width), lambda e: (e, 0, 0)),
        ],
        out_specs=[tokens] * sources,
        out_shape=[jax.ShapeDtypeStruct(x.shape, BF16) for x in both],
        compiler_params=params("arbitrary"),
        cost_estimate=pl.CostEstimate(
            flops=8 * sources * count * width * inner,
            bytes_accessed=4 * experts * width * inner + 4 * sources * count * width * 2,
            transcendentals=sources * count * inner,
        ),
        name="experts",
    )(*both, w_in, b_in[:, None], w_out, b_out[:, None])


def weight_kernel(units, where, both, w_in, b_in, w_out, *refs):
    outs, (merged, grads, turned, total) = refs[:units], refs[units:]
    i, half, unit = pl.program_id(0), where[0], where[1]
    steps = pl.num_programs(0)
    width = both.shape[-1]
    span = turned.shape[0]
    rows = span // units
    height = outs[0].shape[0]
    block = height - 16 - steps * rows
    slices = width // block

    @pl.when(i == 0)
    def _():
        merged[...] = both[:, :, 0, 0].reshape(merged.shape)
        grads[...] = both[:, :, 0, 1].reshape(grads.shape)
        turned[...] = merged[:, pl.ds(pl.multiple_of(half * span, span), span)].T
        sums = jnp.sum(grads[...].astype(F32), axis=0, keepdims=True).astype(BF16)
        for out in outs:
            out[height - 16 :] = jnp.zeros((16, width), BF16)
            out[height - 1 :] = sums

    act, slope = gelu_pair(mm(merged[...], w_in[0]) + b_in[0])
    d_pre = (mm_nt(grads[...], w_out[0]) * slope).astype(BF16)
    bias = jnp.sum(d_pre.astype(F32), axis=0, keepdims=True).astype(BF16)
    total[...] = mm(turned[...], d_pre)
    base = pl.ds(pl.multiple_of(i * rows, rows), rows)
    for d, out in enumerate(outs):
        own = pl.ds(pl.multiple_of(lax.bitwise_xor(unit, d) * rows, rows), rows)
        out[base] = total[own].astype(BF16)
    for step in range(steps):

        @pl.when(i == step)
        def _(step=step):
            for out in outs:
                out[height - 16 + step : height - 15 + step] = bias

    @pl.when(i // (steps // 2) == half)
    def _():
        grad = mm_tn(act.astype(BF16), grads[...]).astype(BF16)
        first = (i - half * (steps // 2)) * slices
        for s in range(slices):
            for d, out in enumerate(outs):

                @pl.when(first + s == lax.bitwise_xor(unit, d))
                def _(s=s, out=out):
                    out[height - 16 - block : height - 16] = grad[s * block : (s + 1) * block]


def expert_weights(where, expert, p, both, w_in, b_in, w_out, wide, units):
    sources, inner_sources, _, _, rows, width = both.shape
    inner = w_in.shape[2]
    count = sources * inner_sources * rows
    span = width * units // wide
    height = inner // width * (width // wide) + inner // wide + 16
    return pl.pallas_call(
        lambda where, expert, *refs: weight_kernel(units, where, *refs),
        grid_spec=pltpu.PrefetchScalarGridSpec(
            num_scalar_prefetch=2,
            grid=(inner // width,),
            in_specs=[
                pl.BlockSpec(
                    (sources, inner_sources, 1, 2, rows, width), lambda i, w, e: (0, 0, p, 0, 0, 0)
                ),
                pl.BlockSpec((1, width, width), lambda i, w, e: (e[0], 0, i)),
                pl.BlockSpec((1, 1, width), lambda i, w, e: (e[0], 0, i)),
                pl.BlockSpec((1, width, width), lambda i, w, e: (e[0], i, 0)),
            ],
            out_specs=[whole((height, width))] * units,
            scratch_shapes=[pltpu.VMEM((count, width), BF16)] * 2
            + [pltpu.VMEM((span, count), BF16), pltpu.VMEM((span, width), F32)],
        ),
        out_shape=[jax.ShapeDtypeStruct((height, width), BF16)] * units,
        compiler_params=params("arbitrary"),
        cost_estimate=pl.CostEstimate(
            flops=6 * count * width * inner,
            bytes_accessed=8 * width * inner + 4 * count * width,
            transcendentals=count * inner,
        ),
        name="expert_weights",
    )(where, expert, both, w_in, b_in[:, None], w_out)


def owner_kernel(count, where, *refs):
    pieces, (g_in, g_out, bias) = refs[:count], refs[-3:]
    rows, block = g_in.shape[1], g_out.shape[1]
    width = g_out.shape[2]
    start = pieces[0].shape[0] - 16 - block
    for j, piece in enumerate(pieces):

        @pl.when(pl.program_id(0) == j)
        def _(piece=piece):
            for c in range(g_in.shape[2] // width):
                g_in[0, :, c * width : (c + 1) * width] = piece[c * rows : (c + 1) * rows].astype(F32)
            g_out[0] = piece[start : start + block].astype(F32)
            bias[0] = piece[start + block :].astype(F32)


def owned_weights(pieces, where, total, inner, wide, rest=()):
    count = len(pieces)
    width = pieces[0].shape[1]
    shapes = [(1, width // wide, inner), (1, inner // wide, width), (1, 16, width)]
    return pl.pallas_call(
        functools.partial(owner_kernel, count),
        grid_spec=pltpu.PrefetchScalarGridSpec(
            num_scalar_prefetch=1,
            grid=(count,),
            in_specs=[whole(x.shape) for x in pieces] + [pl.BlockSpec(memory_space=pl.ANY)] * len(rest),
            out_specs=[pl.BlockSpec(x, lambda j, where: (where[j], 0, 0)) for x in shapes],
        ),
        out_shape=[jax.ShapeDtypeStruct((total,) + x[1:], F32) for x in shapes],
        input_output_aliases={1 + count + i: i for i in range(len(rest))},
        compiler_params=params("arbitrary"),
        cost_estimate=pl.CostEstimate(
            flops=0, bytes_accessed=sum(x.size for x in pieces) * 6, transcendentals=0
        ),
        name="owned_weights",
    )(where, *pieces, *rest)


def attend_back(entry, d_low, packs, joint_in, context_in, causal, masks, total):
    width = entry.shape[1]
    scale = float(HEAD_WIDTH) ** -0.5
    d_entry = None
    for j, pack in enumerate(packs):
        base = j * 3 * LANES
        q, k, v = (joint_in[0, :, base + i * LANES : base + (i + 1) * LANES] for i in range(3))
        context = context_in[0, :, j * LANES : (j + 1) * LANES]
        d_context = mm(d_low, pack[:, 3 * LANES :]).astype(BF16)
        d_q, d_k, d_v = [], [], []
        for mask in masks:
            q_head = keep(mask, q)
            d_head = keep(mask, d_context)
            probs = causal_probs(q_head, k, causal)
            d_probs = mm_nt(d_head, v).astype(BF16).astype(F32)
            d_scores = probs * (d_probs - jnp.sum(probs * d_probs, axis=-1, keepdims=True))
            d_scores = d_scores.astype(BF16)
            d_v.append(mm_tn(probs.astype(BF16), d_head))
            d_q.append(mm(d_scores, keep(mask, k)))
            d_k.append(mm_tn(d_scores, q_head))
        joint = [sum(d_q) * scale, sum(d_k) * scale, sum(d_v)]
        joint = jnp.concatenate(joint, axis=1).astype(BF16)
        term = mm_nt(joint, pack[:, : 3 * LANES])
        d_entry = term if d_entry is None else d_entry + term
        grad = mm_tn(entry, joint)
        for c in range(3):
            total[j, c * width : (c + 1) * width] += grad[:, c * LANES : (c + 1) * LANES]
        grad = mm_tn(context, d_low)
        for c in range(width // LANES):
            at = slice(3 * width + c * LANES, 3 * width + (c + 1) * LANES)
            total[j, at] += grad[:, c * LANES : (c + 1) * LANES]
    return d_entry


def store_weights(total, controllers, outs, lanes, gains=None):
    height = total.shape[1]
    for o, out in enumerate(outs):
        j, at = divmod(o, LANES // lanes)
        piece = total[j].astype(BF16)
        if lanes < LANES:
            own = slice(at * lanes, (at + 1) * lanes)
            split = height // 4 * 3
            piece = [jnp.pad(piece[:split, own], ((0, 0), (0, LANES - lanes)))] + [
                jnp.pad(piece[c : c + LANES][own], ((0, LANES - lanes), (0, 0)))
                for c in range(split, height, LANES)
            ]
            piece = jnp.concatenate(piece, axis=0)
        out[:height] = piece
        tail = [controllers[o]]
        if gains is not None:
            tail.append(gains)
        left = out.shape[0] - height - sum(x.shape[0] for x in tail)
        out[height:] = jnp.concatenate(tail + [jnp.zeros((left, LANES), BF16)], axis=0)


def back_far_kernel(blocks, lanes, place, tokens, cots, grads, mixed, hidden, joint, context, *refs):
    packs, (gain_attn, gain_mix, controllers), refs = refs[:blocks], refs[blocks : blocks + 3], refs[blocks + 3 :]
    (partial_out, d_hidden_out, mixed_out, gain_out), outs, total = refs[:4], refs[4:-1], refs[-1]
    i = pl.program_id(0)
    length, width = hidden.shape[1:]
    live = (place[0] + i < place[1]).astype(F32)

    @pl.when(i == 0)
    def _():
        total[...] = jnp.zeros_like(total)
        gain_out[...] = jnp.zeros_like(gain_out)

    rows = hidden[0]
    inverse = inverse_rms(rows)
    normed = rows * inverse
    grad = grads[...].astype(F32).reshape(length, width)
    gain_out[0:1] += jnp.sum(grad * normed, axis=0, keepdims=True)
    d_normed = grad * gain_mix[...]
    d_hidden = cots[0].astype(F32) * live + inverse * (
        d_normed - normed * jnp.mean(d_normed * normed, axis=-1, keepdims=True)
    )
    d_hidden_out[0] = d_hidden
    mixed_out[0] = (live * (hidden[0] + mixed[...].astype(F32).reshape(length, width))).astype(BF16)
    rows = tokens[0].astype(F32)
    entry = (rows * inverse_rms(rows) * gain_attn[...]).astype(BF16)
    partial_out[0] = attend_back(
        entry, d_hidden.astype(BF16), packs, joint, context, causal_mask(length), head_masks(length), total
    )

    @pl.when(i == pl.num_programs(0) - 1)
    def _():
        store_weights(total, controllers, outs, lanes)


def back_near_kernel(blocks, lanes, place, tokens, d_hidden, partial, joint, context, *refs):
    packs, (gain_attn, gain_in, controllers), refs = refs[:blocks], refs[blocks : blocks + 3], refs[blocks + 3 :]
    d_tokens_out, outs, (total, gain) = refs[0], refs[1:-2], refs[-2:]
    i = pl.program_id(0)
    length, width = d_hidden.shape[1:]

    @pl.when(i == 0)
    def _():
        total[...] = jnp.zeros_like(total)
        gain[...] = jnp.zeros_like(gain)

    rows = tokens[0].astype(F32)
    inverse = inverse_rms(rows)
    normed = rows * inverse
    entry = (normed * gain_attn[...]).astype(BF16)
    d_entry = partial[0] + attend_back(
        entry, d_hidden[0].astype(BF16), packs, joint, context, causal_mask(length), head_masks(length), total
    )
    d_entry = d_entry.astype(BF16).astype(F32)
    gain[0:1] += jnp.sum(d_entry * normed, axis=0, keepdims=True)
    d_normed = d_entry * gain_attn[...]
    d_tokens = d_hidden[0] + inverse * (
        d_normed - normed * jnp.mean(d_normed * normed, axis=-1, keepdims=True)
    )
    live = (place[0] + i < place[1]).astype(F32)
    d_tokens_out[0] = (d_tokens * live).astype(BF16)

    @pl.when(i == pl.num_programs(0) - 1)
    def _():
        pieces = width // LANES
        tail = [x[0:1, c * LANES : (c + 1) * LANES] for x in (gain, gain_in) for c in range(pieces)]
        tail.append(jnp.zeros((16 - 2 * pieces, LANES), F32))
        store_weights(total, controllers, outs, lanes, jnp.concatenate(tail, axis=0).astype(BF16))


def attention_back_far(
    place, tokens, cotangent, back, hidden, joint, context, packs, gain_attn, gain_mix, controllers, height
):
    total, length, width = tokens.shape
    slots = hidden.shape[0]
    spread, part = back.shape[0], back.shape[2] // slots
    inner = context.shape[2]
    blocks = len(packs)
    count = controllers.shape[0]

    def own(i, place):
        return (jnp.minimum(place[0] + i, total - 1), 0, 0)

    rows = pl.BlockSpec((1, length, width), local_block)
    return pl.pallas_call(
        functools.partial(back_far_kernel, blocks, inner // count),
        grid_spec=pltpu.PrefetchScalarGridSpec(
            num_scalar_prefetch=1,
            grid=(slots,),
            in_specs=[
                pl.BlockSpec((1, length, width), own),
                pl.BlockSpec((1, length, width), own),
                pl.BlockSpec((spread, 1, part, width), lambda i, place: (0, 0, i, 0)),
                pl.BlockSpec((spread, 1, part, width), lambda i, place: (0, 1, i, 0)),
                rows,
                pl.BlockSpec((1, length, 3 * inner), local_block),
                pl.BlockSpec((1, length, inner), local_block),
            ]
            + [whole(p.shape) for p in packs]
            + [whole((1, width))] * 2
            + [whole(controllers.shape)],
            out_specs=[rows, rows, rows, whole((8, width))] + [whole((height, LANES))] * count,
            scratch_shapes=[pltpu.VMEM((blocks, 4 * width, LANES), F32)],
        ),
        out_shape=[
            jax.ShapeDtypeStruct((slots, length, width), F32),
            jax.ShapeDtypeStruct((slots, length, width), F32),
            jax.ShapeDtypeStruct((slots, length, width), BF16),
            jax.ShapeDtypeStruct((8, width), F32),
        ]
        + [jax.ShapeDtypeStruct((height, LANES), BF16)] * count,
        compiler_params=params("arbitrary"),
        cost_estimate=pl.CostEstimate(
            flops=0,
            bytes_accessed=slots * length * (width * 18 + inner * 8) + 16 * width * inner,
            transcendentals=slots * length * length * inner // HEAD_WIDTH,
        ),
        name="attention_back_far",
    )(place, tokens, cotangent, back, back, hidden, joint, context, *packs, gain_attn, gain_mix, controllers)


def attention_back_near(
    place, tokens, d_hidden, partial, joint, context, packs, gain_attn, gain_in, controllers, height
):
    total, length, width = tokens.shape
    slots, _, inner = context.shape
    blocks = len(packs)
    count = controllers.shape[0]

    def own(i, place):
        return (jnp.minimum(place[0] + i, total - 1), 0, 0)

    rows = pl.BlockSpec((1, length, width), local_block)
    return pl.pallas_call(
        functools.partial(back_near_kernel, blocks, inner // count),
        grid_spec=pltpu.PrefetchScalarGridSpec(
            num_scalar_prefetch=1,
            grid=(slots,),
            in_specs=[
                pl.BlockSpec((1, length, width), own),
                rows,
                rows,
                pl.BlockSpec((1, length, 3 * inner), local_block),
                pl.BlockSpec((1, length, inner), local_block),
            ]
            + [whole(p.shape) for p in packs]
            + [whole((1, width)), whole((8, width)), whole(controllers.shape)],
            out_specs=[rows] + [whole((height, LANES))] * count,
            scratch_shapes=[
                pltpu.VMEM((blocks, 4 * width, LANES), F32),
                pltpu.VMEM((8, width), F32),
            ],
        ),
        out_shape=[
            jax.ShapeDtypeStruct((slots, length, width), BF16),
        ]
        + [jax.ShapeDtypeStruct((height, LANES), BF16)] * count,
        compiler_params=params("arbitrary"),
        cost_estimate=pl.CostEstimate(
            flops=0,
            bytes_accessed=slots * length * (width * 12 + inner * 8) + 16 * width * inner,
            transcendentals=slots * length * length * inner // HEAD_WIDTH,
        ),
        name="attention_back_near",
    )(place, tokens, d_hidden, partial, joint, context, *packs, gain_attn, gain_in, controllers)


def swap_core(x):
    narrow = lax.axis_size("narrow")
    return lax.ppermute(x, "narrow", [(n, n ^ 1) for n in range(narrow)])


def from_chip(x, k):
    narrow = lax.axis_size("narrow")
    return lax.ppermute(x, "narrow", [((n + 2 * k) % narrow, n) for n in range(narrow)])


def to_chip(x, k):
    narrow = lax.axis_size("narrow")
    return lax.ppermute(x, "narrow", [(n, (n + 2 * k) % narrow) for n in range(narrow)])


def relative_narrow():
    narrow = lax.axis_size("narrow")
    me = lax.axis_index("narrow")
    return [lax.bitwise_xor(lax.rem(me + 2 * (j // 2), narrow), j % 2) for j in range(narrow)]


def gather_narrow(x):
    blocks = []
    for k in range(lax.axis_size("narrow") // 2):
        piece = from_chip(x, k) if k else x
        blocks += [piece, swap_core(piece)]
    return blocks


def far_sums(pieces):
    pairs = [(pieces[2 * k], swap_core(pieces[2 * k + 1])) for k in range(len(pieces) // 2)]
    return [(x.astype(F32) + y.astype(F32)).astype(BF16) for x, y in pairs]


def after(x, *others):
    return lax.optimization_barrier((x, others))[0]


def wide_parts(x):
    wide = lax.axis_size("wide")
    parts = x.astype(BF16).reshape(wide, x.shape[0] // wide, x.shape[1])
    parts = lax.all_to_all(parts, "wide", split_axis=0, concat_axis=0, tiled=True)
    return jnp.sum(parts.astype(F32), axis=0).astype(BF16)


def from_parts(part):
    parts = jnp.broadcast_to(part[None], (lax.axis_size("wide"),) + part.shape)
    parts = lax.all_to_all(parts, "wide", split_axis=0, concat_axis=0, tiled=True)
    return parts.reshape(-1, part.shape[-1]).astype(F32)


def to_relative(x, j):
    narrow = lax.axis_size("narrow")
    k, other = j // 2, j % 2
    return lax.ppermute(x, "narrow", [(n, ((n + 2 * k) % narrow) ^ other) for n in range(narrow)])


def from_relative(x, j):
    narrow = lax.axis_size("narrow")
    k, other = j // 2, j % 2
    return lax.ppermute(x, "narrow", [(((n + 2 * k) % narrow) ^ other, n) for n in range(narrow)])


def to_unit(x, d):
    wide = lax.axis_size("wide")
    return lax.ppermute(x, "wide", [(w, w ^ d) for w in range(wide)])


def place_kernel(count, where, *refs):
    pieces, out = refs[:count], refs[-1]
    for j, piece in enumerate(pieces):

        @pl.when(pl.program_id(0) == j)
        def _(piece=piece):
            out[...] = piece[...]


def place_blocks(pieces, where, total, *rest):
    count = len(pieces)
    shape = pieces[0].shape
    return pl.pallas_call(
        functools.partial(place_kernel, count),
        grid_spec=pltpu.PrefetchScalarGridSpec(
            num_scalar_prefetch=1,
            grid=(count,),
            in_specs=[whole(shape)] * count + [pl.BlockSpec(memory_space=pl.ANY)] * len(rest),
            out_specs=pl.BlockSpec(shape, lambda j, where: (where[j], 0, 0)),
        ),
        out_shape=jax.ShapeDtypeStruct((total * shape[0],) + shape[1:], pieces[0].dtype),
        input_output_aliases={1 + count: 0} if rest else {},
        compiler_params=params("arbitrary"),
        cost_estimate=pl.CostEstimate(
            flops=0, bytes_accessed=pieces[0].size * 4 * count, transcendentals=0
        ),
        name="place_blocks",
    )(where, *pieces, *rest)


def body(
    tokens,
    cotangent,
    counts,
    group_order,
    query_weight,
    key_weight,
    value_weight,
    output_weight,
    gain_attn,
    gain_mix,
    controller,
    w_in,
    b_in,
    w_out,
    b_out,
):
    slot_count, seq_len, model_width = tokens.shape
    wide, narrow = lax.axis_size("wide"), lax.axis_size("narrow")
    spread = wide * narrow
    wide_index, narrow_index = lax.axis_index("wide"), lax.axis_index("narrow")
    slots = -(-slot_count // narrow)
    part = seq_len // spread
    padded_part = -(-part // 8) * 8
    local_experts = w_in.shape[0]
    experts = local_experts * narrow
    relative = jnp.stack(relative_narrow())
    head_columns = query_weight.shape[1]

    seq_ends = jnp.cumsum(counts)
    seq_starts = seq_ends - counts
    own_count = counts[wide_index]
    place = jnp.stack([narrow_index * slots, own_count]).astype(jnp.int32)
    slot_ids = jnp.arange(slots * narrow)
    slot_seqs = jnp.where(slot_ids[None] < counts[:, None], seq_starts[:, None] + slot_ids[None], -1)
    matches = slot_seqs.reshape(-1, 1) == group_order[None]
    slot_group = jnp.sum(jnp.where(matches, 1 + jnp.arange(group_order.shape[0]) // GROUP, 0), axis=1) - 1
    positions = jnp.arange(padded_part)
    row_code = jnp.where(slot_group[:, None] >= 0, slot_group[:, None] * padded_part + positions, -1)
    row_code = row_code.reshape(-1, 1).astype(jnp.int32)
    per_expert = GROUPS * padded_part
    col_code = (jnp.arange(experts * per_expert) % per_expert).astype(jnp.int32)[None]
    tile = jnp.repeat(jnp.eye(experts, dtype=BF16), per_expert, axis=1)

    pack = pack_weights(query_weight, key_weight, value_weight, output_weight)
    packs = [pack, swap_core(pack)]
    far_packs = [from_chip(pack, k) for k in range(1, narrow // 2)]
    joined = LANES // head_columns

    def join(packs):
        if joined == 1:
            return packs
        packs = [p.reshape(model_width, 4, head_columns) for p in packs]
        return [
            jnp.concatenate(packs[i : i + joined], axis=2).reshape(model_width, -1)
            for i in range(0, len(packs), joined)
        ]

    controllers = jnp.stack(gather_narrow(controller.T))
    controllers = controllers[jnp.argsort(relative)].reshape(experts, model_width).T

    gain_attn_row, gain_mix_row = gain_attn[None], gain_mix[None]

    def to_positions(x):
        x = lax.all_to_all(x, BOTH, split_axis=0, concat_axis=0, tiled=True)
        x = jnp.pad(x, ((0, 0), (0, 0), (0, padded_part - part), (0, 0)))
        return x.reshape(-1, model_width)

    def to_slots(x):
        x = x.reshape(spread, 2, slots, padded_part, model_width)[:, :, :, :part]
        x = x.reshape(spread, 2, slots * part, model_width)
        return lax.all_to_all(x, BOTH, split_axis=0, concat_axis=0, tiled=True)

    cots, *packs = lax.optimization_barrier((cotangent, *packs))
    cots = jnp.pad(cots, ((0, slots * narrow - slot_count), (0, 0), (0, 0)))
    cots = cots.reshape(slots * narrow, wide, narrow, part, model_width)
    cots = lax.dynamic_index_in_dim(cots, narrow_index, axis=2, keepdims=False).transpose(1, 0, 2, 3)
    cots = lax.all_to_all(cots, "wide", split_axis=0, concat_axis=0, tiled=True)
    cots = jnp.pad(cots, ((0, 0), (0, 0), (0, padded_part - part), (0, 0)))
    cot_rows = cots.reshape(-1, model_width)

    packs = join(packs)
    partial, joint_near, context_near = attention_near(place, tokens, packs, gain_attn_row, slots)
    partial, far_packs = lax.optimization_barrier((partial, far_packs))
    far_packs = join([x for piece in far_packs for x in (piece, swap_core(piece))])
    mix_sent, hidden, joint_far, context_far = attention_far(
        place, tokens, partial, far_packs, gain_attn_row, gain_mix_row, slots, spread
    )
    mix_rows = to_positions(mix_sent)
    probs, spread_probs, *both = mix_forward(
        padded_part, relative, mix_rows, cot_rows, controllers, row_code, col_code, tile, narrow
    )

    rows = GROUPS * part

    def trim(x):
        x = x.reshape(local_experts, 2, GROUPS, padded_part, model_width)[:, :, :, :part]
        return x.reshape(local_experts, 2, rows, model_width)

    def untrim(x):
        x = x.reshape(local_experts, 2, GROUPS, part, model_width)
        x = jnp.pad(x, ((0, 0), (0, 0), (0, 0), (0, padded_part - part), (0, 0)))
        return x.reshape(local_experts, 2, -1, model_width)

    both = [trim(x) for x in both]
    both = both[:1] + [to_relative(x, j) for j, x in enumerate(both) if j]
    halves = 2 if wide % 4 == 0 else 1
    units = wide // halves
    held, share = max(local_experts // units, 1), max(units // local_experts, 1)
    unit = lax.rem(wide_index, units)
    shape = (held, 2, rows, model_width)
    if share == 1:
        tokens_sent = [x.reshape((units, 1) + shape) for x in both]
        tokens_sent = jnp.concatenate([jnp.concatenate([x] * halves) for x in tokens_sent], axis=1)
    else:
        tokens_sent = jnp.stack(both).reshape((share, narrow // share, units // share) + shape)
        tokens_sent = tokens_sent.transpose(2, 0, 1, 3, 4, 5, 6).reshape((units, narrow // share) + shape)
        tokens_sent = jnp.concatenate([tokens_sent] * halves)
    tokens_sent, both = lax.optimization_barrier((tokens_sent, both))
    tokens_all = lax.all_to_all(tokens_sent, "wide", split_axis=0, concat_axis=0, tiled=True)
    if rows % 16 == 0:
        back = experts_at_positions(both, w_in, b_in, w_out, b_out)
    else:
        lines = jnp.stack(both, axis=2).reshape(local_experts, 2, narrow * rows, model_width)
        (back,) = experts_at_positions([lines], w_in, b_in, w_out, b_out)
        back = back.reshape(local_experts, 2, narrow, rows, model_width)
        back = [back[:, :, j] for j in range(narrow)]

    where = jnp.stack([wide_index // units, unit]).astype(jnp.int32)
    first = (unit * held // share).astype(jnp.int32)
    expert_grads = [
        expert_weights(where, (first + p)[None], p, tokens_all, w_in, b_in, w_out, wide, units)
        for p in range(held)
    ]

    back = [untrim(x if j == 0 else from_relative(x, j)) for j, x in enumerate(back)]
    slot_rows, grad_controller = mix_backward(
        padded_part,
        relative,
        spread_probs,
        mix_rows,
        cot_rows,
        probs,
        back,
        controllers,
        row_code,
        col_code,
        tile,
        spread,
    )
    slot_rows = to_slots(slot_rows)
    expert_grads = [[x[0]] + [to_unit(x[d], d) for d in range(1, units)] for x in expert_grads]
    slot_rows = after(slot_rows, expert_grads[0][:-1], [x[0] for x in expert_grads])

    height = 4 * model_width
    grad_controller = grad_controller.astype(BF16).reshape(narrow, -1, LANES)[relative]
    end = height + grad_controller.shape[1]
    rows_sent = -(-(end + 16) // (16 * wide)) * 16 * wide
    partial, d_hidden, mixed_part, gain_mix_part, *far = attention_back_far(
        place,
        tokens,
        cotangent,
        slot_rows,
        hidden,
        joint_far,
        context_far,
        far_packs,
        gain_attn_row,
        gain_mix_row,
        grad_controller[2:],
        rows_sent,
    )
    early = [x[1:-1] for x in expert_grads[1:]]
    far, early = lax.optimization_barrier((far, early))
    for x, pieces in zip(expert_grads[1:], early):
        x[1:-1] = pieces
    partial, far = lax.optimization_barrier((partial, far_sums(far)))
    far = sum([to_chip(x, k + 1).astype(F32) for k, x in enumerate(far)], 0.0)
    d_tokens, kept, sent = attention_back_near(
        place,
        tokens,
        d_hidden,
        partial,
        joint_near,
        context_near,
        packs,
        gain_attn_row,
        gain_mix_part,
        grad_controller[:2],
        rows_sent,
    )
    d_tokens, kept, sent, far, expert_grads[0][-1] = lax.optimization_barrier(
        (d_tokens, kept, sent, far, expert_grads[0][-1])
    )
    weights = kept.astype(F32) + swap_core(sent).astype(F32) + far
    part_sums = wide_parts(weights)

    far_tokens = [from_chip(d_tokens, k) for k in range(1, narrow // 2)]
    swapped = [swap_core(d_tokens), swap_core(mixed_part)]
    order = lax.bitwise_xor(unit, jnp.arange(units)) * held
    order = order[None] + jnp.arange(held)[:, None]
    order = jnp.concatenate([order[:, :-1].reshape(-1), order[:, -1]])
    pieces = [piece for x in expert_grads for piece in x[:-1]] + [x[-1] for x in expert_grads]
    owned = owned_weights(pieces[:-1], order[:-1], units * held, w_in.shape[2], wide)
    mixed_part, far_tokens, swapped, owned, pieces[-1] = lax.optimization_barrier(
        (mixed_part, far_tokens, swapped, owned, pieces[-1])
    )
    far_mixed = [from_chip(mixed_part, k) for k in range(1, narrow // 2)]
    far_tokens = [y for x in far_tokens for y in (x, swap_core(x))]
    part_sums, far_tokens = lax.optimization_barrier((part_sums, far_tokens))
    d_tokens = place_blocks([d_tokens, swapped[0]] + far_tokens, relative, narrow)
    g_w_in, g_w_out, bias = owned_weights(after(pieces[-1:], part_sums), order[-1:], units * held, w_in.shape[2], wide, owned)
    far_mixed, d_tokens, bias = lax.optimization_barrier((far_mixed, d_tokens, bias))
    far_mixed = [y for x in far_mixed for y in (x, swap_core(x))]
    mixed_part = place_blocks([mixed_part, swapped[1]] + far_mixed, relative, narrow)
    d_tokens, mixed_part = d_tokens[:slot_count], mixed_part[:slot_count]
    weights = from_parts(part_sums)
    gains = weights[end : end + 16].astype(BF16)
    gains = sum([to_chip(gains, k).astype(F32) for k in range(1, narrow // 2)], gains.astype(F32))
    projections = weights[: 3 * model_width, :head_columns].reshape(3, model_width, head_columns)
    output_weight_gradient = weights[3 * model_width : height].reshape(-1, LANES, LANES)[:, :head_columns]
    output_weight_gradient = output_weight_gradient.transpose(1, 0, 2).reshape(head_columns, -1)
    g_controller = weights[height:end].reshape(local_experts, model_width).T
    lines = model_width // LANES
    g_gain_attn = gains[:lines].reshape(-1)
    g_gain_mix = gains[lines : 2 * lines].reshape(-1)

    def over_share(x):
        return jnp.sum(x.reshape((local_experts, share) + x.shape[1:]), axis=1)

    g_w_in, g_w_out, bias = (over_share(x) for x in (g_w_in, g_w_out, bias))
    g_b_in = bias[:, : w_in.shape[2] // model_width].reshape(local_experts, -1)
    g_b_out = bias[:, -1]

    return (
        mixed_part,
        d_tokens,
        projections[0],
        projections[1],
        projections[2],
        output_weight_gradient,
        g_gain_attn,
        g_gain_mix,
        g_controller,
        g_w_in,
        g_b_in,
        g_w_out,
        g_b_out,
    )


def solution(mesh):
    placed = (
        P("wide", None, None),
        P("wide", None, None),
        P(),
        P(),
        P(None, "narrow"),
        P(None, "narrow"),
        P(None, "narrow"),
        P("narrow", None),
        P(),
        P(),
        P(None, "narrow"),
        P("narrow", None, None),
        P("narrow", None),
        P("narrow", None, None),
        P("narrow", None),
    )
    return jax.shard_map(
        body,
        mesh=mesh,
        in_specs=placed,
        out_specs=(
            P("wide", None, None),
            P("wide", None, None),
            P(None, "narrow"),
            P(None, "narrow"),
            P(None, "narrow"),
            P("narrow", None),
            P(),
            P(),
            P(None, "narrow"),
            P("narrow", "wide", None),
            P("narrow", None),
            P("narrow", "wide", None),
            P("narrow", None),
        ),
        check_vma=False,
    )
```

```python
import functools

import jax
import jax.numpy as jnp
from jax import lax
from jax.experimental import pallas as pl
from jax.experimental.pallas import tpu as pltpu
from jax.sharding import PartitionSpec as P

HEAD_WIDTH = 64
GROUP = 32
GROUPS = 2
LANES = 128

EPSILON = 1e-05
NEGATIVE = -1e30
BOTH = ("wide", "narrow")
F32 = jnp.float32
BF16 = jnp.bfloat16
VMEM_LIMIT = 56 * 1024 * 1024


def mm(a, b):
    return lax.dot_general(a, b, (((1,), (0,)), ((), ())), preferred_element_type=F32)


def mm_nt(a, b):
    return lax.dot_general(a, b, (((1,), (1,)), ((), ())), preferred_element_type=F32)


def mm_tn(a, b):
    return lax.dot_general(a, b, (((0,), (0,)), ((), ())), preferred_element_type=F32)


def params(*semantics):
    return pltpu.CompilerParams(dimension_semantics=semantics or None, vmem_limit_bytes=VMEM_LIMIT)


def whole(shape):
    zeros = (0,) * len(shape)
    return pl.BlockSpec(tuple(shape), lambda *_: zeros)


def head_masks(shape, axis):
    lane = lax.broadcasted_iota(jnp.int32, shape, axis)
    return [(lane >= h * HEAD_WIDTH) & (lane < (h + 1) * HEAD_WIDTH) for h in range(LANES // HEAD_WIDTH)]


def masks_of(length):
    return list(zip(head_masks((length, LANES), 1), head_masks((LANES, length), 0)))


def keep(mask, rows):
    return jnp.where(mask, rows, jnp.zeros_like(rows))


def causal_probs(query_head, keys, causal):
    scores = mm_nt(keys, query_head) * (float(HEAD_WIDTH) ** -0.5)
    scores = jnp.where(causal, scores, NEGATIVE)
    powers = jnp.exp(scores - jnp.max(scores, axis=0, keepdims=True))
    return powers * (1.0 / jnp.sum(powers, axis=0, keepdims=True))


def causal_mask(length):
    return lax.broadcasted_iota(jnp.int32, (length, length), 0) <= lax.broadcasted_iota(
        jnp.int32, (length, length), 1
    )


def inverse_rms(rows):
    return lax.rsqrt(jnp.mean(rows * rows, axis=-1, keepdims=True) + EPSILON)


def attend(entry, packs, causal, masks, joint_out, context_out):
    attention = None
    for j, pack in enumerate(packs):
        joint = mm(entry, pack[:, : 3 * LANES]).astype(BF16)
        joint_out[0, :, j * 3 * LANES : (j + 1) * 3 * LANES] = joint
        q, k, v = (joint[:, i * LANES : (i + 1) * LANES] for i in range(3))
        turned, context = v.T, None
        for mask, across in masks:
            probs = causal_probs(keep(mask, q), k, causal)
            term = mm(keep(across, turned), probs.astype(BF16))
            context = term if context is None else context + term
        context = context.astype(BF16).T
        context_out[0, :, j * LANES : (j + 1) * LANES] = context
        term = mm_nt(context, pack[:, 3 * LANES :])
        attention = term if attention is None else attention + term
    return attention


def near_kernel(blocks, place, tokens, *refs):
    packs, (gain_attn, partial_out, joint_out, context_out) = refs[:blocks], refs[blocks:]
    rows = tokens[0].astype(F32)
    entry = (rows * inverse_rms(rows) * gain_attn[...]).astype(BF16)
    length = rows.shape[0]
    partial_out[0] = rows + attend(
        entry, packs, causal_mask(length), masks_of(length), joint_out, context_out
    )


def far_kernel(blocks, place, tokens, partial, *refs):
    packs = refs[:blocks]
    gain_attn, gain_mix, mix_out, hidden_out, joint_out, context_out = refs[blocks:]
    rows = tokens[0].astype(F32)
    entry = (rows * inverse_rms(rows) * gain_attn[...]).astype(BF16)
    length = rows.shape[0]
    hidden = partial[0] + attend(
        entry, packs, causal_mask(length), masks_of(length), joint_out, context_out
    )
    mixed = hidden * inverse_rms(hidden) * gain_mix[...]
    mix_out[...] = mixed.reshape(mix_out.shape).astype(BF16)
    hidden_out[0] = hidden


def local_block(i, place):
    return (i, 0, 0)


def attention_near(place, tokens, packs, gain_attn, slots):
    total, length, width = tokens.shape
    inner = len(packs) * LANES
    return pl.pallas_call(
        functools.partial(near_kernel, len(packs)),
        grid_spec=pltpu.PrefetchScalarGridSpec(
            num_scalar_prefetch=1,
            grid=(slots,),
            in_specs=[
                pl.BlockSpec((1, length, width), lambda i, place: (jnp.minimum(place[0] + i, total - 1), 0, 0))
            ]
            + [whole(p.shape) for p in packs]
            + [whole((1, width))],
            out_specs=[
                pl.BlockSpec((1, length, width), local_block),
                pl.BlockSpec((1, length, 3 * inner), local_block),
                pl.BlockSpec((1, length, inner), local_block),
            ],
        ),
        out_shape=[
            jax.ShapeDtypeStruct((slots, length, width), F32),
            jax.ShapeDtypeStruct((slots, length, 3 * inner), BF16),
            jax.ShapeDtypeStruct((slots, length, inner), BF16),
        ],
        compiler_params=params("arbitrary"),
        cost_estimate=pl.CostEstimate(
            flops=slots * 2 * length * (4 * width * inner + 4 * length * inner),
            bytes_accessed=slots * length * (width * 6 + inner * 8) + 8 * width * inner,
            transcendentals=slots * length * length * inner // HEAD_WIDTH,
        ),
        name="attention_near",
    )(place, tokens, *packs, gain_attn)


def attention_far(place, tokens, partial, packs, gain_attn, gain_mix, slots, spread):
    total, length, width = tokens.shape
    inner = len(packs) * LANES
    part = length // spread
    return pl.pallas_call(
        functools.partial(far_kernel, len(packs)),
        grid_spec=pltpu.PrefetchScalarGridSpec(
            num_scalar_prefetch=1,
            grid=(slots,),
            in_specs=[
                pl.BlockSpec((1, length, width), lambda i, place: (jnp.minimum(place[0] + i, total - 1), 0, 0)),
                pl.BlockSpec((1, length, width), local_block),
            ]
            + [whole(p.shape) for p in packs]
            + [whole((1, width))] * 2,
            out_specs=[
                pl.BlockSpec((spread, 1, part, width), lambda i, place: (0, i, 0, 0)),
                pl.BlockSpec((1, length, width), local_block),
                pl.BlockSpec((1, length, 3 * inner), local_block),
                pl.BlockSpec((1, length, inner), local_block),
            ],
        ),
        out_shape=[
            jax.ShapeDtypeStruct((spread, slots, part, width), BF16),
            jax.ShapeDtypeStruct((slots, length, width), F32),
            jax.ShapeDtypeStruct((slots, length, 3 * inner), BF16),
            jax.ShapeDtypeStruct((slots, length, inner), BF16),
        ],
        compiler_params=params("arbitrary"),
        cost_estimate=pl.CostEstimate(
            flops=slots * 2 * length * (4 * width * inner + 4 * length * inner),
            bytes_accessed=slots * length * (width * 12 + inner * 8) + 8 * width * inner,
            transcendentals=slots * length * length * inner // HEAD_WIDTH,
        ),
        name="attention_far",
    )(place, tokens, partial, *packs, gain_attn, gain_mix)


def pack_kernel(query, key, value, output, out):
    width = query.shape[1]
    for i, ref in enumerate((query, key, value)):
        out[:, i * width : (i + 1) * width] = ref[...]
    out[:, 3 * width :] = output[...].T


def pack_weights(query, key, value, output):
    width, columns = query.shape
    if columns % LANES:
        return jnp.concatenate([query, key, value, output.T], axis=1)
    return pl.pallas_call(
        pack_kernel,
        out_shape=jax.ShapeDtypeStruct((width, 4 * columns), BF16),
        compiler_params=params(),
        cost_estimate=pl.CostEstimate(flops=0, bytes_accessed=16 * width * columns, transcendentals=0),
        name="pack_weights",
    )(query, key, value, output)


def slot_softmax(logits, codes, part):
    experts = logits.shape[1]
    logits = logits.reshape(-1, part, experts)
    codes = jnp.broadcast_to(codes, (codes.shape[0], experts)).reshape(-1, part, experts)
    total = jnp.zeros_like(logits)
    for g in range(GROUPS):
        inside = (codes >= g * part) & (codes < (g + 1) * part)
        held = jnp.where(inside, logits, NEGATIVE)
        powers = jnp.where(inside, jnp.exp(held - jnp.max(held, axis=0, keepdims=True)), 0.0)
        total = total + powers / jnp.sum(powers, axis=0, keepdims=True)
    return total.reshape(-1, experts)


def group_totals(terms, codes, part):
    experts = terms.shape[1]
    terms = terms.reshape(-1, part, experts)
    codes = jnp.broadcast_to(codes, (codes.shape[0], experts)).reshape(-1, part, experts)
    total = jnp.zeros_like(terms)
    for g in range(GROUPS):
        inside = (codes >= g * part) & (codes < (g + 1) * part)
        total = jnp.where(inside, jnp.sum(jnp.where(inside, terms, 0.0), axis=0, keepdims=True), total)
    return total.reshape(-1, experts)


def mix_kernel(part, relative, rows, cots, controller, row_code, col_code, tile, probs_out, spread_out, *refs):
    sent, (merged, grads) = refs[:-2], refs[-2:]
    held = rows[...]
    probs = slot_softmax(mm(held, controller[...]), row_code[...], part)
    probs_out[...] = probs
    wide = mm(probs.astype(BF16), tile[...])
    spread = jnp.where(row_code[...] == col_code[...], wide, 0.0).astype(BF16)
    spread_out[...] = spread
    count, _, lines, _ = sent[0].shape
    merged[...] = mm_tn(spread, held).astype(BF16)
    grads[...] = mm_tn(spread, cots[...]).astype(BF16)
    for j, out in enumerate(sent):
        for e in range(count):
            at = pl.ds(pl.multiple_of((relative[j] * count + e) * lines, lines), lines)
            out[e, 0] = merged[at]
            out[e, 1] = grads[at]


def mix_forward(part, relative, rows, cots, controller, row_code, col_code, tile, narrow):
    count, width = rows.shape
    experts, columns = tile.shape
    sent = (experts // narrow, 2, columns // experts, width)
    return pl.pallas_call(
        functools.partial(mix_kernel, part),
        grid_spec=pltpu.PrefetchScalarGridSpec(
            num_scalar_prefetch=1,
            grid=(1,),
            in_specs=[whole(x.shape) for x in (rows, cots, controller, row_code, col_code, tile)],
            out_specs=[whole((count, experts)), whole((count, columns))]
            + [whole(sent)] * narrow,
            scratch_shapes=[pltpu.VMEM((columns, width), BF16)] * 2,
        ),
        out_shape=[
            jax.ShapeDtypeStruct((count, experts), F32),
            jax.ShapeDtypeStruct((count, columns), BF16),
        ]
        + [jax.ShapeDtypeStruct(sent, BF16)] * narrow,
        compiler_params=params("arbitrary"),
        cost_estimate=pl.CostEstimate(
            flops=4 * count * columns * width,
            bytes_accessed=6 * count * width * 2,
            transcendentals=count * experts * 2,
        ),
        name="mix_forward",
    )(relative, rows, cots, controller, row_code, col_code, tile)


def unmix_kernel(
    part, narrow, relative, spread, rows, cots, probs, controller, row_code, col_code, tile, *refs
):
    back, (sent, gain_out, outs, grads) = refs[:narrow], refs[narrow:]
    count, _, lines, _ = back[0].shape
    for j, piece in enumerate(back):
        for e in range(count):
            at = pl.ds(pl.multiple_of((relative[j] * count + e) * lines, lines), lines)
            outs[at] = piece[e, 0]
            grads[at] = piece[e, 1]
    held = rows[...]
    pairs = (mm_nt(cots[...], outs[...]) + mm_nt(held, grads[...])).astype(BF16)
    pairs = jnp.where(row_code[...] == col_code[...], pairs, jnp.zeros_like(pairs))
    d_weights = mm_nt(pairs, tile[...])
    p = probs[...]
    d_logits = (p * (d_weights - group_totals(p * d_weights, row_code[...], part))).astype(BF16)
    shape = (sent.shape[0],) + sent.shape[2:]
    grad = mm(spread[...], grads[...]) + mm_nt(d_logits, controller[...])
    sent[:, 0] = grad.reshape(shape).astype(BF16)
    sent[:, 1] = mm(spread[...], outs[...]).reshape(shape).astype(BF16)
    gain_out[...] = mm_tn(d_logits, held)


def mix_backward(part, relative, spread, rows, cots, probs, back, controller, row_code, col_code, tile, devices):
    count, width = rows.shape
    experts, columns = tile.shape
    operands = (spread, rows, cots, probs, controller, row_code, col_code, tile) + tuple(back)
    outs = [
        jax.ShapeDtypeStruct((devices, 2, count // devices, width), BF16),
        jax.ShapeDtypeStruct((experts, width), F32),
    ]
    return pl.pallas_call(
        functools.partial(unmix_kernel, part, len(back)),
        grid_spec=pltpu.PrefetchScalarGridSpec(
            num_scalar_prefetch=1,
            grid=(1,),
            in_specs=[whole(x.shape) for x in operands],
            out_specs=[whole(x.shape) for x in outs],
            scratch_shapes=[pltpu.VMEM((columns, width), BF16)] * 2,
        ),
        out_shape=outs,
        compiler_params=params("arbitrary"),
        cost_estimate=pl.CostEstimate(
            flops=8 * count * columns * width,
            bytes_accessed=8 * count * width * 2,
            transcendentals=0,
        ),
        name="mix_backward",
    )(relative, *operands)


GELU_SLOPE = 0.7978845608028654
GELU_CUBE = 0.044715


def gelu_pair(x):
    square = x * x
    bend = jnp.tanh(GELU_SLOPE * x * (1.0 + GELU_CUBE * square))
    gate = 0.5 * (1.0 + bend)
    slope = gate + 0.5 * x * (1.0 - bend * bend) * (GELU_SLOPE * (1.0 + 3.0 * GELU_CUBE * square))
    return x * gate, slope


def expert_kernel(count, *refs):
    both, (w_in, b_in, w_out, b_out), sent = refs[:count], refs[count : count + 4], refs[count + 4 :]
    rows = both[0].shape[2]
    merged = jnp.concatenate([x[0, 0] for x in both], axis=0)
    grads = jnp.concatenate([x[0, 1] for x in both], axis=0)
    act, slope = gelu_pair(mm(merged, w_in[0]) + b_in[0])
    outs = mm(act.astype(BF16), w_out[0]) + b_out[0]
    d_pre = (mm_nt(grads, w_out[0]) * slope).astype(BF16)
    d_merged = mm_nt(d_pre, w_in[0])
    for j, out in enumerate(sent):
        at = slice(j * rows, (j + 1) * rows)
        out[0, 0] = outs[at].astype(BF16)
        out[0, 1] = d_merged[at].astype(BF16)


def experts_at_positions(both, w_in, b_in, w_out, b_out):
    experts, _, rows, width = both[0].shape
    inner = w_in.shape[2]
    sources, count = len(both), experts * rows
    tokens = pl.BlockSpec((1, 2, rows, width), lambda e: (e, 0, 0, 0))
    return pl.pallas_call(
        functools.partial(expert_kernel, sources),
        grid=(experts,),
        in_specs=[tokens] * sources
        + [
            pl.BlockSpec((1, width, inner), lambda e: (e, 0, 0)),
            pl.BlockSpec((1, 1, inner), lambda e: (e, 0, 0)),
            pl.BlockSpec((1, inner, width), lambda e: (e, 0, 0)),
            pl.BlockSpec((1, 1, width), lambda e: (e, 0, 0)),
        ],
        out_specs=[tokens] * sources,
        out_shape=[jax.ShapeDtypeStruct(x.shape, BF16) for x in both],
        compiler_params=params("arbitrary"),
        cost_estimate=pl.CostEstimate(
            flops=8 * sources * count * width * inner,
            bytes_accessed=4 * experts * width * inner + 4 * sources * count * width * 2,
            transcendentals=sources * count * inner,
        ),
        name="experts",
    )(*both, w_in, b_in[:, None], w_out, b_out[:, None])


def weight_kernel(units, where, both, w_in, b_in, w_out, *refs):
    outs, (merged, grads, turned, total) = refs[:units], refs[units:]
    i, half, unit = pl.program_id(0), where[0], where[1]
    steps = pl.num_programs(0)
    width = both.shape[-1]
    span = turned.shape[0]
    rows = span // units
    height = outs[0].shape[0]
    block = height - 16 - steps * rows
    slices = width // block

    @pl.when(i == 0)
    def _():
        merged[...] = both[:, :, 0, 0].reshape(merged.shape)
        grads[...] = both[:, :, 0, 1].reshape(grads.shape)
        turned[...] = merged[:, pl.ds(pl.multiple_of(half * span, span), span)].T
        sums = jnp.sum(grads[...].astype(F32), axis=0, keepdims=True).astype(BF16)
        for out in outs:
            out[height - 16 :] = jnp.zeros((16, width), BF16)
            out[height - 1 :] = sums

    act, slope = gelu_pair(mm(merged[...], w_in[0]) + b_in[0])
    d_pre = (mm_nt(grads[...], w_out[0]) * slope).astype(BF16)
    bias = jnp.sum(d_pre.astype(F32), axis=0, keepdims=True).astype(BF16)
    total[...] = mm(turned[...], d_pre)
    base = pl.ds(pl.multiple_of(i * rows, rows), rows)
    for d, out in enumerate(outs):
        own = pl.ds(pl.multiple_of(lax.bitwise_xor(unit, d) * rows, rows), rows)
        out[base] = total[own].astype(BF16)
    for step in range(steps):

        @pl.when(i == step)
        def _(step=step):
            for out in outs:
                out[height - 16 + step : height - 15 + step] = bias

    @pl.when(i // (steps // 2) == half)
    def _():
        grad = mm_tn(act.astype(BF16), grads[...]).astype(BF16)
        first = (i - half * (steps // 2)) * slices
        for s in range(slices):
            for d, out in enumerate(outs):

                @pl.when(first + s == lax.bitwise_xor(unit, d))
                def _(s=s, out=out):
                    out[height - 16 - block : height - 16] = grad[s * block : (s + 1) * block]


def expert_weights(where, expert, p, both, w_in, b_in, w_out, wide, units):
    sources, inner_sources, _, _, rows, width = both.shape
    inner = w_in.shape[2]
    count = sources * inner_sources * rows
    span = width * units // wide
    height = inner // width * (width // wide) + inner // wide + 16
    return pl.pallas_call(
        lambda where, expert, *refs: weight_kernel(units, where, *refs),
        grid_spec=pltpu.PrefetchScalarGridSpec(
            num_scalar_prefetch=2,
            grid=(inner // width,),
            in_specs=[
                pl.BlockSpec(
                    (sources, inner_sources, 1, 2, rows, width), lambda i, w, e: (0, 0, p, 0, 0, 0)
                ),
                pl.BlockSpec((1, width, width), lambda i, w, e: (e[0], 0, i)),
                pl.BlockSpec((1, 1, width), lambda i, w, e: (e[0], 0, i)),
                pl.BlockSpec((1, width, width), lambda i, w, e: (e[0], i, 0)),
            ],
            out_specs=[whole((height, width))] * units,
            scratch_shapes=[pltpu.VMEM((count, width), BF16)] * 2
            + [pltpu.VMEM((span, count), BF16), pltpu.VMEM((span, width), F32)],
        ),
        out_shape=[jax.ShapeDtypeStruct((height, width), BF16)] * units,
        compiler_params=params("arbitrary"),
        cost_estimate=pl.CostEstimate(
            flops=6 * count * width * inner,
            bytes_accessed=8 * width * inner + 4 * count * width,
            transcendentals=count * inner,
        ),
        name="expert_weights",
    )(where, expert, both, w_in, b_in[:, None], w_out)


def owner_kernel(count, where, *refs):
    pieces, (g_in, g_out, bias) = refs[:count], refs[-3:]
    rows, block = g_in.shape[1], g_out.shape[1]
    width = g_out.shape[2]
    start = pieces[0].shape[0] - 16 - block
    for j, piece in enumerate(pieces):

        @pl.when(pl.program_id(0) == j)
        def _(piece=piece):
            for c in range(g_in.shape[2] // width):
                g_in[0, :, c * width : (c + 1) * width] = piece[c * rows : (c + 1) * rows].astype(F32)
            g_out[0] = piece[start : start + block].astype(F32)
            bias[0] = piece[start + block :].astype(F32)


def owned_weights(pieces, where, total, inner, wide, rest=()):
    count = len(pieces)
    width = pieces[0].shape[1]
    shapes = [(1, width // wide, inner), (1, inner // wide, width), (1, 16, width)]
    return pl.pallas_call(
        functools.partial(owner_kernel, count),
        grid_spec=pltpu.PrefetchScalarGridSpec(
            num_scalar_prefetch=1,
            grid=(count,),
            in_specs=[whole(x.shape) for x in pieces] + [pl.BlockSpec(memory_space=pl.ANY)] * len(rest),
            out_specs=[pl.BlockSpec(x, lambda j, where: (where[j], 0, 0)) for x in shapes],
        ),
        out_shape=[jax.ShapeDtypeStruct((total,) + x[1:], F32) for x in shapes],
        input_output_aliases={1 + count + i: i for i in range(len(rest))},
        compiler_params=params("arbitrary"),
        cost_estimate=pl.CostEstimate(
            flops=0, bytes_accessed=sum(x.size for x in pieces) * 6, transcendentals=0
        ),
        name="owned_weights",
    )(where, *pieces, *rest)


def attend_back(i, entry, d_low, packs, joint_in, context_in, causal, masks, held):
    length = entry.shape[0]
    lines = pl.ds(pl.multiple_of(i * length, length), length)
    for ref, rows in zip(held, (entry, d_low, None, context_in[0])):
        if rows is not None:
            ref[lines] = rows
    scale = float(HEAD_WIDTH) ** -0.5
    d_entry = None
    for j, pack in enumerate(packs):
        base = j * 3 * LANES
        q, k, v = (joint_in[0, :, base + i * LANES : base + (i + 1) * LANES] for i in range(3))
        d_context = mm(d_low, pack[:, 3 * LANES :]).astype(BF16)
        d_q, d_k, d_v = [], [], []
        turned = k.T
        for mask, across in masks:
            q_head = keep(mask, q)
            d_head = keep(mask, d_context)
            probs = causal_probs(q_head, k, causal)
            d_probs = mm_nt(v, d_head).astype(BF16).astype(F32)
            d_scores = probs * (d_probs - jnp.sum(probs * d_probs, axis=0, keepdims=True))
            d_scores = d_scores.astype(BF16)
            d_v.append(mm(probs.astype(BF16), d_head))
            d_q.append(mm(keep(across, turned), d_scores))
            d_k.append(mm(d_scores, q_head))
        joint = [(sum(d_q) * scale).astype(BF16).T, (sum(d_k) * scale).astype(BF16), sum(d_v).astype(BF16)]
        joint = jnp.concatenate(joint, axis=1)
        term = mm_nt(joint, pack[:, : 3 * LANES])
        d_entry = term if d_entry is None else d_entry + term
        held[2][lines, base : base + 3 * LANES] = joint
    return d_entry


def store_weights(held, controllers, outs, lanes, gains=None):
    entry, d_low, joint, context = held
    width = entry.shape[1]
    for o, out in enumerate(outs):
        j, at = divmod(o, LANES // lanes)
        own = slice(at * lanes, (at + 1) * lanes)
        grad = mm_tn(entry[...], joint[:, j * 3 * LANES : (j + 1) * 3 * LANES]).astype(BF16)
        for c in range(3):
            piece = grad[:, c * LANES : (c + 1) * LANES]
            if lanes < LANES:
                piece = jnp.pad(piece[:, own], ((0, 0), (0, LANES - lanes)))
            out[c * width : (c + 1) * width] = piece
        grad = mm_tn(context[:, j * LANES : (j + 1) * LANES], d_low[...]).astype(BF16)
        for c in range(width // LANES):
            piece = grad[:, c * LANES : (c + 1) * LANES]
            if lanes < LANES:
                piece = jnp.pad(piece[own], ((0, LANES - lanes), (0, 0)))
            out[3 * width + c * LANES : 3 * width + (c + 1) * LANES] = piece
        tail = [controllers[o]]
        if gains is not None:
            tail.append(gains)
        left = out.shape[0] - 4 * width - sum(x.shape[0] for x in tail)
        out[4 * width :] = jnp.concatenate(tail + [jnp.zeros((left, LANES), BF16)], axis=0)


def held_rows(slots, length, width, inner):
    return [pltpu.VMEM((slots * length, columns), BF16) for columns in (width, width, 3 * inner, inner)]


def back_far_kernel(blocks, lanes, place, tokens, cots, grads, mixed, hidden, joint, context, *refs):
    packs, (gain_attn, gain_mix, controllers), refs = refs[:blocks], refs[blocks : blocks + 3], refs[blocks + 3 :]
    (partial_out, d_hidden_out, mixed_out, gain_out), outs, held = refs[:4], refs[4:-4], refs[-4:]
    i = pl.program_id(0)
    length, width = hidden.shape[1:]
    live = (place[0] + i < place[1]).astype(F32)

    @pl.when(i == 0)
    def _():
        gain_out[...] = jnp.zeros_like(gain_out)

    rows = hidden[0]
    inverse = inverse_rms(rows)
    normed = rows * inverse
    grad = grads[...].astype(F32).reshape(length, width)
    gain_out[0:1] += jnp.sum(grad * normed, axis=0, keepdims=True)
    d_normed = grad * gain_mix[...]
    d_hidden = cots[0].astype(F32) * live + inverse * (
        d_normed - normed * jnp.mean(d_normed * normed, axis=-1, keepdims=True)
    )
    d_hidden_out[0] = d_hidden
    mixed_out[0] = (live * (hidden[0] + mixed[...].astype(F32).reshape(length, width))).astype(BF16)
    rows = tokens[0].astype(F32)
    entry = (rows * inverse_rms(rows) * gain_attn[...]).astype(BF16)
    partial_out[0] = attend_back(
        i, entry, d_hidden.astype(BF16), packs, joint, context, causal_mask(length), masks_of(length), held
    )

    @pl.when(i == pl.num_programs(0) - 1)
    def _():
        store_weights(held, controllers, outs, lanes)


def back_near_kernel(blocks, lanes, place, tokens, d_hidden, partial, joint, context, *refs):
    packs, (gain_attn, gain_in, controllers), refs = refs[:blocks], refs[blocks : blocks + 3], refs[blocks + 3 :]
    d_tokens_out, outs, held, gain = refs[0], refs[1:-5], refs[-5:-1], refs[-1]
    i = pl.program_id(0)
    length, width = d_hidden.shape[1:]

    @pl.when(i == 0)
    def _():
        gain[...] = jnp.zeros_like(gain)

    rows = tokens[0].astype(F32)
    inverse = inverse_rms(rows)
    normed = rows * inverse
    entry = (normed * gain_attn[...]).astype(BF16)
    d_entry = partial[0] + attend_back(
        i, entry, d_hidden[0].astype(BF16), packs, joint, context, causal_mask(length), masks_of(length), held
    )
    d_entry = d_entry.astype(BF16).astype(F32)
    gain[0:1] += jnp.sum(d_entry * normed, axis=0, keepdims=True)
    d_normed = d_entry * gain_attn[...]
    d_tokens = d_hidden[0] + inverse * (
        d_normed - normed * jnp.mean(d_normed * normed, axis=-1, keepdims=True)
    )
    live = (place[0] + i < place[1]).astype(F32)
    d_tokens_out[0] = (d_tokens * live).astype(BF16)

    @pl.when(i == pl.num_programs(0) - 1)
    def _():
        pieces = width // LANES
        tail = [x[0:1, c * LANES : (c + 1) * LANES] for x in (gain, gain_in) for c in range(pieces)]
        tail.append(jnp.zeros((16 - 2 * pieces, LANES), F32))
        store_weights(held, controllers, outs, lanes, jnp.concatenate(tail, axis=0).astype(BF16))


def attention_back_far(
    place, tokens, cotangent, back, hidden, joint, context, packs, gain_attn, gain_mix, controllers, height
):
    total, length, width = tokens.shape
    slots = hidden.shape[0]
    spread, part = back.shape[0], back.shape[2] // slots
    inner = context.shape[2]
    blocks = len(packs)
    count = controllers.shape[0]

    def own(i, place):
        return (jnp.minimum(place[0] + i, total - 1), 0, 0)

    rows = pl.BlockSpec((1, length, width), local_block)
    return pl.pallas_call(
        functools.partial(back_far_kernel, blocks, inner // count),
        grid_spec=pltpu.PrefetchScalarGridSpec(
            num_scalar_prefetch=1,
            grid=(slots,),
            in_specs=[
                pl.BlockSpec((1, length, width), own),
                pl.BlockSpec((1, length, width), own),
                pl.BlockSpec((spread, 1, part, width), lambda i, place: (0, 0, i, 0)),
                pl.BlockSpec((spread, 1, part, width), lambda i, place: (0, 1, i, 0)),
                rows,
                pl.BlockSpec((1, length, 3 * inner), local_block),
                pl.BlockSpec((1, length, inner), local_block),
            ]
            + [whole(p.shape) for p in packs]
            + [whole((1, width))] * 2
            + [whole(controllers.shape)],
            out_specs=[rows, rows, rows, whole((8, width))] + [whole((height, LANES))] * count,
            scratch_shapes=held_rows(slots, length, width, inner),
        ),
        out_shape=[
            jax.ShapeDtypeStruct((slots, length, width), F32),
            jax.ShapeDtypeStruct((slots, length, width), F32),
            jax.ShapeDtypeStruct((slots, length, width), BF16),
            jax.ShapeDtypeStruct((8, width), F32),
        ]
        + [jax.ShapeDtypeStruct((height, LANES), BF16)] * count,
        compiler_params=params("arbitrary"),
        cost_estimate=pl.CostEstimate(
            flops=0,
            bytes_accessed=slots * length * (width * 18 + inner * 8) + 16 * width * inner,
            transcendentals=slots * length * length * inner // HEAD_WIDTH,
        ),
        name="attention_back_far",
    )(place, tokens, cotangent, back, back, hidden, joint, context, *packs, gain_attn, gain_mix, controllers)


def attention_back_near(
    place, tokens, d_hidden, partial, joint, context, packs, gain_attn, gain_in, controllers, height
):
    total, length, width = tokens.shape
    slots, _, inner = context.shape
    blocks = len(packs)
    count = controllers.shape[0]

    def own(i, place):
        return (jnp.minimum(place[0] + i, total - 1), 0, 0)

    rows = pl.BlockSpec((1, length, width), local_block)
    return pl.pallas_call(
        functools.partial(back_near_kernel, blocks, inner // count),
        grid_spec=pltpu.PrefetchScalarGridSpec(
            num_scalar_prefetch=1,
            grid=(slots,),
            in_specs=[
                pl.BlockSpec((1, length, width), own),
                rows,
                rows,
                pl.BlockSpec((1, length, 3 * inner), local_block),
                pl.BlockSpec((1, length, inner), local_block),
            ]
            + [whole(p.shape) for p in packs]
            + [whole((1, width)), whole((8, width)), whole(controllers.shape)],
            out_specs=[rows] + [whole((height, LANES))] * count,
            scratch_shapes=held_rows(slots, length, width, inner) + [pltpu.VMEM((8, width), F32)],
        ),
        out_shape=[
            jax.ShapeDtypeStruct((slots, length, width), BF16),
        ]
        + [jax.ShapeDtypeStruct((height, LANES), BF16)] * count,
        compiler_params=params("arbitrary"),
        cost_estimate=pl.CostEstimate(
            flops=0,
            bytes_accessed=slots * length * (width * 12 + inner * 8) + 16 * width * inner,
            transcendentals=slots * length * length * inner // HEAD_WIDTH,
        ),
        name="attention_back_near",
    )(place, tokens, d_hidden, partial, joint, context, *packs, gain_attn, gain_in, controllers)


def swap_core(x):
    narrow = lax.axis_size("narrow")
    return lax.ppermute(x, "narrow", [(n, n ^ 1) for n in range(narrow)])


def from_chip(x, k):
    narrow = lax.axis_size("narrow")
    return lax.ppermute(x, "narrow", [((n + 2 * k) % narrow, n) for n in range(narrow)])


def to_chip(x, k):
    narrow = lax.axis_size("narrow")
    return lax.ppermute(x, "narrow", [(n, (n + 2 * k) % narrow) for n in range(narrow)])


def relative_narrow():
    narrow = lax.axis_size("narrow")
    me = lax.axis_index("narrow")
    return [lax.bitwise_xor(lax.rem(me + 2 * (j // 2), narrow), j % 2) for j in range(narrow)]


def gather_narrow(x):
    blocks = []
    for k in range(lax.axis_size("narrow") // 2):
        piece = from_chip(x, k) if k else x
        blocks += [piece, swap_core(piece)]
    return blocks


def far_sums(pieces):
    pairs = [(pieces[2 * k], swap_core(pieces[2 * k + 1])) for k in range(len(pieces) // 2)]
    return [(x.astype(F32) + y.astype(F32)).astype(BF16) for x, y in pairs]


def after(x, *others):
    return lax.optimization_barrier((x, others))[0]


def wide_parts(x):
    wide = lax.axis_size("wide")
    parts = x.astype(BF16).reshape(wide, x.shape[0] // wide, x.shape[1])
    parts = lax.all_to_all(parts, "wide", split_axis=0, concat_axis=0, tiled=True)
    return jnp.sum(parts.astype(F32), axis=0).astype(BF16)


def from_parts(part):
    parts = jnp.broadcast_to(part[None], (lax.axis_size("wide"),) + part.shape)
    parts = lax.all_to_all(parts, "wide", split_axis=0, concat_axis=0, tiled=True)
    return parts.reshape(-1, part.shape[-1]).astype(F32)


def to_relative(x, j):
    narrow = lax.axis_size("narrow")
    k, other = j // 2, j % 2
    return lax.ppermute(x, "narrow", [(n, ((n + 2 * k) % narrow) ^ other) for n in range(narrow)])


def from_relative(x, j):
    narrow = lax.axis_size("narrow")
    k, other = j // 2, j % 2
    return lax.ppermute(x, "narrow", [(((n + 2 * k) % narrow) ^ other, n) for n in range(narrow)])


def to_unit(x, d):
    wide = lax.axis_size("wide")
    return lax.ppermute(x, "wide", [(w, w ^ d) for w in range(wide)])


def place_kernel(count, where, *refs):
    pieces, out = refs[:count], refs[-1]
    for j, piece in enumerate(pieces):

        @pl.when(pl.program_id(0) == j)
        def _(piece=piece):
            out[...] = piece[...]


def place_blocks(pieces, where, total, *rest):
    count = len(pieces)
    shape = pieces[0].shape
    return pl.pallas_call(
        functools.partial(place_kernel, count),
        grid_spec=pltpu.PrefetchScalarGridSpec(
            num_scalar_prefetch=1,
            grid=(count,),
            in_specs=[whole(shape)] * count + [pl.BlockSpec(memory_space=pl.ANY)] * len(rest),
            out_specs=pl.BlockSpec(shape, lambda j, where: (where[j], 0, 0)),
        ),
        out_shape=jax.ShapeDtypeStruct((total * shape[0],) + shape[1:], pieces[0].dtype),
        input_output_aliases={1 + count: 0} if rest else {},
        compiler_params=params("arbitrary"),
        cost_estimate=pl.CostEstimate(
            flops=0, bytes_accessed=pieces[0].size * 4 * count, transcendentals=0
        ),
        name="place_blocks",
    )(where, *pieces, *rest)


def body(
    tokens,
    cotangent,
    counts,
    group_order,
    query_weight,
    key_weight,
    value_weight,
    output_weight,
    gain_attn,
    gain_mix,
    controller,
    w_in,
    b_in,
    w_out,
    b_out,
):
    slot_count, seq_len, model_width = tokens.shape
    wide, narrow = lax.axis_size("wide"), lax.axis_size("narrow")
    spread = wide * narrow
    wide_index, narrow_index = lax.axis_index("wide"), lax.axis_index("narrow")
    slots = -(-slot_count // narrow)
    part = seq_len // spread
    padded_part = -(-part // 8) * 8
    local_experts = w_in.shape[0]
    experts = local_experts * narrow
    relative = jnp.stack(relative_narrow())
    head_columns = query_weight.shape[1]

    seq_ends = jnp.cumsum(counts)
    seq_starts = seq_ends - counts
    own_count = counts[wide_index]
    place = jnp.stack([narrow_index * slots, own_count]).astype(jnp.int32)
    slot_ids = jnp.arange(slots * narrow)
    slot_seqs = jnp.where(slot_ids[None] < counts[:, None], seq_starts[:, None] + slot_ids[None], -1)
    matches = slot_seqs.reshape(-1, 1) == group_order[None]
    slot_group = jnp.sum(jnp.where(matches, 1 + jnp.arange(group_order.shape[0]) // GROUP, 0), axis=1) - 1
    positions = jnp.arange(padded_part)
    row_code = jnp.where(slot_group[:, None] >= 0, slot_group[:, None] * padded_part + positions, -1)
    row_code = row_code.reshape(-1, 1).astype(jnp.int32)
    per_expert = GROUPS * padded_part
    col_code = (jnp.arange(experts * per_expert) % per_expert).astype(jnp.int32)[None]
    tile = jnp.repeat(jnp.eye(experts, dtype=BF16), per_expert, axis=1)

    pack = pack_weights(query_weight, key_weight, value_weight, output_weight)
    packs = [pack, swap_core(pack)]
    far_packs = [from_chip(pack, k) for k in range(1, narrow // 2)]
    joined = LANES // head_columns

    def join(packs):
        if joined == 1:
            return packs
        packs = [p.reshape(model_width, 4, head_columns) for p in packs]
        return [
            jnp.concatenate(packs[i : i + joined], axis=2).reshape(model_width, -1)
            for i in range(0, len(packs), joined)
        ]

    controllers = jnp.stack(gather_narrow(controller.T))
    controllers = controllers[jnp.argsort(relative)].reshape(experts, model_width).T

    gain_attn_row, gain_mix_row = gain_attn[None], gain_mix[None]

    def to_positions(x):
        x = lax.all_to_all(x, BOTH, split_axis=0, concat_axis=0, tiled=True)
        x = jnp.pad(x, ((0, 0), (0, 0), (0, padded_part - part), (0, 0)))
        return x.reshape(-1, model_width)

    def to_slots(x):
        x = x.reshape(spread, 2, slots, padded_part, model_width)[:, :, :, :part]
        x = x.reshape(spread, 2, slots * part, model_width)
        return lax.all_to_all(x, BOTH, split_axis=0, concat_axis=0, tiled=True)

    cots, *packs = lax.optimization_barrier((cotangent, *packs))
    cots = jnp.pad(cots, ((0, slots * narrow - slot_count), (0, 0), (0, 0)))
    cots = cots.reshape(slots * narrow, wide, narrow, part, model_width)
    cots = lax.dynamic_index_in_dim(cots, narrow_index, axis=2, keepdims=False).transpose(1, 0, 2, 3)
    cots = lax.all_to_all(cots, "wide", split_axis=0, concat_axis=0, tiled=True)
    cots = jnp.pad(cots, ((0, 0), (0, 0), (0, padded_part - part), (0, 0)))
    cot_rows = cots.reshape(-1, model_width)

    packs = join(packs)
    partial, joint_near, context_near = attention_near(place, tokens, packs, gain_attn_row, slots)
    partial, far_packs = lax.optimization_barrier((partial, far_packs))
    far_packs = join([x for piece in far_packs for x in (piece, swap_core(piece))])
    mix_sent, hidden, joint_far, context_far = attention_far(
        place, tokens, partial, far_packs, gain_attn_row, gain_mix_row, slots, spread
    )
    mix_rows = to_positions(mix_sent)
    probs, spread_probs, *both = mix_forward(
        padded_part, relative, mix_rows, cot_rows, controllers, row_code, col_code, tile, narrow
    )

    rows = GROUPS * part

    def trim(x):
        x = x.reshape(local_experts, 2, GROUPS, padded_part, model_width)[:, :, :, :part]
        return x.reshape(local_experts, 2, rows, model_width)

    def untrim(x):
        x = x.reshape(local_experts, 2, GROUPS, part, model_width)
        x = jnp.pad(x, ((0, 0), (0, 0), (0, 0), (0, padded_part - part), (0, 0)))
        return x.reshape(local_experts, 2, -1, model_width)

    both = [trim(x) for x in both]
    both = both[:1] + [to_relative(x, j) for j, x in enumerate(both) if j]
    halves = 2 if wide % 4 == 0 else 1
    units = wide // halves
    held, share = max(local_experts // units, 1), max(units // local_experts, 1)
    unit = lax.rem(wide_index, units)
    shape = (held, 2, rows, model_width)
    if share == 1:
        tokens_sent = [x.reshape((units, 1) + shape) for x in both]
        tokens_sent = jnp.concatenate([jnp.concatenate([x] * halves) for x in tokens_sent], axis=1)
    else:
        tokens_sent = jnp.stack(both).reshape((share, narrow // share, units // share) + shape)
        tokens_sent = tokens_sent.transpose(2, 0, 1, 3, 4, 5, 6).reshape((units, narrow // share) + shape)
        tokens_sent = jnp.concatenate([tokens_sent] * halves)
    tokens_sent, both = lax.optimization_barrier((tokens_sent, both))
    tokens_all = lax.all_to_all(tokens_sent, "wide", split_axis=0, concat_axis=0, tiled=True)
    if rows % 16 == 0:
        back = experts_at_positions(both, w_in, b_in, w_out, b_out)
    else:
        lines = jnp.stack(both, axis=2).reshape(local_experts, 2, narrow * rows, model_width)
        (back,) = experts_at_positions([lines], w_in, b_in, w_out, b_out)
        back = back.reshape(local_experts, 2, narrow, rows, model_width)
        back = [back[:, :, j] for j in range(narrow)]

    where = jnp.stack([wide_index // units, unit]).astype(jnp.int32)
    first = (unit * held // share).astype(jnp.int32)
    expert_grads = [
        expert_weights(where, (first + p)[None], p, tokens_all, w_in, b_in, w_out, wide, units)
        for p in range(held)
    ]

    back = [untrim(x if j == 0 else from_relative(x, j)) for j, x in enumerate(back)]
    slot_rows, grad_controller = mix_backward(
        padded_part,
        relative,
        spread_probs,
        mix_rows,
        cot_rows,
        probs,
        back,
        controllers,
        row_code,
        col_code,
        tile,
        spread,
    )
    slot_rows = to_slots(slot_rows)
    expert_grads = [[x[0]] + [to_unit(x[d], d) for d in range(1, units)] for x in expert_grads]
    slot_rows = after(slot_rows, expert_grads[0][:-1], [x[0] for x in expert_grads])

    height = 4 * model_width
    grad_controller = grad_controller.astype(BF16).reshape(narrow, -1, LANES)[relative]
    end = height + grad_controller.shape[1]
    rows_sent = -(-(end + 16) // (16 * wide)) * 16 * wide
    partial, d_hidden, mixed_part, gain_mix_part, *far = attention_back_far(
        place,
        tokens,
        cotangent,
        slot_rows,
        hidden,
        joint_far,
        context_far,
        far_packs,
        gain_attn_row,
        gain_mix_row,
        grad_controller[2:],
        rows_sent,
    )
    early = [x[1:-1] for x in expert_grads[1:]]
    far, early = lax.optimization_barrier((far, early))
    for x, pieces in zip(expert_grads[1:], early):
        x[1:-1] = pieces
    partial, far = lax.optimization_barrier((partial, far_sums(far)))
    far = sum([to_chip(x, k + 1).astype(F32) for k, x in enumerate(far)], 0.0)
    d_tokens, kept, sent = attention_back_near(
        place,
        tokens,
        d_hidden,
        partial,
        joint_near,
        context_near,
        packs,
        gain_attn_row,
        gain_mix_part,
        grad_controller[:2],
        rows_sent,
    )
    d_tokens, kept, sent, far, expert_grads[0][-1] = lax.optimization_barrier(
        (d_tokens, kept, sent, far, expert_grads[0][-1])
    )
    weights = kept.astype(F32) + swap_core(sent).astype(F32) + far
    part_sums = wide_parts(weights)

    far_tokens = [from_chip(d_tokens, k) for k in range(1, narrow // 2)]
    swapped = [swap_core(d_tokens), swap_core(mixed_part)]
    order = lax.bitwise_xor(unit, jnp.arange(units)) * held
    order = order[None] + jnp.arange(held)[:, None]
    order = jnp.concatenate([order[:, :-1].reshape(-1), order[:, -1]])
    pieces = [piece for x in expert_grads for piece in x[:-1]] + [x[-1] for x in expert_grads]
    owned = owned_weights(pieces[:-1], order[:-1], units * held, w_in.shape[2], wide)
    mixed_part, far_tokens, swapped, owned, pieces[-1] = lax.optimization_barrier(
        (mixed_part, far_tokens, swapped, owned, pieces[-1])
    )
    far_mixed = [from_chip(mixed_part, k) for k in range(1, narrow // 2)]
    far_tokens = [y for x in far_tokens for y in (x, swap_core(x))]
    part_sums, far_tokens = lax.optimization_barrier((part_sums, far_tokens))
    d_tokens = place_blocks([d_tokens, swapped[0]] + far_tokens, relative, narrow)
    g_w_in, g_w_out, bias = owned_weights(after(pieces[-1:], part_sums), order[-1:], units * held, w_in.shape[2], wide, owned)
    far_mixed, d_tokens, bias = lax.optimization_barrier((far_mixed, d_tokens, bias))
    far_mixed = [y for x in far_mixed for y in (x, swap_core(x))]
    mixed_part = place_blocks([mixed_part, swapped[1]] + far_mixed, relative, narrow)
    d_tokens, mixed_part = d_tokens[:slot_count], mixed_part[:slot_count]
    weights = from_parts(part_sums)
    gains = weights[end : end + 16].astype(BF16)
    gains = sum([to_chip(gains, k).astype(F32) for k in range(1, narrow // 2)], gains.astype(F32))
    projections = weights[: 3 * model_width, :head_columns].reshape(3, model_width, head_columns)
    output_weight_gradient = weights[3 * model_width : height].reshape(-1, LANES, LANES)[:, :head_columns]
    output_weight_gradient = output_weight_gradient.transpose(1, 0, 2).reshape(head_columns, -1)
    g_controller = weights[height:end].reshape(local_experts, model_width).T
    lines = model_width // LANES
    g_gain_attn = gains[:lines].reshape(-1)
    g_gain_mix = gains[lines : 2 * lines].reshape(-1)

    def over_share(x):
        return jnp.sum(x.reshape((local_experts, share) + x.shape[1:]), axis=1)

    g_w_in, g_w_out, bias = (over_share(x) for x in (g_w_in, g_w_out, bias))
    g_b_in = bias[:, : w_in.shape[2] // model_width].reshape(local_experts, -1)
    g_b_out = bias[:, -1]

    return (
        mixed_part,
        d_tokens,
        projections[0],
        projections[1],
        projections[2],
        output_weight_gradient,
        g_gain_attn,
        g_gain_mix,
        g_controller,
        g_w_in,
        g_b_in,
        g_w_out,
        g_b_out,
    )


def solution(mesh):
    placed = (
        P("wide", None, None),
        P("wide", None, None),
        P(),
        P(),
        P(None, "narrow"),
        P(None, "narrow"),
        P(None, "narrow"),
        P("narrow", None),
        P(),
        P(),
        P(None, "narrow"),
        P("narrow", None, None),
        P("narrow", None),
        P("narrow", None, None),
        P("narrow", None),
    )
    return jax.shard_map(
        body,
        mesh=mesh,
        in_specs=placed,
        out_specs=(
            P("wide", None, None),
            P("wide", None, None),
            P(None, "narrow"),
            P(None, "narrow"),
            P(None, "narrow"),
            P("narrow", None),
            P(),
            P(),
            P(None, "narrow"),
            P("narrow", "wide", None),
            P("narrow", None),
            P("narrow", "wide", None),
            P("narrow", None),
        ),
        check_vma=False,
    )
```

```python
import functools

import jax
import jax.numpy as jnp
from jax import lax
from jax.experimental import pallas as pl
from jax.experimental.pallas import tpu as pltpu
from jax.sharding import PartitionSpec as P

HEAD_WIDTH = 64
GROUP = 32
GROUPS = 2
LANES = 128

EPSILON = 1e-05
NEGATIVE = -1e30
BOTH = ("wide", "narrow")
F32 = jnp.float32
BF16 = jnp.bfloat16
VMEM_LIMIT = 56 * 1024 * 1024


def mm(a, b):
    return lax.dot_general(a, b, (((1,), (0,)), ((), ())), preferred_element_type=F32)


def mm_nt(a, b):
    return lax.dot_general(a, b, (((1,), (1,)), ((), ())), preferred_element_type=F32)


def mm_tn(a, b):
    return lax.dot_general(a, b, (((0,), (0,)), ((), ())), preferred_element_type=F32)


def params(*semantics):
    return pltpu.CompilerParams(dimension_semantics=semantics or None, vmem_limit_bytes=VMEM_LIMIT)


def whole(shape):
    zeros = (0,) * len(shape)
    return pl.BlockSpec(tuple(shape), lambda *_: zeros)


def head_masks(shape, axis):
    lane = lax.broadcasted_iota(jnp.int32, shape, axis)
    return [(lane >= h * HEAD_WIDTH) & (lane < (h + 1) * HEAD_WIDTH) for h in range(LANES // HEAD_WIDTH)]


def masks_of(length):
    return list(zip(head_masks((length, LANES), 1), head_masks((LANES, length), 0)))


def keep(mask, rows):
    return jnp.where(mask, rows, jnp.zeros_like(rows))


def causal_probs(query_head, keys, causal):
    scores = mm_nt(keys, query_head) * (float(HEAD_WIDTH) ** -0.5)
    scores = jnp.where(causal, scores, NEGATIVE)
    powers = jnp.exp(scores - jnp.max(scores, axis=0, keepdims=True))
    return powers * (1.0 / jnp.sum(powers, axis=0, keepdims=True))


def causal_mask(length):
    return lax.broadcasted_iota(jnp.int32, (length, length), 0) <= lax.broadcasted_iota(
        jnp.int32, (length, length), 1
    )


def inverse_rms(rows):
    return lax.rsqrt(jnp.mean(rows * rows, axis=-1, keepdims=True) + EPSILON)


def attend(entry, packs, causal, masks, joint_out, context_out):
    attention = None
    for j, pack in enumerate(packs):
        joint = mm(entry, pack[:, : 3 * LANES]).astype(BF16)
        joint_out[0, :, j * 3 * LANES : (j + 1) * 3 * LANES] = joint
        q, k, v = (joint[:, i * LANES : (i + 1) * LANES] for i in range(3))
        turned, context = v.T, None
        for mask, across in masks:
            probs = causal_probs(keep(mask, q), k, causal)
            term = mm(keep(across, turned), probs.astype(BF16))
            context = term if context is None else context + term
        context = context.astype(BF16).T
        context_out[0, :, j * LANES : (j + 1) * LANES] = context
        term = mm_nt(context, pack[:, 3 * LANES :])
        attention = term if attention is None else attention + term
    return attention


def near_kernel(blocks, place, tokens, *refs):
    packs, (gain_attn, partial_out, joint_out, context_out) = refs[:blocks], refs[blocks:]
    rows = tokens[0].astype(F32)
    entry = (rows * inverse_rms(rows) * gain_attn[...]).astype(BF16)
    length = rows.shape[0]
    partial_out[0] = rows + attend(
        entry, packs, causal_mask(length), masks_of(length), joint_out, context_out
    )


def far_kernel(blocks, place, tokens, partial, *refs):
    packs = refs[:blocks]
    gain_attn, gain_mix, mix_out, hidden_out, joint_out, context_out = refs[blocks:]
    rows = tokens[0].astype(F32)
    entry = (rows * inverse_rms(rows) * gain_attn[...]).astype(BF16)
    length = rows.shape[0]
    hidden = partial[0] + attend(
        entry, packs, causal_mask(length), masks_of(length), joint_out, context_out
    )
    mixed = hidden * inverse_rms(hidden) * gain_mix[...]
    mix_out[...] = mixed.reshape(mix_out.shape).astype(BF16)
    hidden_out[0] = hidden


def local_block(i, place):
    return (i, 0, 0)


def attention_near(place, tokens, packs, gain_attn, slots):
    total, length, width = tokens.shape
    inner = len(packs) * LANES
    return pl.pallas_call(
        functools.partial(near_kernel, len(packs)),
        grid_spec=pltpu.PrefetchScalarGridSpec(
            num_scalar_prefetch=1,
            grid=(slots,),
            in_specs=[
                pl.BlockSpec((1, length, width), lambda i, place: (jnp.minimum(place[0] + i, total - 1), 0, 0))
            ]
            + [whole(p.shape) for p in packs]
            + [whole((1, width))],
            out_specs=[
                pl.BlockSpec((1, length, width), local_block),
                pl.BlockSpec((1, length, 3 * inner), local_block),
                pl.BlockSpec((1, length, inner), local_block),
            ],
        ),
        out_shape=[
            jax.ShapeDtypeStruct((slots, length, width), F32),
            jax.ShapeDtypeStruct((slots, length, 3 * inner), BF16),
            jax.ShapeDtypeStruct((slots, length, inner), BF16),
        ],
        compiler_params=params("arbitrary"),
        cost_estimate=pl.CostEstimate(
            flops=slots * 2 * length * (4 * width * inner + 4 * length * inner),
            bytes_accessed=slots * length * (width * 6 + inner * 8) + 8 * width * inner,
            transcendentals=slots * length * length * inner // HEAD_WIDTH,
        ),
        name="attention_near",
    )(place, tokens, *packs, gain_attn)


def attention_far(place, tokens, partial, packs, gain_attn, gain_mix, slots, spread):
    total, length, width = tokens.shape
    inner = len(packs) * LANES
    part = length // spread
    return pl.pallas_call(
        functools.partial(far_kernel, len(packs)),
        grid_spec=pltpu.PrefetchScalarGridSpec(
            num_scalar_prefetch=1,
            grid=(slots,),
            in_specs=[
                pl.BlockSpec((1, length, width), lambda i, place: (jnp.minimum(place[0] + i, total - 1), 0, 0)),
                pl.BlockSpec((1, length, width), local_block),
            ]
            + [whole(p.shape) for p in packs]
            + [whole((1, width))] * 2,
            out_specs=[
                pl.BlockSpec((spread, 1, part, width), lambda i, place: (0, i, 0, 0)),
                pl.BlockSpec((1, length, width), local_block),
                pl.BlockSpec((1, length, 3 * inner), local_block),
                pl.BlockSpec((1, length, inner), local_block),
            ],
        ),
        out_shape=[
            jax.ShapeDtypeStruct((spread, slots, part, width), BF16),
            jax.ShapeDtypeStruct((slots, length, width), F32),
            jax.ShapeDtypeStruct((slots, length, 3 * inner), BF16),
            jax.ShapeDtypeStruct((slots, length, inner), BF16),
        ],
        compiler_params=params("arbitrary"),
        cost_estimate=pl.CostEstimate(
            flops=slots * 2 * length * (4 * width * inner + 4 * length * inner),
            bytes_accessed=slots * length * (width * 12 + inner * 8) + 8 * width * inner,
            transcendentals=slots * length * length * inner // HEAD_WIDTH,
        ),
        name="attention_far",
    )(place, tokens, partial, *packs, gain_attn, gain_mix)


def pack_kernel(query, key, value, output, out):
    width = query.shape[1]
    for i, ref in enumerate((query, key, value)):
        out[:, i * width : (i + 1) * width] = ref[...]
    out[:, 3 * width :] = output[...].T


def pack_weights(query, key, value, output):
    width, columns = query.shape
    if columns % LANES:
        return jnp.concatenate([query, key, value, output.T], axis=1)
    return pl.pallas_call(
        pack_kernel,
        out_shape=jax.ShapeDtypeStruct((width, 4 * columns), BF16),
        compiler_params=params(),
        cost_estimate=pl.CostEstimate(flops=0, bytes_accessed=16 * width * columns, transcendentals=0),
        name="pack_weights",
    )(query, key, value, output)


def slot_softmax(logits, codes, part):
    experts = logits.shape[1]
    logits = logits.reshape(-1, part, experts)
    codes = jnp.broadcast_to(codes, (codes.shape[0], experts)).reshape(-1, part, experts)
    total = jnp.zeros_like(logits)
    for g in range(GROUPS):
        inside = (codes >= g * part) & (codes < (g + 1) * part)
        held = jnp.where(inside, logits, NEGATIVE)
        powers = jnp.where(inside, jnp.exp(held - jnp.max(held, axis=0, keepdims=True)), 0.0)
        total = total + powers / jnp.sum(powers, axis=0, keepdims=True)
    return total.reshape(-1, experts)


def group_totals(terms, codes, part):
    experts = terms.shape[1]
    terms = terms.reshape(-1, part, experts)
    codes = jnp.broadcast_to(codes, (codes.shape[0], experts)).reshape(-1, part, experts)
    total = jnp.zeros_like(terms)
    for g in range(GROUPS):
        inside = (codes >= g * part) & (codes < (g + 1) * part)
        total = jnp.where(inside, jnp.sum(jnp.where(inside, terms, 0.0), axis=0, keepdims=True), total)
    return total.reshape(-1, experts)


def mix_kernel(part, relative, rows, cots, controller, row_code, col_code, tile, probs_out, spread_out, *refs):
    sent, (merged, grads) = refs[:-2], refs[-2:]
    held = rows[...]
    probs = slot_softmax(mm(held, controller[...]), row_code[...], part)
    probs_out[...] = probs
    wide = mm(probs.astype(BF16), tile[...])
    spread = jnp.where(row_code[...] == col_code[...], wide, 0.0).astype(BF16)
    spread_out[...] = spread
    count, _, lines, _ = sent[0].shape
    merged[...] = mm_tn(spread, held).astype(BF16)
    grads[...] = mm_tn(spread, cots[...]).astype(BF16)
    for j, out in enumerate(sent):
        for e in range(count):
            at = pl.ds(pl.multiple_of((relative[j] * count + e) * lines, lines), lines)
            out[e, 0] = merged[at]
            out[e, 1] = grads[at]


def mix_forward(part, relative, rows, cots, controller, row_code, col_code, tile, narrow):
    count, width = rows.shape
    experts, columns = tile.shape
    sent = (experts // narrow, 2, columns // experts, width)
    return pl.pallas_call(
        functools.partial(mix_kernel, part),
        grid_spec=pltpu.PrefetchScalarGridSpec(
            num_scalar_prefetch=1,
            grid=(1,),
            in_specs=[whole(x.shape) for x in (rows, cots, controller, row_code, col_code, tile)],
            out_specs=[whole((count, experts)), whole((count, columns))]
            + [whole(sent)] * narrow,
            scratch_shapes=[pltpu.VMEM((columns, width), BF16)] * 2,
        ),
        out_shape=[
            jax.ShapeDtypeStruct((count, experts), F32),
            jax.ShapeDtypeStruct((count, columns), BF16),
        ]
        + [jax.ShapeDtypeStruct(sent, BF16)] * narrow,
        compiler_params=params("arbitrary"),
        cost_estimate=pl.CostEstimate(
            flops=4 * count * columns * width,
            bytes_accessed=6 * count * width * 2,
            transcendentals=count * experts * 2,
        ),
        name="mix_forward",
    )(relative, rows, cots, controller, row_code, col_code, tile)


def unmix_kernel(
    part, narrow, relative, spread, rows, cots, probs, controller, row_code, col_code, tile, *refs
):
    back, (sent, gain_out, outs, grads) = refs[:narrow], refs[narrow:]
    count, _, lines, _ = back[0].shape
    for j, piece in enumerate(back):
        for e in range(count):
            at = pl.ds(pl.multiple_of((relative[j] * count + e) * lines, lines), lines)
            outs[at] = piece[e, 0]
            grads[at] = piece[e, 1]
    held = rows[...]
    pairs = (mm_nt(cots[...], outs[...]) + mm_nt(held, grads[...])).astype(BF16)
    pairs = jnp.where(row_code[...] == col_code[...], pairs, jnp.zeros_like(pairs))
    d_weights = mm_nt(pairs, tile[...])
    p = probs[...]
    d_logits = (p * (d_weights - group_totals(p * d_weights, row_code[...], part))).astype(BF16)
    shape = (sent.shape[0],) + sent.shape[2:]
    grad = mm(spread[...], grads[...]) + mm_nt(d_logits, controller[...])
    sent[:, 0] = grad.reshape(shape).astype(BF16)
    sent[:, 1] = mm(spread[...], outs[...]).reshape(shape).astype(BF16)
    gain_out[...] = mm_tn(d_logits, held)


def mix_backward(part, relative, spread, rows, cots, probs, back, controller, row_code, col_code, tile, devices):
    count, width = rows.shape
    experts, columns = tile.shape
    operands = (spread, rows, cots, probs, controller, row_code, col_code, tile) + tuple(back)
    outs = [
        jax.ShapeDtypeStruct((devices, 2, count // devices, width), BF16),
        jax.ShapeDtypeStruct((experts, width), F32),
    ]
    return pl.pallas_call(
        functools.partial(unmix_kernel, part, len(back)),
        grid_spec=pltpu.PrefetchScalarGridSpec(
            num_scalar_prefetch=1,
            grid=(1,),
            in_specs=[whole(x.shape) for x in operands],
            out_specs=[whole(x.shape) for x in outs],
            scratch_shapes=[pltpu.VMEM((columns, width), BF16)] * 2,
        ),
        out_shape=outs,
        compiler_params=params("arbitrary"),
        cost_estimate=pl.CostEstimate(
            flops=8 * count * columns * width,
            bytes_accessed=8 * count * width * 2,
            transcendentals=0,
        ),
        name="mix_backward",
    )(relative, *operands)


GELU_SLOPE = 0.7978845608028654
GELU_CUBE = 0.044715


def gelu_pair(x):
    square = x * x
    bend = jnp.tanh(GELU_SLOPE * x * (1.0 + GELU_CUBE * square))
    gate = 0.5 * (1.0 + bend)
    slope = gate + 0.5 * x * (1.0 - bend * bend) * (GELU_SLOPE * (1.0 + 3.0 * GELU_CUBE * square))
    return x * gate, slope


def expert_kernel(count, *refs):
    both, (w_in, b_in, w_out, b_out), sent = refs[:count], refs[count : count + 4], refs[count + 4 :]
    rows = both[0].shape[2]
    merged = jnp.concatenate([x[0, 0] for x in both], axis=0)
    grads = jnp.concatenate([x[0, 1] for x in both], axis=0)
    act, slope = gelu_pair(mm(merged, w_in[0]) + b_in[0])
    outs = mm(act.astype(BF16), w_out[0]) + b_out[0]
    d_pre = (mm_nt(grads, w_out[0]) * slope).astype(BF16)
    d_merged = mm_nt(d_pre, w_in[0])
    for j, out in enumerate(sent):
        at = slice(j * rows, (j + 1) * rows)
        out[0, 0] = outs[at].astype(BF16)
        out[0, 1] = d_merged[at].astype(BF16)


def experts_at_positions(both, w_in, b_in, w_out, b_out):
    experts, _, rows, width = both[0].shape
    inner = w_in.shape[2]
    sources, count = len(both), experts * rows
    tokens = pl.BlockSpec((1, 2, rows, width), lambda e: (e, 0, 0, 0))
    return pl.pallas_call(
        functools.partial(expert_kernel, sources),
        grid=(experts,),
        in_specs=[tokens] * sources
        + [
            pl.BlockSpec((1, width, inner), lambda e: (e, 0, 0)),
            pl.BlockSpec((1, 1, inner), lambda e: (e, 0, 0)),
            pl.BlockSpec((1, inner, width), lambda e: (e, 0, 0)),
            pl.BlockSpec((1, 1, width), lambda e: (e, 0, 0)),
        ],
        out_specs=[tokens] * sources,
        out_shape=[jax.ShapeDtypeStruct(x.shape, BF16) for x in both],
        compiler_params=params("arbitrary"),
        cost_estimate=pl.CostEstimate(
            flops=8 * sources * count * width * inner,
            bytes_accessed=4 * experts * width * inner + 4 * sources * count * width * 2,
            transcendentals=sources * count * inner,
        ),
        name="experts",
    )(*both, w_in, b_in[:, None], w_out, b_out[:, None])


def weight_kernel(units, where, both, w_in, b_in, w_out, *refs):
    outs, (merged, grads, turned, total) = refs[:units], refs[units:]
    i, half, unit = pl.program_id(0), where[0], where[1]
    steps = pl.num_programs(0)
    width = both.shape[-1]
    span = turned.shape[0]
    rows = span // units
    height = outs[0].shape[0]
    block = height - 16 - steps * rows
    slices = width // block

    @pl.when(i == 0)
    def _():
        merged[...] = both[:, :, 0, 0].reshape(merged.shape)
        grads[...] = both[:, :, 0, 1].reshape(grads.shape)
        turned[...] = merged[:, pl.ds(pl.multiple_of(half * span, span), span)].T
        sums = jnp.sum(grads[...].astype(F32), axis=0, keepdims=True).astype(BF16)
        for out in outs:
            out[height - 16 :] = jnp.zeros((16, width), BF16)
            out[height - 1 :] = sums

    act, slope = gelu_pair(mm(merged[...], w_in[0]) + b_in[0])
    d_pre = (mm_nt(grads[...], w_out[0]) * slope).astype(BF16)
    bias = jnp.sum(d_pre.astype(F32), axis=0, keepdims=True).astype(BF16)
    total[...] = mm(turned[...], d_pre)
    base = pl.ds(pl.multiple_of(i * rows, rows), rows)
    for d, out in enumerate(outs):
        own = pl.ds(pl.multiple_of(lax.bitwise_xor(unit, d) * rows, rows), rows)
        out[base] = total[own].astype(BF16)
    for step in range(steps):

        @pl.when(i == step)
        def _(step=step):
            for out in outs:
                out[height - 16 + step : height - 15 + step] = bias

    @pl.when(i // (steps // 2) == half)
    def _():
        grad = mm_tn(act.astype(BF16), grads[...]).astype(BF16)
        first = (i - half * (steps // 2)) * slices
        for s in range(slices):
            for d, out in enumerate(outs):

                @pl.when(first + s == lax.bitwise_xor(unit, d))
                def _(s=s, out=out):
                    out[height - 16 - block : height - 16] = grad[s * block : (s + 1) * block]


def expert_weights(where, expert, p, both, w_in, b_in, w_out, wide, units):
    sources, inner_sources, _, _, rows, width = both.shape
    inner = w_in.shape[2]
    count = sources * inner_sources * rows
    span = width * units // wide
    height = inner // width * (width // wide) + inner // wide + 16
    return pl.pallas_call(
        lambda where, expert, *refs: weight_kernel(units, where, *refs),
        grid_spec=pltpu.PrefetchScalarGridSpec(
            num_scalar_prefetch=2,
            grid=(inner // width,),
            in_specs=[
                pl.BlockSpec(
                    (sources, inner_sources, 1, 2, rows, width), lambda i, w, e: (0, 0, p, 0, 0, 0)
                ),
                pl.BlockSpec((1, width, width), lambda i, w, e: (e[0], 0, i)),
                pl.BlockSpec((1, 1, width), lambda i, w, e: (e[0], 0, i)),
                pl.BlockSpec((1, width, width), lambda i, w, e: (e[0], i, 0)),
            ],
            out_specs=[whole((height, width))] * units,
            scratch_shapes=[pltpu.VMEM((count, width), BF16)] * 2
            + [pltpu.VMEM((span, count), BF16), pltpu.VMEM((span, width), F32)],
        ),
        out_shape=[jax.ShapeDtypeStruct((height, width), BF16)] * units,
        compiler_params=params("arbitrary"),
        cost_estimate=pl.CostEstimate(
            flops=6 * count * width * inner,
            bytes_accessed=8 * width * inner + 4 * count * width,
            transcendentals=count * inner,
        ),
        name="expert_weights",
    )(where, expert, both, w_in, b_in[:, None], w_out)


def owner_kernel(count, where, *refs):
    pieces, (g_in, g_out, bias) = refs[:count], refs[-3:]
    rows, block = g_in.shape[1], g_out.shape[1]
    width = g_out.shape[2]
    start = pieces[0].shape[0] - 16 - block
    for j, piece in enumerate(pieces):

        @pl.when(pl.program_id(0) == j)
        def _(piece=piece):
            for c in range(g_in.shape[2] // width):
                g_in[0, :, c * width : (c + 1) * width] = piece[c * rows : (c + 1) * rows].astype(F32)
            g_out[0] = piece[start : start + block].astype(F32)
            bias[0] = piece[start + block :].astype(F32)


def owned_weights(pieces, where, total, inner, wide, rest=()):
    count = len(pieces)
    width = pieces[0].shape[1]
    shapes = [(1, width // wide, inner), (1, inner // wide, width), (1, 16, width)]
    return pl.pallas_call(
        functools.partial(owner_kernel, count),
        grid_spec=pltpu.PrefetchScalarGridSpec(
            num_scalar_prefetch=1,
            grid=(count,),
            in_specs=[whole(x.shape) for x in pieces] + [pl.BlockSpec(memory_space=pl.ANY)] * len(rest),
            out_specs=[pl.BlockSpec(x, lambda j, where: (where[j], 0, 0)) for x in shapes],
        ),
        out_shape=[jax.ShapeDtypeStruct((total,) + x[1:], F32) for x in shapes],
        input_output_aliases={1 + count + i: i for i in range(len(rest))},
        compiler_params=params("arbitrary"),
        cost_estimate=pl.CostEstimate(
            flops=0, bytes_accessed=sum(x.size for x in pieces) * 6, transcendentals=0
        ),
        name="owned_weights",
    )(where, *pieces, *rest)


def attend_back(i, entry, d_low, packs, joint_in, context_in, causal, masks, held):
    length = entry.shape[0]
    lines = pl.ds(pl.multiple_of(i * length, length), length)
    for ref, rows in zip(held, (entry, d_low, None, context_in[0])):
        if rows is not None:
            ref[lines] = rows
    scale = float(HEAD_WIDTH) ** -0.5
    d_entry = None
    for j, pack in enumerate(packs):
        base = j * 3 * LANES
        q, k, v = (joint_in[0, :, base + i * LANES : base + (i + 1) * LANES] for i in range(3))
        d_context = mm(d_low, pack[:, 3 * LANES :]).astype(BF16)
        d_q, d_k, d_v = [], [], []
        turned = k.T
        for mask, across in masks:
            q_head = keep(mask, q)
            d_head = keep(mask, d_context)
            probs = causal_probs(q_head, k, causal)
            d_probs = mm_nt(v, d_head).astype(BF16).astype(F32)
            d_scores = probs * (d_probs - jnp.sum(probs * d_probs, axis=0, keepdims=True))
            d_scores = d_scores.astype(BF16)
            d_v.append(mm(probs.astype(BF16), d_head))
            d_q.append(mm(keep(across, turned), d_scores))
            d_k.append(mm(d_scores, q_head))
        joint = [(sum(d_q) * scale).astype(BF16).T, (sum(d_k) * scale).astype(BF16), sum(d_v).astype(BF16)]
        joint = jnp.concatenate(joint, axis=1)
        term = mm_nt(joint, pack[:, : 3 * LANES])
        d_entry = term if d_entry is None else d_entry + term
        held[2][lines, base : base + 3 * LANES] = joint
    return d_entry


def store_weights(held, controllers, outs, lanes, gains=None):
    entry, d_low, joint, context = held
    width = entry.shape[1]
    for o, out in enumerate(outs):
        j, at = divmod(o, LANES // lanes)
        own = slice(at * lanes, (at + 1) * lanes)
        grad = mm_tn(entry[...], joint[:, j * 3 * LANES : (j + 1) * 3 * LANES]).astype(BF16)
        for c in range(3):
            piece = grad[:, c * LANES : (c + 1) * LANES]
            if lanes < LANES:
                piece = jnp.pad(piece[:, own], ((0, 0), (0, LANES - lanes)))
            out[c * width : (c + 1) * width] = piece
        grad = mm_tn(context[:, j * LANES : (j + 1) * LANES], d_low[...]).astype(BF16)
        for c in range(width // LANES):
            piece = grad[:, c * LANES : (c + 1) * LANES]
            if lanes < LANES:
                piece = jnp.pad(piece[own], ((0, LANES - lanes), (0, 0)))
            out[3 * width + c * LANES : 3 * width + (c + 1) * LANES] = piece
        tail = [controllers[o]]
        if gains is not None:
            tail.append(gains)
        left = out.shape[0] - 4 * width - sum(x.shape[0] for x in tail)
        out[4 * width :] = jnp.concatenate(tail + [jnp.zeros((left, LANES), BF16)], axis=0)


def held_rows(slots, length, width, inner):
    return [pltpu.VMEM((slots * length, columns), BF16) for columns in (width, width, 3 * inner, inner)]


def back_far_kernel(blocks, lanes, place, tokens, cots, grads, mixed, hidden, joint, context, *refs):
    packs, (gain_attn, gain_mix, controllers), refs = refs[:blocks], refs[blocks : blocks + 3], refs[blocks + 3 :]
    (partial_out, d_hidden_out, mixed_out, gain_out), outs, held = refs[:4], refs[4:-4], refs[-4:]
    i = pl.program_id(0)
    length, width = hidden.shape[1:]
    live = (place[0] + i < place[1]).astype(F32)

    @pl.when(i == 0)
    def _():
        gain_out[...] = jnp.zeros_like(gain_out)

    rows = hidden[0]
    inverse = inverse_rms(rows)
    normed = rows * inverse
    grad = grads[...].astype(F32).reshape(length, width)
    gain_out[0:1] += jnp.sum(grad * normed, axis=0, keepdims=True)
    d_normed = grad * gain_mix[...]
    d_hidden = cots[0].astype(F32) * live + inverse * (
        d_normed - normed * jnp.mean(d_normed * normed, axis=-1, keepdims=True)
    )
    d_hidden_out[0] = d_hidden
    mixed_out[0] = (live * (hidden[0] + mixed[...].astype(F32).reshape(length, width))).astype(BF16)
    rows = tokens[0].astype(F32)
    entry = (rows * inverse_rms(rows) * gain_attn[...]).astype(BF16)
    partial_out[0] = attend_back(
        i, entry, d_hidden.astype(BF16), packs, joint, context, causal_mask(length), masks_of(length), held
    )

    @pl.when(i == pl.num_programs(0) - 1)
    def _():
        store_weights(held, controllers, outs, lanes)


def back_near_kernel(blocks, lanes, place, tokens, d_hidden, partial, joint, context, *refs):
    packs, (gain_attn, gain_in, controllers), refs = refs[:blocks], refs[blocks : blocks + 3], refs[blocks + 3 :]
    d_tokens_out, outs, held, gain = refs[0], refs[1:-5], refs[-5:-1], refs[-1]
    i = pl.program_id(0)
    length, width = d_hidden.shape[1:]

    @pl.when(i == 0)
    def _():
        gain[...] = jnp.zeros_like(gain)

    rows = tokens[0].astype(F32)
    inverse = inverse_rms(rows)
    normed = rows * inverse
    entry = (normed * gain_attn[...]).astype(BF16)
    d_entry = partial[0] + attend_back(
        i, entry, d_hidden[0].astype(BF16), packs, joint, context, causal_mask(length), masks_of(length), held
    )
    d_entry = d_entry.astype(BF16).astype(F32)
    gain[0:1] += jnp.sum(d_entry * normed, axis=0, keepdims=True)
    d_normed = d_entry * gain_attn[...]
    d_tokens = d_hidden[0] + inverse * (
        d_normed - normed * jnp.mean(d_normed * normed, axis=-1, keepdims=True)
    )
    live = (place[0] + i < place[1]).astype(F32)
    d_tokens_out[0] = (d_tokens * live).astype(BF16)

    @pl.when(i == pl.num_programs(0) - 1)
    def _():
        pieces = width // LANES
        tail = [x[0:1, c * LANES : (c + 1) * LANES] for x in (gain, gain_in) for c in range(pieces)]
        tail.append(jnp.zeros((16 - 2 * pieces, LANES), F32))
        store_weights(held, controllers, outs, lanes, jnp.concatenate(tail, axis=0).astype(BF16))


def attention_back_far(
    place, tokens, cotangent, back, hidden, joint, context, packs, gain_attn, gain_mix, controllers, height
):
    total, length, width = tokens.shape
    slots = hidden.shape[0]
    spread, part = back.shape[0], back.shape[2] // slots
    inner = context.shape[2]
    blocks = len(packs)
    count = controllers.shape[0]

    def own(i, place):
        return (jnp.minimum(place[0] + i, total - 1), 0, 0)

    rows = pl.BlockSpec((1, length, width), local_block)
    return pl.pallas_call(
        functools.partial(back_far_kernel, blocks, inner // count),
        grid_spec=pltpu.PrefetchScalarGridSpec(
            num_scalar_prefetch=1,
            grid=(slots,),
            in_specs=[
                pl.BlockSpec((1, length, width), own),
                pl.BlockSpec((1, length, width), own),
                pl.BlockSpec((spread, 1, part, width), lambda i, place: (0, 0, i, 0)),
                pl.BlockSpec((spread, 1, part, width), lambda i, place: (0, 1, i, 0)),
                rows,
                pl.BlockSpec((1, length, 3 * inner), local_block),
                pl.BlockSpec((1, length, inner), local_block),
            ]
            + [whole(p.shape) for p in packs]
            + [whole((1, width))] * 2
            + [whole(controllers.shape)],
            out_specs=[rows, rows, rows, whole((8, width))] + [whole((height, LANES))] * count,
            scratch_shapes=held_rows(slots, length, width, inner),
        ),
        out_shape=[
            jax.ShapeDtypeStruct((slots, length, width), F32),
            jax.ShapeDtypeStruct((slots, length, width), F32),
            jax.ShapeDtypeStruct((slots, length, width), BF16),
            jax.ShapeDtypeStruct((8, width), F32),
        ]
        + [jax.ShapeDtypeStruct((height, LANES), BF16)] * count,
        compiler_params=params("arbitrary"),
        cost_estimate=pl.CostEstimate(
            flops=0,
            bytes_accessed=slots * length * (width * 18 + inner * 8) + 16 * width * inner,
            transcendentals=slots * length * length * inner // HEAD_WIDTH,
        ),
        name="attention_back_far",
    )(place, tokens, cotangent, back, back, hidden, joint, context, *packs, gain_attn, gain_mix, controllers)


def attention_back_near(
    place, tokens, d_hidden, partial, joint, context, packs, gain_attn, gain_in, controllers, height
):
    total, length, width = tokens.shape
    slots, _, inner = context.shape
    blocks = len(packs)
    count = controllers.shape[0]

    def own(i, place):
        return (jnp.minimum(place[0] + i, total - 1), 0, 0)

    rows = pl.BlockSpec((1, length, width), local_block)
    return pl.pallas_call(
        functools.partial(back_near_kernel, blocks, inner // count),
        grid_spec=pltpu.PrefetchScalarGridSpec(
            num_scalar_prefetch=1,
            grid=(slots,),
            in_specs=[
                pl.BlockSpec((1, length, width), own),
                rows,
                rows,
                pl.BlockSpec((1, length, 3 * inner), local_block),
                pl.BlockSpec((1, length, inner), local_block),
            ]
            + [whole(p.shape) for p in packs]
            + [whole((1, width)), whole((8, width)), whole(controllers.shape)],
            out_specs=[rows] + [whole((height, LANES))] * count,
            scratch_shapes=held_rows(slots, length, width, inner) + [pltpu.VMEM((8, width), F32)],
        ),
        out_shape=[
            jax.ShapeDtypeStruct((slots, length, width), BF16),
        ]
        + [jax.ShapeDtypeStruct((height, LANES), BF16)] * count,
        compiler_params=params("arbitrary"),
        cost_estimate=pl.CostEstimate(
            flops=0,
            bytes_accessed=slots * length * (width * 12 + inner * 8) + 16 * width * inner,
            transcendentals=slots * length * length * inner // HEAD_WIDTH,
        ),
        name="attention_back_near",
    )(place, tokens, d_hidden, partial, joint, context, *packs, gain_attn, gain_in, controllers)


def swap_core(x):
    narrow = lax.axis_size("narrow")
    return lax.ppermute(x, "narrow", [(n, n ^ 1) for n in range(narrow)])


def from_chip(x, k):
    narrow = lax.axis_size("narrow")
    return lax.ppermute(x, "narrow", [((n + 2 * k) % narrow, n) for n in range(narrow)])


def to_chip(x, k):
    narrow = lax.axis_size("narrow")
    return lax.ppermute(x, "narrow", [(n, (n + 2 * k) % narrow) for n in range(narrow)])


def relative_narrow():
    narrow = lax.axis_size("narrow")
    me = lax.axis_index("narrow")
    return [lax.bitwise_xor(lax.rem(me + 2 * (j // 2), narrow), j % 2) for j in range(narrow)]


def gather_narrow(x):
    blocks = []
    for k in range(lax.axis_size("narrow") // 2):
        piece = from_chip(x, k) if k else x
        blocks += [piece, swap_core(piece)]
    return blocks


def far_sums(pieces):
    pairs = [(pieces[2 * k], swap_core(pieces[2 * k + 1])) for k in range(len(pieces) // 2)]
    return [(x.astype(F32) + y.astype(F32)).astype(BF16) for x, y in pairs]


def after(x, *others):
    return lax.optimization_barrier((x, others))[0]


def wide_parts(x):
    wide = lax.axis_size("wide")
    parts = x.astype(BF16).reshape(wide, x.shape[0] // wide, x.shape[1])
    parts = lax.all_to_all(parts, "wide", split_axis=0, concat_axis=0, tiled=True)
    return jnp.sum(parts.astype(F32), axis=0).astype(BF16)


def from_parts(part):
    parts = jnp.broadcast_to(part[None], (lax.axis_size("wide"),) + part.shape)
    parts = lax.all_to_all(parts, "wide", split_axis=0, concat_axis=0, tiled=True)
    return parts.reshape(-1, part.shape[-1]).astype(F32)


def to_relative(x, j):
    narrow = lax.axis_size("narrow")
    k, other = j // 2, j % 2
    return lax.ppermute(x, "narrow", [(n, ((n + 2 * k) % narrow) ^ other) for n in range(narrow)])


def from_relative(x, j):
    narrow = lax.axis_size("narrow")
    k, other = j // 2, j % 2
    return lax.ppermute(x, "narrow", [(((n + 2 * k) % narrow) ^ other, n) for n in range(narrow)])


def to_unit(x, d):
    wide = lax.axis_size("wide")
    return lax.ppermute(x, "wide", [(w, w ^ d) for w in range(wide)])


def place_kernel(count, where, *refs):
    pieces, out = refs[:count], refs[-1]
    for j, piece in enumerate(pieces):

        @pl.when(pl.program_id(0) == j)
        def _(piece=piece):
            out[...] = piece[...]


def place_blocks(pieces, where, total, *rest):
    count = len(pieces)
    shape = pieces[0].shape
    return pl.pallas_call(
        functools.partial(place_kernel, count),
        grid_spec=pltpu.PrefetchScalarGridSpec(
            num_scalar_prefetch=1,
            grid=(count,),
            in_specs=[whole(shape)] * count + [pl.BlockSpec(memory_space=pl.ANY)] * len(rest),
            out_specs=pl.BlockSpec(shape, lambda j, where: (where[j], 0, 0)),
        ),
        out_shape=jax.ShapeDtypeStruct((total * shape[0],) + shape[1:], pieces[0].dtype),
        input_output_aliases={1 + count: 0} if rest else {},
        compiler_params=params("arbitrary"),
        cost_estimate=pl.CostEstimate(
            flops=0, bytes_accessed=pieces[0].size * 4 * count, transcendentals=0
        ),
        name="place_blocks",
    )(where, *pieces, *rest)


def body(
    tokens,
    cotangent,
    counts,
    group_order,
    query_weight,
    key_weight,
    value_weight,
    output_weight,
    gain_attn,
    gain_mix,
    controller,
    w_in,
    b_in,
    w_out,
    b_out,
):
    slot_count, seq_len, model_width = tokens.shape
    wide, narrow = lax.axis_size("wide"), lax.axis_size("narrow")
    spread = wide * narrow
    wide_index, narrow_index = lax.axis_index("wide"), lax.axis_index("narrow")
    slots = -(-slot_count // narrow)
    part = seq_len // spread
    padded_part = -(-part // 8) * 8
    local_experts = w_in.shape[0]
    experts = local_experts * narrow
    relative = jnp.stack(relative_narrow())
    head_columns = query_weight.shape[1]

    seq_ends = jnp.cumsum(counts)
    seq_starts = seq_ends - counts
    own_count = counts[wide_index]
    place = jnp.stack([narrow_index * slots, own_count]).astype(jnp.int32)
    slot_ids = jnp.arange(slots * narrow)
    slot_seqs = jnp.where(slot_ids[None] < counts[:, None], seq_starts[:, None] + slot_ids[None], -1)
    matches = slot_seqs.reshape(-1, 1) == group_order[None]
    slot_group = jnp.sum(jnp.where(matches, 1 + jnp.arange(group_order.shape[0]) // GROUP, 0), axis=1) - 1
    positions = jnp.arange(padded_part)
    row_code = jnp.where(slot_group[:, None] >= 0, slot_group[:, None] * padded_part + positions, -1)
    row_code = row_code.reshape(-1, 1).astype(jnp.int32)
    per_expert = GROUPS * padded_part
    col_code = (jnp.arange(experts * per_expert) % per_expert).astype(jnp.int32)[None]
    tile = jnp.repeat(jnp.eye(experts, dtype=BF16), per_expert, axis=1)

    pack = pack_weights(query_weight, key_weight, value_weight, output_weight)
    packs = [pack, swap_core(pack)]
    far_packs = [from_chip(pack, k) for k in range(1, narrow // 2)]
    joined = LANES // head_columns

    def join(packs):
        if joined == 1:
            return packs
        packs = [p.reshape(model_width, 4, head_columns) for p in packs]
        return [
            jnp.concatenate(packs[i : i + joined], axis=2).reshape(model_width, -1)
            for i in range(0, len(packs), joined)
        ]

    controllers = jnp.stack(gather_narrow(controller.T))
    controllers = controllers[jnp.argsort(relative)].reshape(experts, model_width).T

    gain_attn_row, gain_mix_row = gain_attn[None], gain_mix[None]

    def to_positions(x):
        x = lax.all_to_all(x, BOTH, split_axis=0, concat_axis=0, tiled=True)
        x = jnp.pad(x, ((0, 0), (0, 0), (0, padded_part - part), (0, 0)))
        return x.reshape(-1, model_width)

    def to_slots(x):
        x = x.reshape(spread, 2, slots, padded_part, model_width)[:, :, :, :part]
        x = x.reshape(spread, 2, slots * part, model_width)
        return lax.all_to_all(x, BOTH, split_axis=0, concat_axis=0, tiled=True)

    cots = jnp.pad(cotangent, ((0, slots * narrow - slot_count), (0, 0), (0, 0)))
    cots = cots.reshape(slots * narrow, wide, narrow, part, model_width)
    cots = lax.dynamic_index_in_dim(cots, narrow_index, axis=2, keepdims=False).transpose(1, 0, 2, 3)
    cots = lax.all_to_all(cots, "wide", split_axis=0, concat_axis=0, tiled=True)
    cots = jnp.pad(cots, ((0, 0), (0, 0), (0, padded_part - part), (0, 0)))
    cot_rows = cots.reshape(-1, model_width)

    packs = join(packs)
    partial, joint_near, context_near = attention_near(place, tokens, packs, gain_attn_row, slots)
    partial, far_packs = lax.optimization_barrier((partial, far_packs))
    far_packs = join([x for piece in far_packs for x in (piece, swap_core(piece))])
    mix_sent, hidden, joint_far, context_far = attention_far(
        place, tokens, partial, far_packs, gain_attn_row, gain_mix_row, slots, spread
    )
    mix_rows = to_positions(mix_sent)
    probs, spread_probs, *both = mix_forward(
        padded_part, relative, mix_rows, cot_rows, controllers, row_code, col_code, tile, narrow
    )

    rows = GROUPS * part

    def trim(x):
        x = x.reshape(local_experts, 2, GROUPS, padded_part, model_width)[:, :, :, :part]
        return x.reshape(local_experts, 2, rows, model_width)

    def untrim(x):
        x = x.reshape(local_experts, 2, GROUPS, part, model_width)
        x = jnp.pad(x, ((0, 0), (0, 0), (0, 0), (0, padded_part - part), (0, 0)))
        return x.reshape(local_experts, 2, -1, model_width)

    both = [trim(x) for x in both]
    both = both[:1] + [to_relative(x, j) for j, x in enumerate(both) if j]
    halves = 2 if wide % 4 == 0 else 1
    units = wide // halves
    held, share = max(local_experts // units, 1), max(units // local_experts, 1)
    unit = lax.rem(wide_index, units)
    shape = (held, 2, rows, model_width)
    if share == 1:
        tokens_sent = [x.reshape((units, 1) + shape) for x in both]
        tokens_sent = jnp.concatenate([jnp.concatenate([x] * halves) for x in tokens_sent], axis=1)
    else:
        tokens_sent = jnp.stack(both).reshape((share, narrow // share, units // share) + shape)
        tokens_sent = tokens_sent.transpose(2, 0, 1, 3, 4, 5, 6).reshape((units, narrow // share) + shape)
        tokens_sent = jnp.concatenate([tokens_sent] * halves)
    tokens_sent, both = lax.optimization_barrier((tokens_sent, both))
    tokens_all = lax.all_to_all(tokens_sent, "wide", split_axis=0, concat_axis=0, tiled=True)
    if rows % 16 == 0:
        back = experts_at_positions(both, w_in, b_in, w_out, b_out)
    else:
        lines = jnp.stack(both, axis=2).reshape(local_experts, 2, narrow * rows, model_width)
        (back,) = experts_at_positions([lines], w_in, b_in, w_out, b_out)
        back = back.reshape(local_experts, 2, narrow, rows, model_width)
        back = [back[:, :, j] for j in range(narrow)]

    where = jnp.stack([wide_index // units, unit]).astype(jnp.int32)
    first = (unit * held // share).astype(jnp.int32)
    expert_grads = [
        expert_weights(where, (first + p)[None], p, tokens_all, w_in, b_in, w_out, wide, units)
        for p in range(held)
    ]

    back = [untrim(x if j == 0 else from_relative(x, j)) for j, x in enumerate(back)]
    slot_rows, grad_controller = mix_backward(
        padded_part,
        relative,
        spread_probs,
        mix_rows,
        cot_rows,
        probs,
        back,
        controllers,
        row_code,
        col_code,
        tile,
        spread,
    )
    slot_rows = to_slots(slot_rows)
    expert_grads = [[x[0]] + [to_unit(x[d], d) for d in range(1, units)] for x in expert_grads]
    slot_rows = after(slot_rows, expert_grads[0][:-1], [x[0] for x in expert_grads])

    height = 4 * model_width
    grad_controller = grad_controller.astype(BF16).reshape(narrow, -1, LANES)[relative]
    end = height + grad_controller.shape[1]
    rows_sent = -(-(end + 16) // (16 * wide)) * 16 * wide
    partial, d_hidden, mixed_part, gain_mix_part, *far = attention_back_far(
        place,
        tokens,
        cotangent,
        slot_rows,
        hidden,
        joint_far,
        context_far,
        far_packs,
        gain_attn_row,
        gain_mix_row,
        grad_controller[2:],
        rows_sent,
    )
    early = [x[1:-1] for x in expert_grads[1:]]
    far, early = lax.optimization_barrier((far, early))
    for x, pieces in zip(expert_grads[1:], early):
        x[1:-1] = pieces
    partial, far = lax.optimization_barrier((partial, far_sums(far)))
    far = sum([to_chip(x, k + 1).astype(F32) for k, x in enumerate(far)], 0.0)
    d_tokens, kept, sent = attention_back_near(
        place,
        tokens,
        d_hidden,
        partial,
        joint_near,
        context_near,
        packs,
        gain_attn_row,
        gain_mix_part,
        grad_controller[:2],
        rows_sent,
    )
    d_tokens, kept, sent, far, expert_grads[0][-1] = lax.optimization_barrier(
        (d_tokens, kept, sent, far, expert_grads[0][-1])
    )
    weights = kept.astype(F32) + swap_core(sent).astype(F32) + far
    part_sums = wide_parts(weights)

    far_tokens = [from_chip(d_tokens, k) for k in range(1, narrow // 2)]
    swapped = [swap_core(d_tokens), swap_core(mixed_part)]
    order = lax.bitwise_xor(unit, jnp.arange(units)) * held
    order = order[None] + jnp.arange(held)[:, None]
    order = jnp.concatenate([order[:, :-1].reshape(-1), order[:, -1]])
    pieces = [piece for x in expert_grads for piece in x[:-1]] + [x[-1] for x in expert_grads]
    owned = owned_weights(pieces[:-1], order[:-1], units * held, w_in.shape[2], wide)
    mixed_near = place_blocks([mixed_part, swapped[1]], relative[:2], narrow)
    mixed_part, far_tokens, swapped, owned, pieces[-1], mixed_near = lax.optimization_barrier(
        (mixed_part, far_tokens, swapped, owned, pieces[-1], mixed_near)
    )
    far_mixed = [from_chip(mixed_part, k) for k in range(1, narrow // 2)]
    far_tokens = [y for x in far_tokens for y in (x, swap_core(x))]
    part_sums, far_tokens = lax.optimization_barrier((part_sums, far_tokens))
    d_tokens = place_blocks([d_tokens, swapped[0]] + far_tokens, relative, narrow)
    g_w_in, g_w_out, bias = owned_weights(after(pieces[-1:], part_sums), order[-1:], units * held, w_in.shape[2], wide, owned)
    far_mixed, d_tokens, bias = lax.optimization_barrier((far_mixed, d_tokens, bias))
    far_mixed = [y for x in far_mixed for y in (x, swap_core(x))]
    mixed_part = place_blocks(far_mixed, relative[2:], narrow, mixed_near)
    d_tokens, mixed_part = d_tokens[:slot_count], mixed_part[:slot_count]
    weights = from_parts(part_sums)
    gains = weights[end : end + 16].astype(BF16)
    gains = sum([to_chip(gains, k).astype(F32) for k in range(1, narrow // 2)], gains.astype(F32))
    projections = weights[: 3 * model_width, :head_columns].reshape(3, model_width, head_columns)
    output_weight_gradient = weights[3 * model_width : height].reshape(-1, LANES, LANES)[:, :head_columns]
    output_weight_gradient = output_weight_gradient.transpose(1, 0, 2).reshape(head_columns, -1)
    g_controller = weights[height:end].reshape(local_experts, model_width).T
    lines = model_width // LANES
    g_gain_attn = gains[:lines].reshape(-1)
    g_gain_mix = gains[lines : 2 * lines].reshape(-1)

    def over_share(x):
        return jnp.sum(x.reshape((local_experts, share) + x.shape[1:]), axis=1)

    g_w_in, g_w_out, bias = (over_share(x) for x in (g_w_in, g_w_out, bias))
    g_b_in = bias[:, : w_in.shape[2] // model_width].reshape(local_experts, -1)
    g_b_out = bias[:, -1]

    return (
        mixed_part,
        d_tokens,
        projections[0],
        projections[1],
        projections[2],
        output_weight_gradient,
        g_gain_attn,
        g_gain_mix,
        g_controller,
        g_w_in,
        g_b_in,
        g_w_out,
        g_b_out,
    )


def solution(mesh):
    placed = (
        P("wide", None, None),
        P("wide", None, None),
        P(),
        P(),
        P(None, "narrow"),
        P(None, "narrow"),
        P(None, "narrow"),
        P("narrow", None),
        P(),
        P(),
        P(None, "narrow"),
        P("narrow", None, None),
        P("narrow", None),
        P("narrow", None, None),
        P("narrow", None),
    )
    return jax.shard_map(
        body,
        mesh=mesh,
        in_specs=placed,
        out_specs=(
            P("wide", None, None),
            P("wide", None, None),
            P(None, "narrow"),
            P(None, "narrow"),
            P(None, "narrow"),
            P("narrow", None),
            P(),
            P(),
            P(None, "narrow"),
            P("narrow", "wide", None),
            P("narrow", None),
            P("narrow", "wide", None),
            P("narrow", None),
        ),
        check_vma=False,
    )
```
